256 devices in a mesh: grp: 8 (over y_lo, x), ctx: 32 (over y_hi, z, core).
Axes of the slice: x: 4, y: 4 (y_hi: 2, y_lo: 2; y = y_hi * 2 + y_lo), z: 8, core: 2. Of those that a mesh axis runs over, the one named last changes fastest.
Arguments:
- query_rows: bfloat16 [32768, 4096], P(('grp', 'ctx')), may hold values from -6 to 6
- key_rows: bfloat16 [32768, 512], P(('grp', 'ctx')), may hold values from -6 to 6
- value_rows: bfloat16 [32768, 512], P(('grp', 'ctx')), may hold values from -6 to 6
- output_grad: bfloat16 [32768, 4096], P(('grp', 'ctx')), may hold values from -6 to 6
- block_target: int32 [8, 32, 16], replicated, may hold values from 0 to 4095, as said below
- doc_lengths: int32 [8, 16], P('grp'), may hold values from 1 to 512, 4096 in all within a row
Outputs:
- query_grad: bfloat16 [32768, 4096], P(('grp', 'ctx'))
- key_grad: bfloat16 [32768, 512], P(('grp', 'ctx'))
- value_grad: bfloat16 [32768, 512], P(('grp', 'ctx'))
The draws below stay inside these ranges and needn't reach their ends.
Inputs may be any that keep to these rules, and one draw needn't show every extreme that they name: `block_target`: all entries together are a permutation of the packed blocks. Slot j of every loader device targets packed group j // 2. Of the slots that the devices with one ctx index (over all groups) send to one packed group, at most 1 target any one device of it. `doc_lengths`: each row sums to 4096.
All inputs are finite; a program needn't handle non-finite values.
Results may differ from the reference program's by a relative error of at most 0.012.
Values may be sent and summed in bfloat16 or wider, within the bound.
A program may use at most 128 MiB of HBM per device.

```python
import math
import jax
import jax.numpy as jnp
import numpy as np
from jax import lax

HEADS = 32
KV_HEADS = 4
HEAD_DIM = 128
TOK_DEV = 128
BLOCK_ROWS = 8
REACH = 4
SHARE = 8
BLOCKS_DEV = 16
PER_GROUP = 2
GROUP_TOKENS = 4096
GROUP_BLOCKS = 512
TOKENS = 32768
DOC_MAX = 512
DOCS = 16
N_GRP = 8
N_CTX = 32


def draw_query_rows(key, part):
    key = jax.random.fold_in(key, 11)
    values_out = jnp.clip(jax.random.normal(key, (TOKENS, HEADS * HEAD_DIM), jnp.float32), -6.0, 6.0)
    return values_out.astype(jnp.bfloat16)


def draw_key_rows(key, part):
    key = jax.random.fold_in(key, 23)
    values_out = jnp.clip(jax.random.normal(key, (TOKENS, KV_HEADS * HEAD_DIM), jnp.float32), -6.0, 6.0)
    return values_out.astype(jnp.bfloat16)


def draw_block_target(key, part):
    key = jax.random.fold_in(key, 37)
    perm_keys = jax.random.split(key, N_GRP * BLOCKS_DEV)
    orders = jax.vmap(lambda single_key: jax.random.permutation(single_key, N_CTX))(perm_keys).reshape(N_GRP, BLOCKS_DEV, N_CTX)
    group_ids = jnp.arange(N_GRP, dtype=jnp.int32)[:, None, None]
    member_ids = jnp.arange(N_CTX, dtype=jnp.int32)[None, :, None]
    slot_ids = jnp.arange(BLOCKS_DEV, dtype=jnp.int32)[None, None, :]
    target_group = jnp.broadcast_to(slot_ids // PER_GROUP, (N_GRP, N_CTX, BLOCKS_DEV))
    held_index = jnp.broadcast_to(group_ids * PER_GROUP + slot_ids % PER_GROUP, (N_GRP, N_CTX, BLOCKS_DEV))
    member_full = jnp.broadcast_to(member_ids, (N_GRP, N_CTX, BLOCKS_DEV))
    picked = orders[target_group, held_index, member_full]
    return (target_group * GROUP_BLOCKS + N_CTX * held_index + picked).astype(jnp.int32)


def shard_levels(own_key, extent, pieces, least, largest):
    def one(dim, blocks):
        draws = jax.random.uniform(jax.random.fold_in(jax.random.fold_in(own_key, 6), dim), (blocks,), jnp.float32, least / len(pieces), largest / len(pieces))
        return jnp.repeat(jnp.exp(draws), extent[dim] // blocks).reshape((-1,) + (1,) * (len(extent) - dim - 1))

    loudness = one(*pieces[0])
    for cut in pieces[1:]:
        loudness = loudness * one(*cut)
    return loudness


def length_profile(number_of, total, limit, skew):
    weights = [(1 << 20) // math.isqrt(rank ** skew) + 1 for rank in range(2, number_of + 1)]
    rest, holding = total - limit - (number_of - 1), [1] * (number_of - 1)
    while rest > 0:
        movable = [i for i in range(number_of - 1) if holding[i] < limit]
        pool, budget = sum([weights[i] for i in movable]), rest
        for i in movable:
            more = min(limit - holding[i], max(1, budget * weights[i] // pool), rest)
            holding[i] = holding[i] + more
            rest = rest - more
    return np.array([limit] + holding)


def ragged(stream_key, count, total, bound, slope):
    if count == 2:
        one = jax.random.randint(stream_key, (), max(1, total - bound), min(bound, total - 1) + 1)
        return jnp.stack([one, total - one])
    tallies = jnp.asarray(length_profile(count, total, bound, slope), jnp.int32)
    pairs = (count - 1) // 2
    source_of, sink = tallies[1:1 + 2 * pairs:2], tallies[2:2 + 2 * pairs:2]
    room = jnp.minimum(source_of - 1, bound - sink)
    moved = jax.random.randint(jax.random.fold_in(stream_key, 1), (pairs,), 0, 1 << 20) % (room + 1)
    tallies = tallies.at[1:1 + 2 * pairs:2].set(source_of - moved).at[2:2 + 2 * pairs:2].set(sink + moved)
    return tallies[jax.random.permutation(jax.random.fold_in(stream_key, 2), count)]


def noise(stream_key, dims, deviation, reach, shards=(), kind=jnp.bfloat16):
    values = jax.random.normal(stream_key, dims, jnp.float32) * deviation
    if len(shards) > 0:
        values = shard_levels(stream_key, dims, shards, -0.22, 0.18) * values
    return jnp.clip(values, min=-reach, max=reach).astype(kind)


def setup_inputs(seed: int = 0) -> dict:
    streams_of = jax.random.split(jax.random.key(seed), 7)
    return {
        "query_rows": draw_query_rows(jax.random.fold_in(streams_of[6], 71), 0),
        "key_rows": draw_key_rows(jax.random.fold_in(streams_of[6], 71), 0),
        "value_rows": noise(streams_of[2], (TOKENS, KV_HEADS * HEAD_DIM), 1.0, 6.0, ((0, 256),)),
        "output_grad": noise(streams_of[3], (TOKENS, HEADS * HEAD_DIM), 1.0, 6.0, ((0, 256),)),
        "block_target": draw_block_target(jax.random.fold_in(streams_of[6], 71), 0),
        "doc_lengths": jax.vmap(lambda own: ragged(own, DOCS, GROUP_TOKENS, DOC_MAX, 2))(jax.random.split(streams_of[5], N_GRP)).reshape((N_GRP, DOCS)).astype(jnp.int32),
    }


def doc_index(doc_ends, positions):
    return jnp.sum((doc_ends[None, :] <= positions[:, None]).astype(jnp.int32), axis=1)


def to_packed(source, block_target):
    row_width = source.shape[1]
    blocks = source.reshape(-1, BLOCK_ROWS, row_width)
    packed = jnp.zeros_like(blocks).at[block_target.reshape(-1)].set(blocks)
    return packed.reshape(N_GRP, GROUP_TOKENS, row_width)


def to_loader(packed, block_target):
    row_width = packed.shape[-1]
    blocks = packed.reshape(-1, BLOCK_ROWS, row_width)
    return blocks[block_target.reshape(-1)].reshape(-1, row_width)


def group_grads(inputs):
    query_pack, key_pack, value_pack, grad_pack, length_row = inputs
    score_scale = HEAD_DIM ** -0.5
    window = TOK_DEV * (REACH + 1)
    doc_ends = jnp.cumsum(length_row).astype(jnp.int32)
    query_all = query_pack.reshape(GROUP_TOKENS, KV_HEADS, SHARE, HEAD_DIM)
    grad_all = grad_pack.reshape(GROUP_TOKENS, KV_HEADS, SHARE, HEAD_DIM)
    key_all = key_pack.reshape(GROUP_TOKENS, KV_HEADS, HEAD_DIM)
    value_all = value_pack.reshape(GROUP_TOKENS, KV_HEADS, HEAD_DIM)

    def one_block(accums, block_index):
        key_acc, value_acc = accums
        first_row = (block_index * TOK_DEV).astype(jnp.int32)
        first_key = jnp.maximum(first_row - REACH * TOK_DEV, 0).astype(jnp.int32)
        queries = lax.dynamic_slice_in_dim(query_all, first_row, TOK_DEV, 0).astype(jnp.float32)
        grad_block = lax.dynamic_slice_in_dim(grad_all, first_row, TOK_DEV, 0).astype(jnp.float32)
        key_window = lax.dynamic_slice_in_dim(key_all, first_key, window, 0).astype(jnp.float32)
        value_window = lax.dynamic_slice_in_dim(value_all, first_key, window, 0).astype(jnp.float32)
        query_pos = first_row + jnp.arange(TOK_DEV, dtype=jnp.int32)
        key_pos = first_key + jnp.arange(window, dtype=jnp.int32)
        allowed = (doc_index(doc_ends, query_pos)[:, None] == doc_index(doc_ends, key_pos)[None, :]) & (key_pos[None, :] <= query_pos[:, None])
        scores = jnp.einsum('ihgd,jhd->hgij', queries, key_window) * score_scale
        row_max = jnp.max(jnp.where(allowed, scores, -jnp.inf), axis=-1, keepdims=True)
        row_sum = jnp.sum(jnp.where(allowed, jnp.exp(scores - row_max), 0.0), axis=-1, keepdims=True)
        log_total = row_max + jnp.log(row_sum)
        weights = jnp.where(allowed, jnp.exp(scores - log_total), 0.0)
        weights_low = lax.optimization_barrier(weights.astype(jnp.bfloat16)).astype(jnp.float32)
        out_sum = jnp.einsum('hgij,jhd->ihgd', weights_low, value_window)
        row_delta = jnp.transpose(jnp.sum(grad_block * out_sum, axis=-1), (1, 2, 0))[..., None]
        prob_grad = jnp.einsum('ihgd,jhd->hgij', grad_block, value_window)
        score_grad = lax.optimization_barrier((weights * (prob_grad - row_delta)).astype(jnp.bfloat16)).astype(jnp.float32)
        query_part = jnp.einsum('hgij,jhd->ihgd', score_grad, key_window) * score_scale
        key_part = jnp.einsum('hgij,ihgd->jhd', score_grad, queries) * score_scale
        value_part = jnp.einsum('hgij,ihgd->jhd', weights_low, grad_block)
        key_acc = lax.dynamic_update_slice_in_dim(key_acc, lax.dynamic_slice_in_dim(key_acc, first_key, window, 0) + key_part, first_key, 0)
        value_acc = lax.dynamic_update_slice_in_dim(value_acc, lax.dynamic_slice_in_dim(value_acc, first_key, window, 0) + value_part, first_key, 0)
        return (key_acc, value_acc), query_part.astype(jnp.bfloat16)

    start_acc = (jnp.zeros((GROUP_TOKENS, KV_HEADS, HEAD_DIM), jnp.float32), jnp.zeros((GROUP_TOKENS, KV_HEADS, HEAD_DIM), jnp.float32))
    accums, query_blocks = lax.scan(one_block, start_acc, jnp.arange(GROUP_TOKENS // TOK_DEV, dtype=jnp.int32))
    query_out = query_blocks.reshape(GROUP_TOKENS, HEADS * HEAD_DIM)
    key_out = accums[0].astype(jnp.bfloat16).reshape(GROUP_TOKENS, KV_HEADS * HEAD_DIM)
    value_out = accums[1].astype(jnp.bfloat16).reshape(GROUP_TOKENS, KV_HEADS * HEAD_DIM)
    return query_out, key_out, value_out


def reference(query_rows, key_rows, value_rows, output_grad, block_target, doc_lengths):
    packed_inputs = (to_packed(query_rows, block_target), to_packed(key_rows, block_target), to_packed(value_rows, block_target), to_packed(output_grad, block_target), doc_lengths)
    query_out, key_out, value_out = lax.map(group_grads, packed_inputs)
    return (to_loader(query_out, block_target), to_loader(key_out, block_target), to_loader(value_out, block_target))
```

```python
import jax
import jax.numpy as jnp
from jax import lax
from jax.experimental import pallas as pl
from jax.experimental.pallas import tpu as pltpu
from jax.sharding import PartitionSpec as P

KV_HEADS = 4
HEAD_DIM = 128
SHARE = 8
BLOCK_ROWS = 8
GROUPS = 8
PLANES = 8
PEERS = 32
RUN = 16
UNIT = SHARE * HEAD_DIM
GROUP_BLOCKS = 512
GROUP_TOKENS = 4096
PLANE_BLOCKS = 64
DOCS = 16
TILE_BLOCKS = 4
TILE_ROWS = TILE_BLOCKS * SHARE * BLOCK_ROWS
TILES = PLANE_BLOCKS // TILE_BLOCKS
KEY_TILE = 256
KEY_TILES = GROUP_TOKENS // KEY_TILE
SCORE_SCALE = HEAD_DIM**-0.5
EXP2_SCALE = SCORE_SCALE * 1.4426950408889634
MESH = pl.DeviceIdType.MESH
F32 = jnp.float32
BF16 = jnp.bfloat16


def place():
    group = lax.axis_index("grp")
    ctx = lax.axis_index("ctx")
    y_hi = ctx // 16
    plane = (ctx // 2) % PLANES
    core = ctx % 2
    head = y_hi * 2 + core
    return group, head, plane


def device_of(group, head, plane):
    return {"grp": group, "ctx": (head // 2) * 16 + plane * 2 + head % 2}


def greet(group, head, plane):
    barrier = pltpu.get_barrier_semaphore()
    me = group * KV_HEADS + head

    def one(step, carry):
        peer = lax.rem(me + step, PEERS)
        pl.semaphore_signal(
            barrier,
            inc=1,
            device_id=device_of(peer // KV_HEADS, lax.rem(peer, KV_HEADS), plane),
            device_id_type=MESH,
        )
        return carry

    lax.fori_loop(1, PEERS, one, 0)
    for by in (1, PLANES - 1):
        pl.semaphore_signal(
            barrier,
            inc=1,
            device_id=device_of(group, head, lax.rem(plane + by, PLANES)),
            device_id_type=MESH,
        )
    pl.semaphore_wait(barrier, PEERS - 1 + 2)


def remote(src, dst, send, recv, device):
    return pltpu.make_async_remote_copy(
        src_ref=src, dst_ref=dst, send_sem=send, recv_sem=recv, device_id=device, device_id_type=MESH
    )


def scatter_kernel(
    q_ref, g_ref, k_ref, v_ref, q_out, g_out, k_out, v_out, in_send, in_recv, own_sem, ring_send, ring_recv
):
    group, head, plane = place()
    me = group * KV_HEADS + head
    greet(group, head, plane)
    narrow = ((k_ref, k_out), (v_ref, v_out))
    wide = ((q_ref, q_out), (g_ref, g_out))

    def run_of(ref, to_group, to_head, width):
        return ref.at[
            pl.ds(pl.multiple_of(to_group * RUN, RUN), RUN),
            pl.ds(pl.multiple_of(to_head * width, width), width),
        ]

    def send_narrow(step, carry):
        peer = lax.rem(me + step, PEERS)
        to_group, to_head = peer // KV_HEADS, lax.rem(peer, KV_HEADS)
        for n, (src, dst) in enumerate(narrow):
            remote(
                run_of(src, to_group, to_head, HEAD_DIM),
                dst.at[plane, me],
                in_send.at[n],
                in_recv.at[n],
                device_of(to_group, to_head, plane),
            ).start()
        return carry

    def send_wide(step, carry):
        peer = lax.rem(me + step, PEERS)
        to_group, to_head = peer // KV_HEADS, lax.rem(peer, KV_HEADS)
        for n, (src, dst) in enumerate(wide):
            remote(
                run_of(src, to_group, to_head, UNIT),
                dst.at[me],
                in_send.at[2 + n],
                in_recv.at[2 + n],
                device_of(to_group, to_head, plane),
            ).start()
        return carry

    lax.fori_loop(1, PEERS, send_narrow, 0)
    own = [
        pltpu.make_async_copy(run_of(src, group, head, HEAD_DIM), dst.at[plane, me], own_sem.at[n])
        for n, (src, dst) in enumerate(narrow)
    ] + [
        pltpu.make_async_copy(run_of(src, group, head, UNIT), dst.at[me], own_sem.at[2 + n])
        for n, (src, dst) in enumerate(wide)
    ]
    for copy in own:
        copy.start()
    lax.fori_loop(1, PEERS, send_wide, 0)

    here = device_of(group, head, plane)
    rest_narrow = [
        remote(dst.at[0, pl.ds(0, PEERS - 1)], dst.at[0, pl.ds(0, PEERS - 1)], in_send.at[n], in_recv.at[n], here)
        for n, (_, dst) in enumerate(narrow)
    ]
    rest_wide = [
        remote(dst.at[pl.ds(0, PEERS - 1)], dst.at[pl.ds(0, PEERS - 1)], in_send.at[2 + n], in_recv.at[2 + n], here)
        for n, (_, dst) in enumerate(wide)
    ]
    for n in range(2):
        own[n].wait()
        rest_narrow[n].wait_recv()

    def ring(way, step, n):
        chunk = lax.rem(plane + (PLANES - step if way == 0 else step), PLANES)
        target = lax.rem(plane + (1 if way == 0 else PLANES - 1), PLANES)
        out = narrow[n][1]
        return remote(
            out.at[chunk],
            out.at[chunk],
            ring_send.at[way, step, n],
            ring_recv.at[way, step, n],
            device_of(group, head, target),
        )

    started = []
    for step in range(4):
        for way in range(2):
            for n in range(2):
                if step == 3 and n != way:
                    continue
                if step > 0:
                    ring(way, step - 1, n).wait_recv()
                copy = ring(way, step, n)
                copy.start()
                started.append(copy)
    for way in range(2):
        ring(way, 3, way).wait_recv()
        ring(way, 2, 1 - way).wait_recv()
    for copy in started:
        copy.wait_send()
    for n in range(2):
        rest_narrow[n].wait_send()
        own[2 + n].wait()
        rest_wide[n].wait_recv()
        rest_wide[n].wait_send()


def scatter(query_rows, output_grad, key_rows, value_rows):
    wide = jax.ShapeDtypeStruct((PEERS, RUN, UNIT), BF16)
    narrow = jax.ShapeDtypeStruct((PLANES, PEERS, RUN, HEAD_DIM), BF16)
    return pl.pallas_call(
        scatter_kernel,
        name="scatter",
        out_shape=(wide, wide, narrow, narrow),
        in_specs=[pl.BlockSpec(memory_space=pl.ANY)] * 4,
        out_specs=[pl.BlockSpec(memory_space=pl.ANY)] * 4,
        scratch_shapes=[
            pltpu.SemaphoreType.DMA((4,)),
            pltpu.SemaphoreType.DMA((4,)),
            pltpu.SemaphoreType.DMA((4,)),
            pltpu.SemaphoreType.DMA((2, 4, 2)),
            pltpu.SemaphoreType.DMA((2, 4, 2)),
        ],
        compiler_params=pltpu.CompilerParams(collective_id=0, has_side_effects=True),
    )(query_rows, output_grad, key_rows, value_rows)


def attention_kernel(
    packed_from,
    packed_to,
    query_order,
    query_block,
    doc_ends,
    q_ref,
    g_ref,
    k_ref,
    v_ref,
    dq_ref,
    dk_ref,
    dv_ref,
    k_pack,
    v_pack,
    k_turned,
    dk_acc,
    dv_acc,
    dq_acc,
    exps,
    probs,
    maxes,
):
    def half_of(pair, which):
        wide = pair.astype(F32)
        return jnp.where(which == 0, wide[:BLOCK_ROWS], wide[BLOCK_ROWS:])

    def gather(step, carry):
        first = packed_from[2 * step]
        second = packed_from[2 * step + 1]
        for src, dst in ((k_ref, k_pack), (v_ref, v_pack)):
            rows = jnp.concatenate(
                [half_of(src[first >> 1], first & 1), half_of(src[second >> 1], second & 1)], axis=0
            )
            dst[pl.ds(pl.multiple_of(step * RUN, RUN), RUN), :] = rows.astype(BF16)
        return carry

    lax.fori_loop(0, GROUP_BLOCKS // 2, gather, 0, unroll=8)

    def turn(step, carry):
        rows = pl.ds(pl.multiple_of(step * KEY_TILE, KEY_TILE), KEY_TILE)
        k_turned[step] = jnp.transpose(k_pack[rows, :].astype(F32)).astype(BF16)
        dk_acc[rows, :] = jnp.zeros((KEY_TILE, HEAD_DIM), F32)
        dv_acc[rows, :] = jnp.zeros((KEY_TILE, HEAD_DIM), F32)
        return carry

    lax.fori_loop(0, KEY_TILES, turn, 0)

    lane = lax.broadcasted_iota(jnp.int32, (1, TILE_ROWS), 1)
    key_iota = lax.broadcasted_iota(jnp.int32, (KEY_TILE, TILE_ROWS), 0)

    def query_tile(tile, carry):
        slots = [query_order[tile * TILE_BLOCKS + n] for n in range(TILE_BLOCKS)]
        blocks = [query_block[tile * TILE_BLOCKS + n] for n in range(TILE_BLOCKS)]

        def stacked(ref):
            parts = []
            for slot in slots:
                rows = half_of(ref[slot >> 1], slot & 1)
                parts += [rows[:, h * HEAD_DIM : (h + 1) * HEAD_DIM] for h in range(SHARE)]
            return jnp.concatenate(parts, axis=0)

        queries = stacked(q_ref)
        grads = stacked(g_ref)
        q_low, g_low = queries.astype(BF16), grads.astype(BF16)
        q_turned = jnp.transpose(queries).astype(BF16)
        g_turned = jnp.transpose(grads).astype(BF16)

        owner = lane // (SHARE * BLOCK_ROWS)
        last = jnp.full((1, TILE_ROWS), blocks[0], jnp.int32)
        for n in range(1, TILE_BLOCKS):
            last = jnp.where(owner == n, blocks[n], last)
        last = last * BLOCK_ROWS + (lane & (BLOCK_ROWS - 1))
        start = jnp.zeros((1, TILE_ROWS), jnp.int32)
        tile_start = jnp.int32(0)
        for n in range(DOCS):
            end = doc_ends[n]
            start = jnp.where(end <= last, end, start)
            tile_start = jnp.where(end <= blocks[0] * BLOCK_ROWS, end, tile_start)
        first_tile = tile_start // KEY_TILE
        last_tile = (blocks[-1] * BLOCK_ROWS + BLOCK_ROWS - 1) // KEY_TILE

        def totals(key_tile, state):
            top, total, weighted = state
            rows = pl.ds(pl.multiple_of(key_tile * KEY_TILE, KEY_TILE), KEY_TILE)
            scores = jnp.dot(k_pack[rows, :], q_turned, preferred_element_type=F32)
            prob_grad = jnp.dot(v_pack[rows, :], g_turned, preferred_element_type=F32)
            position = key_iota + key_tile * KEY_TILE
            allowed = (position >= start) & (position <= last)
            scores = jnp.where(allowed, scores, -1e30)
            new_top = jnp.maximum(top, jnp.max(scores, axis=0, keepdims=True))
            weights = jnp.exp2((scores - new_top) * EXP2_SCALE)
            fade = jnp.exp2((top - new_top) * EXP2_SCALE)
            total = total * fade + jnp.sum(weights, axis=0, keepdims=True)
            weighted = weighted * fade + jnp.sum(weights * prob_grad, axis=0, keepdims=True)
            slot = key_tile - first_tile
            exps[slot] = weights
            probs[slot] = prob_grad
            maxes[slot] = jnp.broadcast_to(new_top, (8, TILE_ROWS))
            return new_top, total, weighted

        top, total, weighted = lax.fori_loop(
            first_tile,
            last_tile + 1,
            totals,
            (jnp.full((1, TILE_ROWS), -1e20, F32), jnp.zeros((1, TILE_ROWS), F32), jnp.zeros((1, TILE_ROWS), F32)),
        )
        scale_row = 1.0 / total
        delta = weighted * scale_row

        def gradients(key_tile, dq_turned):
            rows = pl.ds(pl.multiple_of(key_tile * KEY_TILE, KEY_TILE), KEY_TILE)
            slot = key_tile - first_tile
            factor = jnp.exp2((maxes[slot][:1] - top) * EXP2_SCALE) * scale_row
            weights = exps[slot] * factor
            score_grad = (weights * (probs[slot] - delta)).astype(BF16)
            dv_acc[rows, :] += jnp.dot(weights.astype(BF16), g_low, preferred_element_type=F32)
            dk_acc[rows, :] += jnp.dot(score_grad, q_low, preferred_element_type=F32)
            return dq_turned + jnp.dot(k_turned[key_tile], score_grad, preferred_element_type=F32)

        dq_turned = lax.fori_loop(
            first_tile, last_tile + 1, gradients, jnp.zeros((HEAD_DIM, TILE_ROWS), F32)
        )
        dq = jnp.transpose(dq_turned) * SCORE_SCALE
        for n, slot in enumerate(slots):
            for h in range(SHARE):
                part = (n * SHARE + h) * BLOCK_ROWS
                dq_acc[
                    pl.ds(pl.multiple_of(slot * BLOCK_ROWS, BLOCK_ROWS), BLOCK_ROWS),
                    h * HEAD_DIM : (h + 1) * HEAD_DIM,
                ] = dq[part : part + BLOCK_ROWS]
        return carry

    lax.fori_loop(0, TILES, query_tile, 0)

    def finish_queries(step, carry):
        dq_ref[step] = dq_acc[pl.ds(pl.multiple_of(step * RUN, RUN), RUN), :].astype(BF16)
        return carry

    lax.fori_loop(0, PEERS, finish_queries, 0, unroll=2)

    def finish_keys(step, carry):
        first = pl.multiple_of(packed_to[2 * step] * BLOCK_ROWS, BLOCK_ROWS)
        second = pl.multiple_of(packed_to[2 * step + 1] * BLOCK_ROWS, BLOCK_ROWS)
        for src, dst, scale in ((dk_acc, dk_ref, SCORE_SCALE), (dv_acc, dv_ref, 1.0)):
            rows = jnp.concatenate([src[pl.ds(first, BLOCK_ROWS), :], src[pl.ds(second, BLOCK_ROWS), :]], axis=0)
            dst[step] = (rows * scale).astype(BF16)
        return carry

    lax.fori_loop(0, GROUP_BLOCKS // 2, finish_keys, 0, unroll=8)


def attention(tables, queries, grads, keys, values):
    narrow = jax.ShapeDtypeStruct((GROUP_BLOCKS // 2, RUN, HEAD_DIM), BF16)
    return pl.pallas_call(
        attention_kernel,
        name="attention",
        out_shape=(jax.ShapeDtypeStruct((PEERS, RUN, UNIT), BF16), narrow, narrow),
        in_specs=[pl.BlockSpec(memory_space=pltpu.SMEM)] * 5 + [pl.BlockSpec(memory_space=pltpu.VMEM)] * 4,
        out_specs=[pl.BlockSpec(memory_space=pltpu.VMEM)] * 3,
        scratch_shapes=[
            pltpu.VMEM((GROUP_TOKENS, HEAD_DIM), BF16),
            pltpu.VMEM((GROUP_TOKENS, HEAD_DIM), BF16),
            pltpu.VMEM((KEY_TILES, HEAD_DIM, KEY_TILE), BF16),
            pltpu.VMEM((GROUP_TOKENS, HEAD_DIM), F32),
            pltpu.VMEM((GROUP_TOKENS, HEAD_DIM), F32),
            pltpu.VMEM((PLANE_BLOCKS * BLOCK_ROWS, UNIT), F32),
            pltpu.VMEM((KEY_TILES, KEY_TILE, TILE_ROWS), F32),
            pltpu.VMEM((KEY_TILES, KEY_TILE, TILE_ROWS), F32),
            pltpu.VMEM((KEY_TILES, 8, TILE_ROWS), F32),
        ],
        compiler_params=pltpu.CompilerParams(vmem_limit_bytes=48 * 1024 * 1024),
    )(*tables, queries, grads, keys, values)


def collect_kernel(
    dq_ref,
    dk_ref,
    dv_ref,
    dq_out,
    dk_out,
    dv_out,
    inbox,
    total,
    in_send,
    in_recv,
    own_sem,
    ring_send,
    ring_recv,
):
    group, head, plane = place()
    me = group * KV_HEADS + head
    greet(group, head, plane)
    here = device_of(group, head, plane)

    def home_of(ref, width):
        return ref.at[
            pl.ds(pl.multiple_of(group * RUN, RUN), RUN), pl.ds(pl.multiple_of(head * width, width), width)
        ]

    def send_wide(step, carry):
        peer = lax.rem(me + step, PEERS)
        remote(
            dq_ref.at[peer],
            home_of(dq_out, UNIT),
            in_send.at[2],
            in_recv.at[2],
            device_of(peer // KV_HEADS, lax.rem(peer, KV_HEADS), plane),
        ).start()
        return carry

    parts = (dk_ref, dv_ref)

    def ring(way, step, n, src):
        target = lax.rem(plane + (1 if way == 0 else PLANES - 1), PLANES)
        return remote(
            src,
            inbox.at[way, n, step],
            ring_send.at[way, step, n],
            ring_recv.at[way, step, n],
            device_of(group, head, target),
        )

    def chunk_at(way, step):
        distance = 4 - step
        return lax.rem(plane + (distance if way == 0 else PLANES - distance), PLANES)

    started = []
    for step in range(4):
        for way in range(2):
            chunk = chunk_at(way, step)
            for n in range(2):
                if step == 0 and n != way:
                    continue
                if step == 0 or (step == 1 and n != way):
                    copy = ring(way, step, n, parts[n].at[chunk])
                else:
                    held = inbox.at[way, n, step - 1]
                    ring(way, step - 1, n, held).wait_recv()
                    held[...] = (held[...].astype(F32) + parts[n][chunk].astype(F32)).astype(BF16)
                    copy = ring(way, step, n, held)
                copy.start()
                started.append(copy)
        if step == 0:
            own_wide = pltpu.make_async_copy(dq_ref.at[me], home_of(dq_out, UNIT), own_sem.at[2])
            own_wide.start()
            lax.fori_loop(1, PEERS, send_wide, 0)
    for n in range(2):
        for way in range(2):
            ring(way, 3, n, inbox.at[way, n, 3]).wait_recv()
        total[n] = (
            parts[n][plane].astype(F32) + inbox[0, n, 3].astype(F32) + inbox[1, n, 3].astype(F32)
        ).astype(BF16)

    outs = (dk_out, dv_out)

    def send_narrow(step, carry):
        peer = lax.rem(me + step, PEERS)
        for n in range(2):
            remote(
                total.at[n, peer],
                home_of(outs[n], HEAD_DIM),
                in_send.at[n],
                in_recv.at[n],
                device_of(peer // KV_HEADS, lax.rem(peer, KV_HEADS), plane),
            ).start()
        return carry

    lax.fori_loop(1, PEERS, send_narrow, 0)
    own = [pltpu.make_async_copy(total.at[n, me], home_of(outs[n], HEAD_DIM), own_sem.at[n]) for n in range(2)]
    for copy in own:
        copy.start()
    for copy in started:
        copy.wait_send()
    own_wide.wait()
    rest_wide = remote(
        dq_ref.at[pl.ds(0, PEERS - 1)], dq_ref.at[pl.ds(0, PEERS - 1)], in_send.at[2], in_recv.at[2], here
    )
    rest_wide.wait_send()
    rest_wide.wait_recv()
    for n in range(2):
        rest = remote(
            total.at[n, pl.ds(0, PEERS - 1)], total.at[n, pl.ds(0, PEERS - 1)], in_send.at[n], in_recv.at[n], here
        )
        rest.wait_send()
        rest.wait_recv()
        own[n].wait()


def collect(dq, dk, dv):
    return pl.pallas_call(
        collect_kernel,
        name="collect",
        out_shape=(
            jax.ShapeDtypeStruct((GROUPS * RUN, KV_HEADS * UNIT), BF16),
            jax.ShapeDtypeStruct((GROUPS * RUN, KV_HEADS * HEAD_DIM), BF16),
            jax.ShapeDtypeStruct((GROUPS * RUN, KV_HEADS * HEAD_DIM), BF16),
        ),
        in_specs=[
            pl.BlockSpec(memory_space=pl.ANY),
            pl.BlockSpec(memory_space=pltpu.VMEM),
            pl.BlockSpec(memory_space=pltpu.VMEM),
        ],
        out_specs=[pl.BlockSpec(memory_space=pl.ANY)] * 3,
        scratch_shapes=[
            pltpu.VMEM((2, 2, 4, PEERS, RUN, HEAD_DIM), BF16),
            pltpu.VMEM((2, PEERS, RUN, HEAD_DIM), BF16),
            pltpu.SemaphoreType.DMA((3,)),
            pltpu.SemaphoreType.DMA((3,)),
            pltpu.SemaphoreType.DMA((3,)),
            pltpu.SemaphoreType.DMA((2, 4, 2)),
            pltpu.SemaphoreType.DMA((2, 4, 2)),
        ],
        compiler_params=pltpu.CompilerParams(
            collective_id=1, has_side_effects=True, vmem_limit_bytes=32 * 1024 * 1024
        ),
    )(dq, dk, dv)


def tables_of(block_target, doc_lengths):
    group, _, plane = place()
    targets = lax.dynamic_slice(block_target, (0, 0, 2 * group), (GROUPS, PEERS, 2)) - group * GROUP_BLOCKS
    targets = targets.reshape(GROUPS, 2, PLANES, 2, 2).transpose(2, 0, 1, 3, 4)
    packed_to = targets.reshape(GROUP_BLOCKS)
    count = jnp.arange(GROUP_BLOCKS, dtype=jnp.int32)
    packed_from = jnp.sum(jnp.where(packed_to[None, :] == count[:, None], count[None, :], 0), axis=1)
    mine = lax.dynamic_index_in_dim(targets.reshape(PLANES, PLANE_BLOCKS), plane, 0, keepdims=False)
    rank = jnp.sum((mine[None, :] < mine[:, None]).astype(jnp.int32), axis=1)
    small = jnp.arange(PLANE_BLOCKS, dtype=jnp.int32)
    hit = rank[None, :] == small[:, None]
    query_order = jnp.sum(jnp.where(hit, small[None, :], 0), axis=1)
    query_block = jnp.sum(jnp.where(hit, mine[None, :], 0), axis=1)
    doc_ends = jnp.cumsum(doc_lengths[0])
    return packed_from, packed_to, query_order, query_block, doc_ends


def on_device(query_rows, key_rows, value_rows, output_grad, block_target, doc_lengths):
    tables = tables_of(block_target, doc_lengths)
    queries, grads, keys, values = scatter(query_rows, output_grad, key_rows, value_rows)
    pairs = (GROUP_BLOCKS // 2, RUN, HEAD_DIM)
    dq, dk, dv = attention(tables, queries, grads, keys.reshape(pairs), values.reshape(pairs))
    planes = (PLANES, PEERS, RUN, HEAD_DIM)
    return collect(dq, dk.reshape(planes), dv.reshape(planes))


def solution(mesh):
    in_specs = (
        P(("grp", "ctx"), None),
        P(("grp", "ctx"), None),
        P(("grp", "ctx"), None),
        P(("grp", "ctx"), None),
        P(),
        P("grp", None),
    )
    out_specs = (P(("grp", "ctx"), None), P(("grp", "ctx"), None), P(("grp", "ctx"), None))
    return jax.shard_map(
        on_device, mesh=mesh, in_specs=in_specs, out_specs=out_specs, check_vma=False
    )
```

```python
import jax
import jax.numpy as jnp
from jax import lax
from jax.experimental import pallas as pl
from jax.experimental.pallas import tpu as pltpu
from jax.sharding import PartitionSpec as P

KV_HEADS = 4
HEAD_DIM = 128
SHARE = 8
BLOCK_ROWS = 8
GROUPS = 8
PLANES = 8
PEERS = 32
RUN = 16
UNIT = SHARE * HEAD_DIM
GROUP_BLOCKS = 512
GROUP_TOKENS = 4096
PLANE_BLOCKS = 64
DOCS = 16
TILE_BLOCKS = 4
TILE_ROWS = TILE_BLOCKS * SHARE * BLOCK_ROWS
TILES = PLANE_BLOCKS // TILE_BLOCKS
CHUNK = 128
CHUNKS = GROUP_TOKENS // CHUNK
FIXED_MAX = 7
TOGETHER = 2
UNROLL_PREP = 2
SCORE_SCALE = HEAD_DIM**-0.5
EXP2_SCALE = SCORE_SCALE * 1.4426950408889634
PARTS = 4
PART = PEERS // PARTS
WIDE_STEPS = (1, 32, 32, 32, 32)
MESH = pl.DeviceIdType.MESH
F32 = jnp.float32
BF16 = jnp.bfloat16


def place():
    group = lax.axis_index("grp")
    ctx = lax.axis_index("ctx")
    y_hi = ctx // 16
    plane = (ctx // 2) % PLANES
    core = ctx % 2
    head = y_hi * 2 + core
    return group, head, plane


def device_of(group, head, plane):
    return {"grp": group, "ctx": (head // 2) * 16 + plane * 2 + head % 2}


def greet(group, head, plane):
    barrier = pltpu.get_barrier_semaphore()
    me = group * KV_HEADS + head

    def one(step, carry):
        peer = lax.rem(me + step, PEERS)
        pl.semaphore_signal(
            barrier,
            inc=1,
            device_id=device_of(peer // KV_HEADS, lax.rem(peer, KV_HEADS), plane),
            device_id_type=MESH,
        )
        return carry

    lax.fori_loop(1, PEERS, one, 0)
    for by in (1, PLANES - 1):
        pl.semaphore_signal(
            barrier,
            inc=1,
            device_id=device_of(group, head, lax.rem(plane + by, PLANES)),
            device_id_type=MESH,
        )
    pl.semaphore_wait(barrier, PEERS - 1 + 2)


def remote(src, dst, send, recv, device):
    return pltpu.make_async_remote_copy(
        src_ref=src, dst_ref=dst, send_sem=send, recv_sem=recv, device_id=device, device_id_type=MESH
    )


def scatter_kernel(
    q_ref, g_ref, k_ref, v_ref, q_out, g_out, k_out, v_out, send_sem, narrow_recv, wide_recv, own_sem, ring_send, ring_recv
):
    group, head, plane = place()
    me = group * KV_HEADS + head
    greet(group, head, plane)
    here = device_of(group, head, plane)
    narrow = ((k_ref, k_out), (v_ref, v_out))
    wide = ((q_ref, q_out), (g_ref, g_out))

    def run_of(ref, to_group, to_head, width):
        return ref.at[
            pl.ds(pl.multiple_of(to_group * RUN, RUN), RUN),
            pl.ds(pl.multiple_of(to_head * width, width), width),
        ]

    def send_narrow(step, carry):
        peer = lax.rem(me + step, PEERS)
        to_group, to_head = peer // KV_HEADS, lax.rem(peer, KV_HEADS)
        for n, (src, dst) in enumerate(narrow):
            remote(
                run_of(src, to_group, to_head, HEAD_DIM),
                dst.at[plane, step],
                send_sem.at[n],
                narrow_recv.at[n, step // PART],
                device_of(to_group, to_head, plane),
            ).start()
        return carry

    def send_wide(step, carry):
        peer = lax.rem(me + step, PEERS)
        to_group, to_head = peer // KV_HEADS, lax.rem(peer, KV_HEADS)
        for n, (src, dst) in enumerate(wide):
            remote(
                run_of(src, to_group, to_head, UNIT),
                dst.at[step],
                send_sem.at[2 + n],
                wide_recv.at[n],
                device_of(to_group, to_head, plane),
            ).start()
        return carry

    own = [
        pltpu.make_async_copy(run_of(src, group, head, HEAD_DIM), dst.at[plane, 0], own_sem.at[n])
        for n, (src, dst) in enumerate(narrow)
    ] + [
        pltpu.make_async_copy(run_of(src, group, head, UNIT), dst.at[0], own_sem.at[2 + n])
        for n, (src, dst) in enumerate(wide)
    ]
    own[0].start()
    own[1].start()
    lax.fori_loop(1, PEERS, send_narrow, 0)
    own[2].start()
    own[3].start()

    def ring(way, step, n, part):
        chunk = lax.rem(plane + (PLANES - step if way == 0 else step), PLANES)
        target = lax.rem(plane + (1 if way == 0 else PLANES - 1), PLANES)
        piece = narrow[n][1].at[chunk, pl.ds(part * PART, PART)]
        return remote(
            piece,
            piece,
            ring_send.at[way, n],
            ring_recv.at[way, step, n, part],
            device_of(group, head, target),
        )

    for step in range(4):
        lax.fori_loop(WIDE_STEPS[step], WIDE_STEPS[step + 1], send_wide, 0)
        for part in range(PARTS):
            for n in range(2):
                if step == 0:
                    if part == 0:
                        own[n].wait()
                    landed = narrow[n][1].at[plane, pl.ds(part * PART, PART - (part == 0))]
                    remote(landed, landed, send_sem.at[n], narrow_recv.at[n, part], here).wait_recv()
                for way in range(2):
                    if step == 3 and n != way:
                        continue
                    if step > 0:
                        ring(way, step - 1, n, part).wait_recv()
                    ring(way, step, n, part).start()
    for part in range(PARTS):
        for way in range(2):
            ring(way, 2, 1 - way, part).wait_recv()
    for part in range(PARTS):
        for way in range(2):
            ring(way, 3, way, part).wait_recv()
    for way in range(2):
        for n in range(2):
            sent = narrow[n][1].at[pl.ds(0, 4 if n == way else 3)]
            remote(sent, sent, ring_send.at[way, n], ring_recv.at[way, 0, n, 0], here).wait_send()
    for n in range(2):
        sent = narrow[n][1].at[0, pl.ds(0, PEERS - 1)]
        remote(sent, sent, send_sem.at[n], narrow_recv.at[n, 0], here).wait_send()
        own[2 + n].wait()
        landed = wide[n][1].at[pl.ds(0, PEERS - 1)]
        rest = remote(landed, landed, send_sem.at[2 + n], wide_recv.at[n], here)
        rest.wait_recv()
        rest.wait_send()


def scatter(query_rows, output_grad, key_rows, value_rows):
    wide = jax.ShapeDtypeStruct((PEERS, RUN, UNIT), BF16)
    narrow = jax.ShapeDtypeStruct((PLANES, PEERS, RUN, HEAD_DIM), BF16)
    return pl.pallas_call(
        scatter_kernel,
        name="scatter",
        out_shape=(wide, wide, narrow, narrow),
        in_specs=[pl.BlockSpec(memory_space=pl.ANY)] * 4,
        out_specs=[pl.BlockSpec(memory_space=pl.ANY)] * 4,
        scratch_shapes=[
            pltpu.SemaphoreType.DMA((4,)),
            pltpu.SemaphoreType.DMA((2, PARTS)),
            pltpu.SemaphoreType.DMA((2,)),
            pltpu.SemaphoreType.DMA((4,)),
            pltpu.SemaphoreType.DMA((2, 2)),
            pltpu.SemaphoreType.DMA((2, 4, 2, PARTS)),
        ],
        compiler_params=pltpu.CompilerParams(
            collective_id=0, has_side_effects=True, vmem_limit_bytes=2 * 1024 * 1024
        ),
    )(query_rows, output_grad, key_rows, value_rows)


def attention_kernel(
    target_ref,
    length_ref,
    q_ref,
    g_ref,
    k_ref,
    v_ref,
    dq_ref,
    dk_ref,
    dv_ref,
    packed_to,
    holder,
    query_order,
    query_block,
    doc_ends,
    k_pack,
    v_pack,
    q_tiles,
    g_tiles,
    bounds,
    spans,
    k_turned,
    dk_acc,
    dv_acc,
    dq_turned,
    dq_acc,
    exps,
    probs,
    maxes,
):
    def half_of(pair, which):
        wide = pair.astype(F32)
        return jnp.where(which == 0, wide[:BLOCK_ROWS], wide[BLOCK_ROWS:])

    group, head, plane = place()
    me = group * KV_HEADS + head

    def target_of(source, from_plane, which):
        ctx = ((source >> 1) & 1) * 16 + (source & 1) + from_plane * 2
        return target_ref[source >> 2, ctx, 2 * group + which] - group * GROUP_BLOCKS

    def clear(step, carry):
        holder[step] = 0
        return carry

    lax.fori_loop(0, GROUP_BLOCKS, clear, 0, unroll=16)

    def hold(slot, carry):
        for which in range(2):
            holder[target_of((me - slot) & (PEERS - 1), plane, which)] = 2 * slot + which + 1
        return carry

    lax.fori_loop(0, PEERS, hold, 0, unroll=4)

    end = jnp.int32(0)
    for n in range(DOCS):
        end = end + length_ref[0, n]
        doc_ends[n] = end

    def pack(source, carry):
        slot = (me - source) & (PEERS - 1)
        for from_plane in range(PLANES):
            pair = from_plane * PEERS + slot
            keys = k_ref[pair].astype(F32)
            values = v_ref[pair].astype(F32)
            for which in range(2):
                block = target_of(source, from_plane, which)
                packed_to[2 * pair + which] = block
                rows = pl.ds(pl.multiple_of(block * BLOCK_ROWS, BLOCK_ROWS), BLOCK_ROWS)
                half = slice(which * BLOCK_ROWS, (which + 1) * BLOCK_ROWS)
                dk_acc[rows, :] = keys[half]
                dv_acc[rows, :] = values[half]
        return carry

    lax.fori_loop(0, PEERS, pack, 0, unroll=2)

    def turn(step, found):
        rows = pl.ds(pl.multiple_of(step * CHUNK, CHUNK), CHUNK)
        keys = dk_acc[rows, :]
        k_pack[rows, :] = keys.astype(BF16)
        k_turned[step] = jnp.transpose(keys).astype(BF16)
        v_pack[rows, :] = dv_acc[rows, :].astype(BF16)
        dk_acc[rows, :] = jnp.zeros((CHUNK, HEAD_DIM), F32)
        dv_acc[rows, :] = jnp.zeros((CHUNK, HEAD_DIM), F32)
        for n in range(CHUNK // BLOCK_ROWS):
            block = step * (CHUNK // BLOCK_ROWS) + n
            slot = holder[block]
            query_order[found] = slot - 1
            query_block[found] = block
            found = found + jnp.where(slot > 0, 1, 0)
        return found

    lax.fori_loop(0, CHUNKS, turn, jnp.int32(0), unroll=2)

    lane = lax.broadcasted_iota(jnp.int32, (1, TILE_ROWS), 1)
    owner = lane // (SHARE * BLOCK_ROWS)

    def prepare(tile, carry):
        slots = [query_order[tile * TILE_BLOCKS + n] for n in range(TILE_BLOCKS)]
        blocks = [query_block[tile * TILE_BLOCKS + n] for n in range(TILE_BLOCKS)]
        for src, dst in ((q_ref, q_tiles), (g_ref, g_tiles)):
            parts = []
            for slot in slots:
                rows = half_of(src[slot >> 1], slot & 1)
                parts += [rows[:, h * HEAD_DIM : (h + 1) * HEAD_DIM] for h in range(SHARE)]
            dst[tile] = jnp.concatenate(parts, axis=0).astype(BF16)
        last = jnp.full((1, TILE_ROWS), blocks[0], jnp.int32)
        for n in range(1, TILE_BLOCKS):
            last = jnp.where(owner == n, blocks[n], last)
        last = last * BLOCK_ROWS + (lane & (BLOCK_ROWS - 1))
        start = jnp.zeros((1, TILE_ROWS), jnp.int32)
        tile_start = jnp.int32(0)
        for n in range(DOCS):
            end = doc_ends[n]
            start = jnp.where(end <= last, end, start)
            tile_start = jnp.where(end <= blocks[0] * BLOCK_ROWS, end, tile_start)
        bounds[tile, 0:1] = start
        bounds[tile, 1:2] = last
        first_chunk = tile_start // CHUNK
        spans[2 * tile] = first_chunk
        spans[2 * tile + 1] = (blocks[-1] * BLOCK_ROWS + BLOCK_ROWS - 1) // CHUNK - first_chunk + 1
        return carry

    lax.fori_loop(0, TILES, prepare, 0, unroll=UNROLL_PREP)

    key_iota = lax.broadcasted_iota(jnp.int32, (CHUNK, TILE_ROWS), 0)
    no_sum = jnp.zeros((8, TILE_ROWS), F32)

    def fold(array, op):
        return op(array.reshape(CHUNK // 8, 8, TILE_ROWS), axis=0)

    def rows_of(chunk):
        return pl.ds(pl.multiple_of(chunk * CHUNK, CHUNK), CHUNK)

    def against(rows_ref, chunk, tile_rows):
        return lax.dot_general(
            rows_ref[rows_of(chunk), :], tile_rows, (((1,), (1,)), ((), ())), preferred_element_type=F32
        )

    def masked(scores, chunk, start, last):
        position = key_iota + chunk * CHUNK
        return jnp.where((position >= start) & (position <= last), scores, -1e30)

    def put_keys(chunk, weights, score_grad, q_low, g_low):
        rows = rows_of(chunk)
        dv_acc[rows, :] += jnp.dot(weights.astype(BF16), g_low, preferred_element_type=F32)
        dk_acc[rows, :] += jnp.dot(score_grad, q_low, preferred_element_type=F32)
        return jnp.dot(k_turned[chunk], score_grad, preferred_element_type=F32)

    def query_tiles(step, carry):
        tiles = [step * TOGETHER + n for n in range(TOGETHER)]
        firsts = [spans[2 * tile] for tile in tiles]
        counts = [spans[2 * tile + 1] for tile in tiles]
        most = counts[0]
        for count in counts[1:]:
            most = jnp.maximum(most, count)

        def fixed(chunks):
            begins = [jnp.minimum(first, CHUNKS - chunks) for first in firsts]
            ways = range(TOGETHER)
            q_low = [q_tiles[tile] for tile in tiles]
            g_low = [g_tiles[tile] for tile in tiles]
            start = [bounds[tile, 0:1] for tile in tiles]
            last = [bounds[tile, 1:2] for tile in tiles]
            top = [jnp.full((8, TILE_ROWS), -1e30, F32)] * TOGETHER
            for n in range(chunks):
                for w in ways:
                    chunk = begins[w] + n
                    scores = masked(against(k_pack, chunk, q_low[w]), chunk, start[w], last[w])
                    exps[w * FIXED_MAX + n] = scores
                    top[w] = jnp.maximum(top[w], fold(scores, jnp.max))
            top = [jnp.max(t, axis=0, keepdims=True) for t in top]
            total, weighted = [no_sum] * TOGETHER, [no_sum] * TOGETHER
            for n in range(chunks):
                for w in ways:
                    prob_grad = against(v_pack, begins[w] + n, g_low[w])
                    weights = jnp.exp2((exps[w * FIXED_MAX + n] - top[w]) * EXP2_SCALE)
                    total[w] += fold(weights, jnp.sum)
                    weighted[w] += fold(weights * prob_grad, jnp.sum)
                    exps[w * FIXED_MAX + n] = weights
                    probs[w * FIXED_MAX + n] = prob_grad
            factor = [1.0 / jnp.sum(t, axis=0, keepdims=True) for t in total]
            delta = [jnp.sum(t, axis=0, keepdims=True) * f for t, f in zip(weighted, factor)]
            dq = [jnp.zeros((HEAD_DIM, TILE_ROWS), F32)] * TOGETHER
            for n in range(chunks):
                for w in ways:
                    weights = exps[w * FIXED_MAX + n] * factor[w]
                    score_grad = (weights * (probs[w * FIXED_MAX + n] - delta[w])).astype(BF16)
                    dq[w] += put_keys(begins[w] + n, weights, score_grad, q_low[w], g_low[w])
            for w in ways:
                dq_turned[tiles[w]] = dq[w]

        for chunks in range(1, FIXED_MAX + 1):

            @pl.when(most == chunks)
            def _():
                fixed(chunks)

        @pl.when(most > FIXED_MAX)
        def _():
            for tile, first, count in zip(tiles, firsts, counts):
                any_length(tile, first, count)

        return carry

    def any_length(tile, first, count):
        q_low, g_low = q_tiles[tile], g_tiles[tile]
        start, last = bounds[tile, 0:1], bounds[tile, 1:2]

        def totals(slot, state):
            top, total, weighted = state
            chunk = first + slot
            scores = masked(against(k_pack, chunk, q_low), chunk, start, last)
            prob_grad = against(v_pack, chunk, g_low)
            new_top = jnp.maximum(top, jnp.max(scores, axis=0, keepdims=True))
            weights = jnp.exp2((scores - new_top) * EXP2_SCALE)
            fade = jnp.exp2((top - new_top) * EXP2_SCALE)
            total = total * fade + jnp.sum(weights, axis=0, keepdims=True)
            weighted = weighted * fade + jnp.sum(weights * prob_grad, axis=0, keepdims=True)
            exps[slot] = weights
            probs[slot] = prob_grad
            maxes[slot] = jnp.broadcast_to(new_top, (8, TILE_ROWS))
            return new_top, total, weighted

        top, total, weighted = lax.fori_loop(
            0, count, totals, (jnp.full((1, TILE_ROWS), -1e20, F32), no_sum[:1], no_sum[:1])
        )
        scale_row = 1.0 / total
        delta = weighted * scale_row

        def gradients(slot, dq):
            factor = jnp.exp2((maxes[slot][:1] - top) * EXP2_SCALE) * scale_row
            weights = exps[slot] * factor
            score_grad = (weights * (probs[slot] - delta)).astype(BF16)
            return dq + put_keys(first + slot, weights, score_grad, q_low, g_low)

        dq_turned[tile] = lax.fori_loop(0, count, gradients, jnp.zeros((HEAD_DIM, TILE_ROWS), F32))

    lax.fori_loop(0, TILES // TOGETHER, query_tiles, 0)

    def place_queries(tile, carry):
        dq = jnp.transpose(dq_turned[tile]) * SCORE_SCALE
        for n in range(TILE_BLOCKS):
            rows = pl.ds(pl.multiple_of(query_order[tile * TILE_BLOCKS + n] * BLOCK_ROWS, BLOCK_ROWS), BLOCK_ROWS)
            for h in range(SHARE):
                part = (n * SHARE + h) * BLOCK_ROWS
                dq_acc[rows, h * HEAD_DIM : (h + 1) * HEAD_DIM] = dq[part : part + BLOCK_ROWS]
        return carry

    lax.fori_loop(0, TILES, place_queries, 0, unroll=UNROLL_PREP)

    def finish_queries(step, carry):
        dq_ref[step] = dq_acc[pl.ds(pl.multiple_of(step * RUN, RUN), RUN), :].astype(BF16)
        return carry

    lax.fori_loop(0, PEERS, finish_queries, 0, unroll=2)

    def finish_keys(step, carry):
        first = pl.multiple_of(packed_to[2 * step] * BLOCK_ROWS, BLOCK_ROWS)
        second = pl.multiple_of(packed_to[2 * step + 1] * BLOCK_ROWS, BLOCK_ROWS)
        for src, dst, scale in ((dk_acc, dk_ref, SCORE_SCALE), (dv_acc, dv_ref, 1.0)):
            rows = jnp.concatenate([src[pl.ds(first, BLOCK_ROWS), :], src[pl.ds(second, BLOCK_ROWS), :]], axis=0)
            dst[step] = (rows * scale).astype(BF16)
        return carry

    lax.fori_loop(0, GROUP_BLOCKS // 2, finish_keys, 0, unroll=8)


def attention(block_target, doc_lengths, queries, grads, keys, values):
    narrow = jax.ShapeDtypeStruct((GROUP_BLOCKS // 2, RUN, HEAD_DIM), BF16)
    return pl.pallas_call(
        attention_kernel,
        name="attention",
        out_shape=(jax.ShapeDtypeStruct((PEERS, RUN, UNIT), BF16), narrow, narrow),
        in_specs=[pl.BlockSpec(memory_space=pltpu.SMEM)] * 2 + [pl.BlockSpec(memory_space=pltpu.VMEM)] * 4,
        out_specs=[pl.BlockSpec(memory_space=pltpu.VMEM)] * 3,
        scratch_shapes=[
            pltpu.SMEM((GROUP_BLOCKS,), jnp.int32),
            pltpu.SMEM((GROUP_BLOCKS,), jnp.int32),
            pltpu.SMEM((PLANE_BLOCKS + 1,), jnp.int32),
            pltpu.SMEM((PLANE_BLOCKS + 1,), jnp.int32),
            pltpu.SMEM((DOCS,), jnp.int32),
            pltpu.VMEM((GROUP_TOKENS, HEAD_DIM), BF16),
            pltpu.VMEM((GROUP_TOKENS, HEAD_DIM), BF16),
            pltpu.VMEM((TILES, TILE_ROWS, HEAD_DIM), BF16),
            pltpu.VMEM((TILES, TILE_ROWS, HEAD_DIM), BF16),
            pltpu.VMEM((TILES, 8, TILE_ROWS), jnp.int32),
            pltpu.SMEM((2 * TILES,), jnp.int32),
            pltpu.VMEM((CHUNKS, HEAD_DIM, CHUNK), BF16),
            pltpu.VMEM((GROUP_TOKENS, HEAD_DIM), F32),
            pltpu.VMEM((GROUP_TOKENS, HEAD_DIM), F32),
            pltpu.VMEM((TILES, HEAD_DIM, TILE_ROWS), F32),
            pltpu.VMEM((PLANE_BLOCKS * BLOCK_ROWS, UNIT), F32),
            pltpu.VMEM((CHUNKS, CHUNK, TILE_ROWS), F32),
            pltpu.VMEM((CHUNKS, CHUNK, TILE_ROWS), F32),
            pltpu.VMEM((CHUNKS, 8, TILE_ROWS), F32),
        ],
        compiler_params=pltpu.CompilerParams(vmem_limit_bytes=34 * 1024 * 1024),
    )(block_target, doc_lengths, queries, grads, keys, values)


def collect_kernel(
    dq_ref,
    dk_ref,
    dv_ref,
    dq_out,
    dk_out,
    dv_out,
    inbox,
    total,
    send_sem,
    recv_sem,
    own_sem,
    ring_send,
    ring_recv,
):
    group, head, plane = place()
    me = group * KV_HEADS + head
    greet(group, head, plane)
    here = device_of(group, head, plane)
    parts = (dk_ref, dv_ref)
    outs = (dk_out, dv_out)

    def home_of(ref, width):
        return ref.at[
            pl.ds(pl.multiple_of(group * RUN, RUN), RUN), pl.ds(pl.multiple_of(head * width, width), width)
        ]

    def owner_of(slot):
        peer = lax.rem(me + PEERS - slot, PEERS)
        return device_of(peer // KV_HEADS, lax.rem(peer, KV_HEADS), plane)

    def send_wide(slot, carry):
        remote(dq_ref.at[slot], home_of(dq_out, UNIT), send_sem.at[2], recv_sem.at[2], owner_of(slot)).start()
        return carry

    def ring(way, step, n, part, src):
        target = lax.rem(plane + (1 if way == 0 else PLANES - 1), PLANES)
        return remote(
            src,
            inbox.at[way, n, step, pl.ds(part * PART, PART)],
            ring_send.at[way, n],
            ring_recv.at[way, step, n, part],
            device_of(group, head, target),
        )

    def chunk_at(way, step):
        distance = 4 - step
        return lax.rem(plane + (distance if way == 0 else PLANES - distance), PLANES)

    for step in range(4):
        for part in range(PARTS):
            piece = pl.ds(part * PART, PART)
            for n in range(2):
                for way in range(2):
                    chunk = chunk_at(way, step)
                    if step == 0 and n != way:
                        continue
                    if step == 0 or (step == 1 and n != way):
                        ring(way, step, n, part, parts[n].at[chunk, piece]).start()
                    else:
                        held = inbox.at[way, n, step - 1, piece]
                        ring(way, step - 1, n, part, held).wait_recv()
                        held[...] = (held[...].astype(F32) + parts[n][chunk, piece].astype(F32)).astype(BF16)
                        ring(way, step, n, part, held).start()
        if step == 0:
            own_wide = pltpu.make_async_copy(dq_ref.at[0], home_of(dq_out, UNIT), own_sem.at[2])
            own_wide.start()
            lax.fori_loop(1, PEERS, send_wide, 0)
    own = [pltpu.make_async_copy(total.at[n, 0], home_of(outs[n], HEAD_DIM), own_sem.at[n]) for n in range(2)]
    for part in range(PARTS):
        piece = pl.ds(part * PART, PART)
        for n in range(2):
            for way in range(2):
                ring(way, 3, n, part, inbox.at[way, n, 3, piece]).wait_recv()
            total[n, piece] = (
                parts[n][plane, piece].astype(F32)
                + inbox[0, n, 3, piece].astype(F32)
                + inbox[1, n, 3, piece].astype(F32)
            ).astype(BF16)

            def send_narrow(slot, carry):
                remote(
                    total.at[n, slot], home_of(outs[n], HEAD_DIM), send_sem.at[n], recv_sem.at[n], owner_of(slot)
                ).start()
                return carry

            if part == 0:
                own[n].start()
            lax.fori_loop(max(1, part * PART), (part + 1) * PART, send_narrow, 0)
    for way in range(2):
        for n in range(2):
            sent = inbox.at[way, n, pl.ds(0, 4 if n == way else 3)]
            remote(sent, sent, ring_send.at[way, n], ring_recv.at[way, 0, n, 0], here).wait_send()
    own_wide.wait()
    sent = dq_ref.at[pl.ds(0, PEERS - 1)]
    rest = remote(sent, sent, send_sem.at[2], recv_sem.at[2], here)
    rest.wait_send()
    rest.wait_recv()
    for n in range(2):
        sent = total.at[n, pl.ds(0, PEERS - 1)]
        rest = remote(sent, sent, send_sem.at[n], recv_sem.at[n], here)
        rest.wait_send()
        rest.wait_recv()
        own[n].wait()


def collect(dq, dk, dv):
    return pl.pallas_call(
        collect_kernel,
        name="collect",
        out_shape=(
            jax.ShapeDtypeStruct((GROUPS * RUN, KV_HEADS * UNIT), BF16),
            jax.ShapeDtypeStruct((GROUPS * RUN, KV_HEADS * HEAD_DIM), BF16),
            jax.ShapeDtypeStruct((GROUPS * RUN, KV_HEADS * HEAD_DIM), BF16),
        ),
        in_specs=[
            pl.BlockSpec(memory_space=pl.ANY),
            pl.BlockSpec(memory_space=pltpu.VMEM),
            pl.BlockSpec(memory_space=pltpu.VMEM),
        ],
        out_specs=[pl.BlockSpec(memory_space=pl.ANY)] * 3,
        scratch_shapes=[
            pltpu.VMEM((2, 2, 4, PEERS, RUN, HEAD_DIM), BF16),
            pltpu.VMEM((2, PEERS, RUN, HEAD_DIM), BF16),
            pltpu.SemaphoreType.DMA((3,)),
            pltpu.SemaphoreType.DMA((3,)),
            pltpu.SemaphoreType.DMA((3,)),
            pltpu.SemaphoreType.DMA((2, 2)),
            pltpu.SemaphoreType.DMA((2, 4, 2, PARTS)),
        ],
        compiler_params=pltpu.CompilerParams(
            collective_id=1, has_side_effects=True, vmem_limit_bytes=12 * 1024 * 1024
        ),
    )(dq, dk, dv)


def on_device(query_rows, key_rows, value_rows, output_grad, block_target, doc_lengths):
    queries, grads, keys, values = scatter(query_rows, output_grad, key_rows, value_rows)
    pairs = (GROUP_BLOCKS // 2, RUN, HEAD_DIM)
    dq, dk, dv = attention(block_target, doc_lengths, queries, grads, keys.reshape(pairs), values.reshape(pairs))
    planes = (PLANES, PEERS, RUN, HEAD_DIM)
    return collect(dq, dk.reshape(planes), dv.reshape(planes))


def solution(mesh):
    in_specs = (
        P(("grp", "ctx"), None),
        P(("grp", "ctx"), None),
        P(("grp", "ctx"), None),
        P(("grp", "ctx"), None),
        P(),
        P("grp", None),
    )
    out_specs = (P(("grp", "ctx"), None), P(("grp", "ctx"), None), P(("grp", "ctx"), None))
    return jax.shard_map(
        on_device, mesh=mesh, in_specs=in_specs, out_specs=out_specs, check_vma=False
    )
```

```python
import jax
import jax.numpy as jnp
from jax import lax
from jax.experimental import pallas as pl
from jax.experimental.pallas import tpu as pltpu
from jax.sharding import PartitionSpec as P

KV_HEADS = 4
HEAD_DIM = 128
SHARE = 8
BLOCK_ROWS = 8
GROUPS = 8
PLANES = 8
PEERS = 32
RUN = 16
UNIT = SHARE * HEAD_DIM
GROUP_BLOCKS = 512
GROUP_TOKENS = 4096
PLANE_BLOCKS = 64
DOCS = 16
TILE_BLOCKS = 4
TILE_ROWS = TILE_BLOCKS * SHARE * BLOCK_ROWS
TILES = PLANE_BLOCKS // TILE_BLOCKS
CHUNK = 128
CHUNKS = GROUP_TOKENS // CHUNK
FIXED_MAX = 7
TOGETHER = 2
UNROLL_PREP = 2
SCORE_SCALE = HEAD_DIM**-0.5
EXP2_SCALE = SCORE_SCALE * 1.4426950408889634
PARTS = 4
PART = PEERS // PARTS
WIDE_STEPS = (1, 32, 32, 32, 32)
MESH = pl.DeviceIdType.MESH
F32 = jnp.float32
BF16 = jnp.bfloat16


def place():
    group = lax.axis_index("grp")
    ctx = lax.axis_index("ctx")
    y_hi = ctx // 16
    plane = (ctx // 2) % PLANES
    core = ctx % 2
    head = y_hi * 2 + core
    return group, head, plane


def device_of(group, head, plane):
    return {"grp": group, "ctx": (head // 2) * 16 + plane * 2 + head % 2}


def greet(group, head, plane):
    barrier = pltpu.get_barrier_semaphore()
    me = group * KV_HEADS + head

    def one(step, carry):
        peer = lax.rem(me + step, PEERS)
        pl.semaphore_signal(
            barrier,
            inc=1,
            device_id=device_of(peer // KV_HEADS, lax.rem(peer, KV_HEADS), plane),
            device_id_type=MESH,
        )
        return carry

    lax.fori_loop(1, PEERS, one, 0)
    for by in (1, PLANES - 1):
        pl.semaphore_signal(
            barrier,
            inc=1,
            device_id=device_of(group, head, lax.rem(plane + by, PLANES)),
            device_id_type=MESH,
        )
    pl.semaphore_wait(barrier, PEERS - 1 + 2)


def remote(src, dst, send, recv, device):
    return pltpu.make_async_remote_copy(
        src_ref=src, dst_ref=dst, send_sem=send, recv_sem=recv, device_id=device, device_id_type=MESH
    )


def scatter_kernel(
    q_ref,
    g_ref,
    k_ref,
    v_ref,
    target_ref,
    length_ref,
    q_out,
    g_out,
    k_out,
    v_out,
    target_out,
    length_out,
    send_sem,
    narrow_recv,
    wide_recv,
    own_sem,
    ring_send,
    ring_recv,
):
    group, head, plane = place()
    me = group * KV_HEADS + head
    greet(group, head, plane)
    here = device_of(group, head, plane)
    narrow = ((k_ref, k_out), (v_ref, v_out))
    wide = ((q_ref, q_out), (g_ref, g_out))

    def run_of(ref, to_group, to_head, width):
        return ref.at[
            pl.ds(pl.multiple_of(to_group * RUN, RUN), RUN),
            pl.ds(pl.multiple_of(to_head * width, width), width),
        ]

    def send_narrow(step, carry):
        peer = lax.rem(me + step, PEERS)
        to_group, to_head = peer // KV_HEADS, lax.rem(peer, KV_HEADS)
        for n, (src, dst) in enumerate(narrow):
            remote(
                run_of(src, to_group, to_head, HEAD_DIM),
                dst.at[plane, step],
                send_sem.at[n],
                narrow_recv.at[n, step // PART],
                device_of(to_group, to_head, plane),
            ).start()
        return carry

    def send_wide(step, carry):
        peer = lax.rem(me + step, PEERS)
        to_group, to_head = peer // KV_HEADS, lax.rem(peer, KV_HEADS)
        for n, (src, dst) in enumerate(wide):
            remote(
                run_of(src, to_group, to_head, UNIT),
                dst.at[step],
                send_sem.at[2 + n],
                wide_recv.at[n],
                device_of(to_group, to_head, plane),
            ).start()
        return carry

    own = [
        pltpu.make_async_copy(run_of(src, group, head, HEAD_DIM), dst.at[plane, 0], own_sem.at[n])
        for n, (src, dst) in enumerate(narrow)
    ] + [
        pltpu.make_async_copy(run_of(src, group, head, UNIT), dst.at[0], own_sem.at[2 + n])
        for n, (src, dst) in enumerate(wide)
    ]
    own += [
        pltpu.make_async_copy(target_ref, target_out, own_sem.at[4]),
        pltpu.make_async_copy(length_ref, length_out, own_sem.at[5]),
    ]
    own[0].start()
    own[1].start()
    lax.fori_loop(1, PEERS, send_narrow, 0)
    for copy in own[2:]:
        copy.start()

    def ring(way, step, n, part):
        chunk = lax.rem(plane + (PLANES - step if way == 0 else step), PLANES)
        target = lax.rem(plane + (1 if way == 0 else PLANES - 1), PLANES)
        piece = narrow[n][1].at[chunk, pl.ds(part * PART, PART)]
        return remote(
            piece,
            piece,
            ring_send.at[way, n],
            ring_recv.at[way, step, n, part],
            device_of(group, head, target),
        )

    for step in range(4):
        lax.fori_loop(WIDE_STEPS[step], WIDE_STEPS[step + 1], send_wide, 0)
        for part in range(PARTS):
            for n in range(2):
                if step == 0:
                    if part == 0:
                        own[n].wait()
                    landed = narrow[n][1].at[plane, pl.ds(part * PART, PART - (part == 0))]
                    remote(landed, landed, send_sem.at[n], narrow_recv.at[n, part], here).wait_recv()
                for way in range(2):
                    if step == 3 and n != way:
                        continue
                    if step > 0:
                        ring(way, step - 1, n, part).wait_recv()
                    ring(way, step, n, part).start()
    for part in range(PARTS):
        for way in range(2):
            ring(way, 2, 1 - way, part).wait_recv()
    for part in range(PARTS):
        for way in range(2):
            ring(way, 3, way, part).wait_recv()
    for way in range(2):
        for n in range(2):
            sent = narrow[n][1].at[pl.ds(0, 4 if n == way else 3)]
            remote(sent, sent, ring_send.at[way, n], ring_recv.at[way, 0, n, 0], here).wait_send()
    own[4].wait()
    own[5].wait()
    for n in range(2):
        sent = narrow[n][1].at[0, pl.ds(0, PEERS - 1)]
        remote(sent, sent, send_sem.at[n], narrow_recv.at[n, 0], here).wait_send()
        own[2 + n].wait()
        landed = wide[n][1].at[pl.ds(0, PEERS - 1)]
        rest = remote(landed, landed, send_sem.at[2 + n], wide_recv.at[n], here)
        rest.wait_recv()
        rest.wait_send()


def scatter(query_rows, output_grad, key_rows, value_rows, block_target, doc_lengths):
    wide = jax.ShapeDtypeStruct((PEERS, RUN, UNIT), BF16)
    narrow = jax.ShapeDtypeStruct((PLANES, PEERS, RUN, HEAD_DIM), BF16)
    return pl.pallas_call(
        scatter_kernel,
        name="scatter",
        out_shape=(
            wide,
            wide,
            narrow,
            narrow,
            jax.ShapeDtypeStruct(block_target.shape, jnp.int32),
            jax.ShapeDtypeStruct(doc_lengths.shape, jnp.int32),
        ),
        in_specs=[pl.BlockSpec(memory_space=pltpu.HBM)] * 6,
        out_specs=[pl.BlockSpec(memory_space=pl.ANY)] * 4 + [pl.BlockSpec(memory_space=pltpu.SMEM)] * 2,
        scratch_shapes=[
            pltpu.SemaphoreType.DMA((4,)),
            pltpu.SemaphoreType.DMA((2, PARTS)),
            pltpu.SemaphoreType.DMA((2,)),
            pltpu.SemaphoreType.DMA((6,)),
            pltpu.SemaphoreType.DMA((2, 2)),
            pltpu.SemaphoreType.DMA((2, 4, 2, PARTS)),
        ],
        compiler_params=pltpu.CompilerParams(
            collective_id=0, has_side_effects=True, vmem_limit_bytes=2 * 1024 * 1024
        ),
    )(
        *(
            pltpu.with_memory_space_constraint(rows, pltpu.HBM)
            for rows in (query_rows, output_grad, key_rows, value_rows, block_target, doc_lengths)
        )
    )


def attention_kernel(
    target_ref,
    length_ref,
    q_ref,
    g_ref,
    k_ref,
    v_ref,
    dq_ref,
    dk_ref,
    dv_ref,
    packed_to,
    holder,
    query_order,
    query_block,
    doc_ends,
    k_pack,
    v_pack,
    q_tiles,
    g_tiles,
    bounds,
    spans,
    k_turned,
    dk_acc,
    dv_acc,
    dq_turned,
    dq_acc,
    exps,
    probs,
    maxes,
):
    def half_of(pair, which):
        wide = pair.astype(F32)
        return jnp.where(which == 0, wide[:BLOCK_ROWS], wide[BLOCK_ROWS:])

    group, head, plane = place()
    me = group * KV_HEADS + head

    def target_of(source, from_plane, which):
        ctx = ((source >> 1) & 1) * 16 + (source & 1) + from_plane * 2
        return target_ref[source >> 2, 2 * group + which, ctx] - group * GROUP_BLOCKS

    def clear(step, carry):
        holder[step] = 0
        return carry

    lax.fori_loop(0, GROUP_BLOCKS, clear, 0, unroll=16)

    def hold(slot, carry):
        for which in range(2):
            holder[target_of((me - slot) & (PEERS - 1), plane, which)] = 2 * slot + which + 1
        return carry

    lax.fori_loop(0, PEERS, hold, 0, unroll=4)

    end = jnp.int32(0)
    for n in range(DOCS):
        end = end + length_ref[0, n]
        doc_ends[n] = end

    def pack(source, carry):
        slot = (me - source) & (PEERS - 1)
        for from_plane in range(PLANES):
            pair = from_plane * PEERS + slot
            keys = k_ref[pair].astype(F32)
            values = v_ref[pair].astype(F32)
            for which in range(2):
                block = target_of(source, from_plane, which)
                packed_to[2 * pair + which] = block
                rows = pl.ds(pl.multiple_of(block * BLOCK_ROWS, BLOCK_ROWS), BLOCK_ROWS)
                half = slice(which * BLOCK_ROWS, (which + 1) * BLOCK_ROWS)
                dk_acc[rows, :] = keys[half]
                dv_acc[rows, :] = values[half]
        return carry

    lax.fori_loop(0, PEERS, pack, 0, unroll=2)

    def turn(step, found):
        rows = pl.ds(pl.multiple_of(step * CHUNK, CHUNK), CHUNK)
        keys = dk_acc[rows, :]
        k_pack[rows, :] = keys.astype(BF16)
        k_turned[step] = jnp.transpose(keys).astype(BF16)
        v_pack[rows, :] = dv_acc[rows, :].astype(BF16)
        dk_acc[rows, :] = jnp.zeros((CHUNK, HEAD_DIM), F32)
        dv_acc[rows, :] = jnp.zeros((CHUNK, HEAD_DIM), F32)
        for n in range(CHUNK // BLOCK_ROWS):
            block = step * (CHUNK // BLOCK_ROWS) + n
            slot = holder[block]
            query_order[found] = slot - 1
            query_block[found] = block
            found = found + jnp.where(slot > 0, 1, 0)
        return found

    lax.fori_loop(0, CHUNKS, turn, jnp.int32(0), unroll=2)

    lane = lax.broadcasted_iota(jnp.int32, (1, TILE_ROWS), 1)
    owner = lane // (SHARE * BLOCK_ROWS)

    def prepare(tile, carry):
        slots = [query_order[tile * TILE_BLOCKS + n] for n in range(TILE_BLOCKS)]
        blocks = [query_block[tile * TILE_BLOCKS + n] for n in range(TILE_BLOCKS)]
        for src, dst in ((q_ref, q_tiles), (g_ref, g_tiles)):
            parts = []
            for slot in slots:
                rows = half_of(src[slot >> 1], slot & 1)
                parts += [rows[:, h * HEAD_DIM : (h + 1) * HEAD_DIM] for h in range(SHARE)]
            dst[tile] = jnp.concatenate(parts, axis=0).astype(BF16)
        last = jnp.full((1, TILE_ROWS), blocks[0], jnp.int32)
        for n in range(1, TILE_BLOCKS):
            last = jnp.where(owner == n, blocks[n], last)
        last = last * BLOCK_ROWS + (lane & (BLOCK_ROWS - 1))
        start = jnp.zeros((1, TILE_ROWS), jnp.int32)
        tile_start = jnp.int32(0)
        for n in range(DOCS):
            end = doc_ends[n]
            start = jnp.where(end <= last, end, start)
            tile_start = jnp.where(end <= blocks[0] * BLOCK_ROWS, end, tile_start)
        bounds[tile, 0:1] = start
        bounds[tile, 1:2] = last
        first_chunk = tile_start // CHUNK
        spans[2 * tile] = first_chunk
        spans[2 * tile + 1] = (blocks[-1] * BLOCK_ROWS + BLOCK_ROWS - 1) // CHUNK - first_chunk + 1
        return carry

    lax.fori_loop(0, TILES, prepare, 0, unroll=UNROLL_PREP)

    key_iota = lax.broadcasted_iota(jnp.int32, (CHUNK, TILE_ROWS), 0)
    no_sum = jnp.zeros((8, TILE_ROWS), F32)

    def fold(array, op):
        return op(array.reshape(CHUNK // 8, 8, TILE_ROWS), axis=0)

    def rows_of(chunk):
        return pl.ds(pl.multiple_of(chunk * CHUNK, CHUNK), CHUNK)

    def against(rows_ref, chunk, tile_rows):
        return lax.dot_general(
            rows_ref[rows_of(chunk), :], tile_rows, (((1,), (1,)), ((), ())), preferred_element_type=F32
        )

    def masked(scores, chunk, start, last):
        position = key_iota + chunk * CHUNK
        return jnp.where((position >= start) & (position <= last), scores, -1e30)

    def put_keys(chunk, weights, score_grad, q_low, g_low):
        rows = rows_of(chunk)
        dv_acc[rows, :] += jnp.dot(weights.astype(BF16), g_low, preferred_element_type=F32)
        dk_acc[rows, :] += jnp.dot(score_grad, q_low, preferred_element_type=F32)
        return jnp.dot(k_turned[chunk], score_grad, preferred_element_type=F32)

    def query_tiles(step, carry):
        tiles = [step * TOGETHER + n for n in range(TOGETHER)]
        firsts = [spans[2 * tile] for tile in tiles]
        counts = [spans[2 * tile + 1] for tile in tiles]
        most = counts[0]
        for count in counts[1:]:
            most = jnp.maximum(most, count)

        def fixed(chunks):
            begins = [jnp.minimum(first, CHUNKS - chunks) for first in firsts]
            ways = range(TOGETHER)
            q_low = [q_tiles[tile] for tile in tiles]
            g_low = [g_tiles[tile] for tile in tiles]
            start = [bounds[tile, 0:1] for tile in tiles]
            last = [bounds[tile, 1:2] for tile in tiles]
            top = [jnp.full((8, TILE_ROWS), -1e30, F32)] * TOGETHER
            for n in range(chunks):
                for w in ways:
                    chunk = begins[w] + n
                    scores = masked(against(k_pack, chunk, q_low[w]), chunk, start[w], last[w])
                    exps[w * FIXED_MAX + n] = scores
                    top[w] = jnp.maximum(top[w], fold(scores, jnp.max))
            top = [jnp.max(t, axis=0, keepdims=True) for t in top]
            total, weighted = [no_sum] * TOGETHER, [no_sum] * TOGETHER
            for n in range(chunks):
                for w in ways:
                    prob_grad = against(v_pack, begins[w] + n, g_low[w])
                    weights = jnp.exp2((exps[w * FIXED_MAX + n] - top[w]) * EXP2_SCALE)
                    total[w] += fold(weights, jnp.sum)
                    weighted[w] += fold(weights * prob_grad, jnp.sum)
                    exps[w * FIXED_MAX + n] = weights
                    probs[w * FIXED_MAX + n] = prob_grad
            factor = [1.0 / jnp.sum(t, axis=0, keepdims=True) for t in total]
            delta = [jnp.sum(t, axis=0, keepdims=True) * f for t, f in zip(weighted, factor)]
            dq = [jnp.zeros((HEAD_DIM, TILE_ROWS), F32)] * TOGETHER
            for n in range(chunks):
                for w in ways:
                    weights = exps[w * FIXED_MAX + n] * factor[w]
                    score_grad = (weights * (probs[w * FIXED_MAX + n] - delta[w])).astype(BF16)
                    dq[w] += put_keys(begins[w] + n, weights, score_grad, q_low[w], g_low[w])
            for w in ways:
                dq_turned[tiles[w]] = dq[w]

        for chunks in range(1, FIXED_MAX + 1):

            @pl.when(most == chunks)
            def _():
                fixed(chunks)

        @pl.when(most > FIXED_MAX)
        def _():
            for tile, first, count in zip(tiles, firsts, counts):
                any_length(tile, first, count)

        return carry

    def any_length(tile, first, count):
        q_low, g_low = q_tiles[tile], g_tiles[tile]
        start, last = bounds[tile, 0:1], bounds[tile, 1:2]

        def totals(slot, state):
            top, total, weighted = state
            chunk = first + slot
            scores = masked(against(k_pack, chunk, q_low), chunk, start, last)
            prob_grad = against(v_pack, chunk, g_low)
            new_top = jnp.maximum(top, jnp.max(scores, axis=0, keepdims=True))
            weights = jnp.exp2((scores - new_top) * EXP2_SCALE)
            fade = jnp.exp2((top - new_top) * EXP2_SCALE)
            total = total * fade + jnp.sum(weights, axis=0, keepdims=True)
            weighted = weighted * fade + jnp.sum(weights * prob_grad, axis=0, keepdims=True)
            exps[slot] = weights
            probs[slot] = prob_grad
            maxes[slot] = jnp.broadcast_to(new_top, (8, TILE_ROWS))
            return new_top, total, weighted

        top, total, weighted = lax.fori_loop(
            0, count, totals, (jnp.full((1, TILE_ROWS), -1e20, F32), no_sum[:1], no_sum[:1])
        )
        scale_row = 1.0 / total
        delta = weighted * scale_row

        def gradients(slot, dq):
            factor = jnp.exp2((maxes[slot][:1] - top) * EXP2_SCALE) * scale_row
            weights = exps[slot] * factor
            score_grad = (weights * (probs[slot] - delta)).astype(BF16)
            return dq + put_keys(first + slot, weights, score_grad, q_low, g_low)

        dq_turned[tile] = lax.fori_loop(0, count, gradients, jnp.zeros((HEAD_DIM, TILE_ROWS), F32))

    lax.fori_loop(0, TILES // TOGETHER, query_tiles, 0)

    def place_queries(tile, carry):
        dq = jnp.transpose(dq_turned[tile]) * SCORE_SCALE
        for n in range(TILE_BLOCKS):
            rows = pl.ds(pl.multiple_of(query_order[tile * TILE_BLOCKS + n] * BLOCK_ROWS, BLOCK_ROWS), BLOCK_ROWS)
            for h in range(SHARE):
                part = (n * SHARE + h) * BLOCK_ROWS
                dq_acc[rows, h * HEAD_DIM : (h + 1) * HEAD_DIM] = dq[part : part + BLOCK_ROWS]
        return carry

    lax.fori_loop(0, TILES, place_queries, 0, unroll=UNROLL_PREP)

    def finish_queries(step, carry):
        dq_ref[step] = dq_acc[pl.ds(pl.multiple_of(step * RUN, RUN), RUN), :].astype(BF16)
        return carry

    lax.fori_loop(0, PEERS, finish_queries, 0, unroll=2)

    def finish_keys(step, carry):
        first = pl.multiple_of(packed_to[2 * step] * BLOCK_ROWS, BLOCK_ROWS)
        second = pl.multiple_of(packed_to[2 * step + 1] * BLOCK_ROWS, BLOCK_ROWS)
        for src, dst, scale in ((dk_acc, dk_ref, SCORE_SCALE), (dv_acc, dv_ref, 1.0)):
            rows = jnp.concatenate([src[pl.ds(first, BLOCK_ROWS), :], src[pl.ds(second, BLOCK_ROWS), :]], axis=0)
            dst[step] = (rows * scale).astype(BF16)
        return carry

    lax.fori_loop(0, GROUP_BLOCKS // 2, finish_keys, 0, unroll=8)


def attention(block_target, doc_lengths, queries, grads, keys, values):
    narrow = jax.ShapeDtypeStruct((GROUP_BLOCKS // 2, RUN, HEAD_DIM), BF16)
    return pl.pallas_call(
        attention_kernel,
        name="attention",
        out_shape=(jax.ShapeDtypeStruct((PEERS, RUN, UNIT), BF16), narrow, narrow),
        in_specs=[pl.BlockSpec(memory_space=pltpu.SMEM)] * 2 + [pl.BlockSpec(memory_space=pltpu.VMEM)] * 4,
        out_specs=[pl.BlockSpec(memory_space=pltpu.VMEM)] * 3,
        scratch_shapes=[
            pltpu.SMEM((GROUP_BLOCKS,), jnp.int32),
            pltpu.SMEM((GROUP_BLOCKS,), jnp.int32),
            pltpu.SMEM((PLANE_BLOCKS + 1,), jnp.int32),
            pltpu.SMEM((PLANE_BLOCKS + 1,), jnp.int32),
            pltpu.SMEM((DOCS,), jnp.int32),
            pltpu.VMEM((GROUP_TOKENS, HEAD_DIM), BF16),
            pltpu.VMEM((GROUP_TOKENS, HEAD_DIM), BF16),
            pltpu.VMEM((TILES, TILE_ROWS, HEAD_DIM), BF16),
            pltpu.VMEM((TILES, TILE_ROWS, HEAD_DIM), BF16),
            pltpu.VMEM((TILES, 8, TILE_ROWS), jnp.int32),
            pltpu.SMEM((2 * TILES,), jnp.int32),
            pltpu.VMEM((CHUNKS, HEAD_DIM, CHUNK), BF16),
            pltpu.VMEM((GROUP_TOKENS, HEAD_DIM), F32),
            pltpu.VMEM((GROUP_TOKENS, HEAD_DIM), F32),
            pltpu.VMEM((TILES, HEAD_DIM, TILE_ROWS), F32),
            pltpu.VMEM((PLANE_BLOCKS * BLOCK_ROWS, UNIT), F32),
            pltpu.VMEM((CHUNKS, CHUNK, TILE_ROWS), F32),
            pltpu.VMEM((CHUNKS, CHUNK, TILE_ROWS), F32),
            pltpu.VMEM((CHUNKS, 8, TILE_ROWS), F32),
        ],
        compiler_params=pltpu.CompilerParams(vmem_limit_bytes=34 * 1024 * 1024),
    )(block_target, doc_lengths, queries, grads, keys, values)


def collect_kernel(
    dq_ref,
    dk_ref,
    dv_ref,
    dq_out,
    dk_out,
    dv_out,
    inbox,
    total,
    send_sem,
    recv_sem,
    own_sem,
    ring_send,
    ring_recv,
):
    group, head, plane = place()
    me = group * KV_HEADS + head
    greet(group, head, plane)
    here = device_of(group, head, plane)
    parts = (dk_ref, dv_ref)
    outs = (dk_out, dv_out)

    def home_of(ref, width):
        return ref.at[
            pl.ds(pl.multiple_of(group * RUN, RUN), RUN), pl.ds(pl.multiple_of(head * width, width), width)
        ]

    def owner_of(slot):
        peer = lax.rem(me + PEERS - slot, PEERS)
        return device_of(peer // KV_HEADS, lax.rem(peer, KV_HEADS), plane)

    def send_wide(slot, carry):
        remote(dq_ref.at[slot], home_of(dq_out, UNIT), send_sem.at[2], recv_sem.at[2], owner_of(slot)).start()
        return carry

    def ring(way, step, n, part, src):
        target = lax.rem(plane + (1 if way == 0 else PLANES - 1), PLANES)
        return remote(
            src,
            inbox.at[way, n, step, pl.ds(part * PART, PART)],
            ring_send.at[way, n],
            ring_recv.at[way, step, n, part],
            device_of(group, head, target),
        )

    def chunk_at(way, step):
        distance = 4 - step
        return lax.rem(plane + (distance if way == 0 else PLANES - distance), PLANES)

    for step in range(4):
        for part in range(PARTS):
            piece = pl.ds(part * PART, PART)
            for n in range(2):
                for way in range(2):
                    chunk = chunk_at(way, step)
                    if step == 0 and n != way:
                        continue
                    if step == 0 or (step == 1 and n != way):
                        ring(way, step, n, part, parts[n].at[chunk, piece]).start()
                    else:
                        held = inbox.at[way, n, step - 1, piece]
                        ring(way, step - 1, n, part, held).wait_recv()
                        held[...] = (held[...].astype(F32) + parts[n][chunk, piece].astype(F32)).astype(BF16)
                        ring(way, step, n, part, held).start()
        if step == 0:
            own_wide = pltpu.make_async_copy(dq_ref.at[0], home_of(dq_out, UNIT), own_sem.at[2])
            own_wide.start()
            lax.fori_loop(1, PEERS, send_wide, 0)
    own = [pltpu.make_async_copy(total.at[n, 0], home_of(outs[n], HEAD_DIM), own_sem.at[n]) for n in range(2)]
    for part in range(PARTS):
        piece = pl.ds(part * PART, PART)
        for n in range(2):
            for way in range(2):
                ring(way, 3, n, part, inbox.at[way, n, 3, piece]).wait_recv()
            total[n, piece] = (
                parts[n][plane, piece].astype(F32)
                + inbox[0, n, 3, piece].astype(F32)
                + inbox[1, n, 3, piece].astype(F32)
            ).astype(BF16)

            def send_narrow(slot, carry):
                remote(
                    total.at[n, slot], home_of(outs[n], HEAD_DIM), send_sem.at[n], recv_sem.at[n], owner_of(slot)
                ).start()
                return carry

            if part == 0:
                own[n].start()
            lax.fori_loop(max(1, part * PART), (part + 1) * PART, send_narrow, 0)
    for way in range(2):
        for n in range(2):
            sent = inbox.at[way, n, pl.ds(0, 4 if n == way else 3)]
            remote(sent, sent, ring_send.at[way, n], ring_recv.at[way, 0, n, 0], here).wait_send()
    own_wide.wait()
    sent = dq_ref.at[pl.ds(0, PEERS - 1)]
    rest = remote(sent, sent, send_sem.at[2], recv_sem.at[2], here)
    rest.wait_send()
    rest.wait_recv()
    for n in range(2):
        sent = total.at[n, pl.ds(0, PEERS - 1)]
        rest = remote(sent, sent, send_sem.at[n], recv_sem.at[n], here)
        rest.wait_send()
        rest.wait_recv()
        own[n].wait()


def collect(dq, dk, dv):
    return pl.pallas_call(
        collect_kernel,
        name="collect",
        out_shape=(
            jax.ShapeDtypeStruct((GROUPS * RUN, KV_HEADS * UNIT), BF16),
            jax.ShapeDtypeStruct((GROUPS * RUN, KV_HEADS * HEAD_DIM), BF16),
            jax.ShapeDtypeStruct((GROUPS * RUN, KV_HEADS * HEAD_DIM), BF16),
        ),
        in_specs=[
            pl.BlockSpec(memory_space=pl.ANY),
            pl.BlockSpec(memory_space=pltpu.VMEM),
            pl.BlockSpec(memory_space=pltpu.VMEM),
        ],
        out_specs=[pl.BlockSpec(memory_space=pl.ANY)] * 3,
        scratch_shapes=[
            pltpu.VMEM((2, 2, 4, PEERS, RUN, HEAD_DIM), BF16),
            pltpu.VMEM((2, PEERS, RUN, HEAD_DIM), BF16),
            pltpu.SemaphoreType.DMA((3,)),
            pltpu.SemaphoreType.DMA((3,)),
            pltpu.SemaphoreType.DMA((3,)),
            pltpu.SemaphoreType.DMA((2, 2)),
            pltpu.SemaphoreType.DMA((2, 4, 2, PARTS)),
        ],
        compiler_params=pltpu.CompilerParams(
            collective_id=1, has_side_effects=True, vmem_limit_bytes=12 * 1024 * 1024
        ),
    )(dq, dk, dv)


def deliver_kernel(*refs):
    copies = [pltpu.make_async_copy(refs[n], refs[3 + n], refs[6].at[n]) for n in range(3)]
    for copy in copies:
        copy.start()
    for copy in copies:
        copy.wait()


def deliver(*grads):
    return pl.pallas_call(
        deliver_kernel,
        name="deliver",
        out_shape=tuple(jax.ShapeDtypeStruct(grad.shape, grad.dtype) for grad in grads),
        in_specs=[pl.BlockSpec(memory_space=pl.ANY)] * 3,
        out_specs=[pl.BlockSpec(memory_space=pl.ANY)] * 3,
        scratch_shapes=[pltpu.SemaphoreType.DMA((3,))],
        compiler_params=pltpu.CompilerParams(vmem_limit_bytes=1024 * 1024),
    )(*grads)


def on_device(query_rows, key_rows, value_rows, output_grad, block_target, doc_lengths):
    queries, grads, keys, values, targets, lengths = scatter(
        query_rows, output_grad, key_rows, value_rows, block_target.transpose(0, 2, 1), doc_lengths
    )
    pairs = (GROUP_BLOCKS // 2, RUN, HEAD_DIM)
    dq, dk, dv = attention(targets, lengths, queries, grads, keys.reshape(pairs), values.reshape(pairs))
    planes = (PLANES, PEERS, RUN, HEAD_DIM)
    return deliver(*collect(dq, dk.reshape(planes), dv.reshape(planes)))


def solution(mesh):
    in_specs = (
        P(("grp", "ctx"), None),
        P(("grp", "ctx"), None),
        P(("grp", "ctx"), None),
        P(("grp", "ctx"), None),
        P(),
        P("grp", None),
    )
    out_specs = (P(("grp", "ctx"), None), P(("grp", "ctx"), None), P(("grp", "ctx"), None))
    return jax.shard_map(
        on_device, mesh=mesh, in_specs=in_specs, out_specs=out_specs, check_vma=False
    )
```

```python
import jax
import jax.numpy as jnp
from jax import lax
from jax.experimental import pallas as pl
from jax.experimental.pallas import tpu as pltpu
from jax.sharding import PartitionSpec as P

KV_HEADS = 4
HEAD_DIM = 128
SHARE = 8
BLOCK_ROWS = 8
GROUPS = 8
PLANES = 8
PEERS = 32
RUN = 16
UNIT = SHARE * HEAD_DIM
GROUP_BLOCKS = 512
GROUP_TOKENS = 4096
PLANE_BLOCKS = 64
DOCS = 16
TILE_BLOCKS = 4
TILE_ROWS = TILE_BLOCKS * SHARE * BLOCK_ROWS
TILE_PARTS = TILE_ROWS // BLOCK_ROWS
TILES = PLANE_BLOCKS // TILE_BLOCKS
CHUNK = 128
CHUNKS = GROUP_TOKENS // CHUNK
CHUNK_BLOCKS = CHUNK // BLOCK_ROWS
FIXED_MAX = 7
TOGETHER = 2
UNROLL_PREP = 2
SCORE_SCALE = HEAD_DIM**-0.5
EXP2_SCALE = SCORE_SCALE * 1.4426950408889634
PARTS = 4
PART = PEERS // PARTS
WIDE_EARLY = 4
WIDE_EACH = 2
MESH = pl.DeviceIdType.MESH
F32 = jnp.float32
BF16 = jnp.bfloat16


def place():
    group = lax.axis_index("grp")
    ctx = lax.axis_index("ctx")
    y_hi = ctx // 16
    plane = (ctx // 2) % PLANES
    core = ctx % 2
    head = y_hi * 2 + core
    return group, head, plane


def device_of(group, head, plane):
    return {"grp": group, "ctx": (head // 2) * 16 + plane * 2 + head % 2}


def half_of(pair, which):
    wide = pair.astype(F32)
    return jnp.where(which == 0, wide[:BLOCK_ROWS], wide[BLOCK_ROWS:])


def target_of(target_ref, group, source, from_plane, which):
    ctx = lax.rem(lax.div(source, 2), 2) * 16 + lax.rem(source, 2) + from_plane * 2
    return lax.rem(target_ref[lax.div(source, KV_HEADS), 2 * group + which, ctx], GROUP_BLOCKS)


def greet(group, head, plane):
    barrier = pltpu.get_barrier_semaphore()
    me = group * KV_HEADS + head

    def one(step, carry):
        peer = lax.rem(me + step, PEERS)
        pl.semaphore_signal(
            barrier,
            inc=1,
            device_id=device_of(peer // KV_HEADS, lax.rem(peer, KV_HEADS), plane),
            device_id_type=MESH,
        )
        return carry

    lax.fori_loop(1, PEERS, one, 0)
    for by in (1, PLANES - 1):
        pl.semaphore_signal(
            barrier,
            inc=1,
            device_id=device_of(group, head, lax.rem(plane + by, PLANES)),
            device_id_type=MESH,
        )
    pl.semaphore_wait(barrier, PEERS - 1 + 2)


def remote(src, dst, send, recv, device):
    return pltpu.make_async_remote_copy(
        src_ref=src, dst_ref=dst, send_sem=send, recv_sem=recv, device_id=device, device_id_type=MESH
    )


def scatter_kernel(
    q_ref,
    g_ref,
    k_ref,
    v_ref,
    target_ref,
    length_ref,
    q_out,
    g_out,
    k_pack,
    v_pack,
    k_turned,
    target_out,
    length_out,
    ranks_out,
    k_out,
    v_out,
    table,
    packed_from,
    send_sem,
    narrow_recv,
    wide_recv,
    own_sem,
    ring_send,
    ring_recv,
):
    group, head, plane = place()
    me = group * KV_HEADS + head
    greet(group, head, plane)
    here = device_of(group, head, plane)
    narrow = ((k_ref, k_out), (v_ref, v_out))
    wide = ((q_ref, q_out), (g_ref, g_out))

    def run_of(ref, to_group, to_head, width):
        return ref.at[
            pl.ds(pl.multiple_of(to_group * RUN, RUN), RUN),
            pl.ds(pl.multiple_of(to_head * width, width), width),
        ]

    def send_narrow(step, carry):
        peer = lax.rem(me + step, PEERS)
        to_group, to_head = peer // KV_HEADS, lax.rem(peer, KV_HEADS)
        for n, (src, dst) in enumerate(narrow):
            remote(
                run_of(src, to_group, to_head, HEAD_DIM),
                dst.at[plane, step],
                send_sem.at[n],
                narrow_recv.at[n, step // PART],
                device_of(to_group, to_head, plane),
            ).start()
        return carry

    def send_wide(step, carry):
        peer = lax.rem(me + step, PEERS)
        to_group, to_head = peer // KV_HEADS, lax.rem(peer, KV_HEADS)
        for n, (src, dst) in enumerate(wide):
            remote(
                run_of(src, to_group, to_head, UNIT),
                dst.at[step],
                send_sem.at[2 + n],
                wide_recv.at[n],
                device_of(to_group, to_head, plane),
            ).start()
        return carry

    own = [
        pltpu.make_async_copy(run_of(src, group, head, HEAD_DIM), dst.at[plane, 0], own_sem.at[n])
        for n, (src, dst) in enumerate(narrow)
    ] + [
        pltpu.make_async_copy(run_of(src, group, head, UNIT), dst.at[0], own_sem.at[2 + n])
        for n, (src, dst) in enumerate(wide)
    ]
    own += [
        pltpu.make_async_copy(target_ref, target_out, own_sem.at[4]),
        pltpu.make_async_copy(length_ref, length_out, own_sem.at[5]),
    ]
    own[0].start()
    own[1].start()
    lax.fori_loop(1, PEERS, send_narrow, 0)
    for copy in own[2:]:
        copy.start()

    def ring(way, step, n, part):
        chunk = lax.rem(plane + (PLANES - step if way == 0 else step), PLANES)
        target = lax.rem(plane + (1 if way == 0 else PLANES - 1), PLANES)
        piece = narrow[n][1].at[chunk, pl.ds(part * PART, PART)]
        return remote(
            piece,
            piece,
            ring_send.at[way, n],
            ring_recv.at[way, step, n, part],
            device_of(group, head, target),
        )

    def make_tables():
        own[4].wait()
        own[5].wait()
        lane = lax.broadcasted_iota(jnp.int32, (8, 128), 1)
        place_of = lax.broadcasted_iota(jnp.int32, (8, 128), 0) * 128 + lane

        def invert(source, inverse):
            slot = lax.rem(me + PEERS - source, PEERS)
            for from_plane in range(PLANES):
                for which in range(2):
                    block = target_of(target_out, group, source, from_plane, which)
                    inverse = jnp.where(place_of == block, 2 * (from_plane * PEERS + slot) + which, inverse)
            return inverse

        table[0] = lax.fori_loop(0, PEERS, invert, jnp.zeros((8, 128), jnp.int32))

        def mine(step):
            return target_of(target_out, group, lax.rem(me + PEERS - lax.div(step, 2), PEERS), plane, lax.rem(step, 2))

        blocks = lax.fori_loop(
            0,
            PLANE_BLOCKS,
            lambda step, blocks: jnp.where(lane == step, mine(step), blocks),
            jnp.full((8, 128), GROUP_BLOCKS, jnp.int32),
            unroll=8,
        )
        table[1] = lax.fori_loop(
            0,
            PLANE_BLOCKS,
            lambda step, rank: rank + jnp.where(blocks > mine(step), 1, 0),
            jnp.zeros((8, 128), jnp.int32),
            unroll=8,
        )
        for n, dst in enumerate((packed_from, ranks_out)):
            copy = pltpu.make_async_copy(table.at[n], dst, own_sem.at[6 + n])
            copy.start()
            copy.wait()

    lax.fori_loop(1, WIDE_EARLY, send_wide, 0)
    wide_next = WIDE_EARLY
    for step in range(4):
        for part in range(PARTS):
            for n in range(2):
                if step == 0:
                    if part == 0:
                        own[n].wait()
                    landed = narrow[n][1].at[plane, pl.ds(part * PART, PART - (part == 0))]
                    remote(landed, landed, send_sem.at[n], narrow_recv.at[n, part], here).wait_recv()
                for way in range(2):
                    if step == 3 and n != way:
                        continue
                    if step > 0:
                        ring(way, step - 1, n, part).wait_recv()
                    ring(way, step, n, part).start()
                wide_after = min(wide_next + WIDE_EACH, PEERS)
                lax.fori_loop(wide_next, wide_after, send_wide, 0)
                wide_next = wide_after
        if step == 1:
            make_tables()
    for part in range(PARTS):
        for way in range(2):
            ring(way, 2, 1 - way, part).wait_recv()
    for part in range(PARTS):
        for way in range(2):
            ring(way, 3, way, part).wait_recv()
    for way in range(2):
        for n in range(2):
            sent = narrow[n][1].at[pl.ds(0, 4 if n == way else 3)]
            remote(sent, sent, ring_send.at[way, n], ring_recv.at[way, 0, n, 0], here).wait_send()

    def pack(chunk, carry):
        first = chunk * CHUNK_BLOCKS
        rows = pl.ds(pl.multiple_of(chunk * CHUNK, CHUNK), CHUNK)
        held = [packed_from[lax.div(first + n, 128), lax.rem(first + n, 128)] for n in range(CHUNK_BLOCKS)]
        keys = jnp.concatenate([half_of(k_out[h >> 6, (h >> 1) & (PEERS - 1)], h & 1) for h in held], axis=0)
        k_pack[rows, :] = keys.astype(BF16)
        k_turned[chunk] = jnp.transpose(keys).astype(BF16)
        values = jnp.concatenate([half_of(v_out[h >> 6, (h >> 1) & (PEERS - 1)], h & 1) for h in held], axis=0)
        v_pack[rows, :] = values.astype(BF16)
        return carry

    lax.fori_loop(0, CHUNKS, pack, 0)
    for n in range(2):
        sent = narrow[n][1].at[0, pl.ds(0, PEERS - 1)]
        remote(sent, sent, send_sem.at[n], narrow_recv.at[n, 0], here).wait_send()
        own[2 + n].wait()
        landed = wide[n][1].at[pl.ds(0, PEERS - 1)]
        rest = remote(landed, landed, send_sem.at[2 + n], wide_recv.at[n], here)
        rest.wait_recv()
        rest.wait_send()


def scatter(query_rows, output_grad, key_rows, value_rows, block_target, doc_lengths):
    wide = jax.ShapeDtypeStruct((PEERS, RUN, UNIT), BF16)
    narrow = pltpu.VMEM((PLANES, PEERS, RUN, HEAD_DIM), BF16)
    packed = jax.ShapeDtypeStruct((GROUP_TOKENS, HEAD_DIM), BF16)
    return pl.pallas_call(
        scatter_kernel,
        name="scatter",
        out_shape=(
            wide,
            wide,
            packed,
            packed,
            jax.ShapeDtypeStruct((CHUNKS, HEAD_DIM, CHUNK), BF16),
            jax.ShapeDtypeStruct(block_target.shape, jnp.int32),
            jax.ShapeDtypeStruct(doc_lengths.shape, jnp.int32),
            jax.ShapeDtypeStruct((8, 128), jnp.int32),
        ),
        in_specs=[pl.BlockSpec(memory_space=pltpu.HBM)] * 6,
        out_specs=[pl.BlockSpec(memory_space=pl.ANY)] * 2
        + [pl.BlockSpec(memory_space=pltpu.VMEM)] * 3
        + [pl.BlockSpec(memory_space=pltpu.SMEM)] * 3,
        scratch_shapes=[
            narrow,
            narrow,
            pltpu.VMEM((2, 8, 128), jnp.int32),
            pltpu.SMEM((8, 128), jnp.int32),
            pltpu.SemaphoreType.DMA((4,)),
            pltpu.SemaphoreType.DMA((2, PARTS)),
            pltpu.SemaphoreType.DMA((2,)),
            pltpu.SemaphoreType.DMA((8,)),
            pltpu.SemaphoreType.DMA((2, 2)),
            pltpu.SemaphoreType.DMA((2, 4, 2, PARTS)),
        ],
        compiler_params=pltpu.CompilerParams(
            collective_id=0, has_side_effects=True, vmem_limit_bytes=10 * 1024 * 1024
        ),
    )(
        *(
            pltpu.with_memory_space_constraint(rows, pltpu.HBM)
            for rows in (query_rows, output_grad, key_rows, value_rows, block_target, doc_lengths)
        )
    )


def attention_kernel(
    length_ref,
    rank_ref,
    target_ref,
    q_ref,
    g_ref,
    k_pack,
    v_pack,
    k_turned,
    dq_turned,
    dk_acc,
    dv_acc,
    query_order,
    query_block,
    doc_ends,
    q_tiles,
    g_tiles,
    bounds,
    spans,
    exps,
    probs,
    maxes,
):
    group, head, plane = place()
    me = group * KV_HEADS + head

    def sort(step, carry):
        rank = rank_ref[0, step]
        query_order[rank] = step
        query_block[rank] = target_of(target_ref, group, lax.rem(me + PEERS - lax.div(step, 2), PEERS), plane, lax.rem(step, 2))
        return carry

    lax.fori_loop(0, PLANE_BLOCKS, sort, 0, unroll=8)

    end = jnp.int32(0)
    for n in range(DOCS):
        end = end + length_ref[0, n]
        doc_ends[n] = end

    def clear(step, carry):
        rows = pl.ds(pl.multiple_of(step * CHUNK, CHUNK), CHUNK)
        dk_acc[rows, :] = jnp.zeros((CHUNK, HEAD_DIM), F32)
        dv_acc[rows, :] = jnp.zeros((CHUNK, HEAD_DIM), F32)
        return carry

    lax.fori_loop(0, CHUNKS, clear, 0, unroll=2)

    lane = lax.broadcasted_iota(jnp.int32, (1, TILE_ROWS), 1)
    owner = lane // (SHARE * BLOCK_ROWS)

    def prepare(tile, carry):
        slots = [query_order[tile * TILE_BLOCKS + n] for n in range(TILE_BLOCKS)]
        blocks = [query_block[tile * TILE_BLOCKS + n] for n in range(TILE_BLOCKS)]
        for src, dst in ((q_ref, q_tiles), (g_ref, g_tiles)):
            parts = []
            for slot in slots:
                rows = half_of(src[slot >> 1], slot & 1)
                parts += [rows[:, h * HEAD_DIM : (h + 1) * HEAD_DIM] for h in range(SHARE)]
            dst[tile] = jnp.concatenate(parts, axis=0).astype(BF16)
        last = jnp.full((1, TILE_ROWS), blocks[0], jnp.int32)
        for n in range(1, TILE_BLOCKS):
            last = jnp.where(owner == n, blocks[n], last)
        last = last * BLOCK_ROWS + (lane & (BLOCK_ROWS - 1))
        start = jnp.zeros((1, TILE_ROWS), jnp.int32)
        tile_start = jnp.int32(0)
        for n in range(DOCS):
            end = doc_ends[n]
            start = jnp.where(end <= last, end, start)
            tile_start = jnp.where(end <= blocks[0] * BLOCK_ROWS, end, tile_start)
        bounds[tile, 0:1] = start
        bounds[tile, 1:2] = last
        first_chunk = tile_start // CHUNK
        spans[2 * tile] = first_chunk
        spans[2 * tile + 1] = (blocks[-1] * BLOCK_ROWS + BLOCK_ROWS - 1) // CHUNK - first_chunk + 1
        return carry

    lax.fori_loop(0, TILES, prepare, 0, unroll=UNROLL_PREP)

    key_iota = lax.broadcasted_iota(jnp.int32, (CHUNK, TILE_ROWS), 0)
    no_sum = jnp.zeros((8, TILE_ROWS), F32)

    def fold(array, op):
        return op(array.reshape(CHUNK // 8, 8, TILE_ROWS), axis=0)

    def rows_of(chunk):
        return pl.ds(pl.multiple_of(chunk * CHUNK, CHUNK), CHUNK)

    def against(rows_ref, chunk, tile_rows):
        return lax.dot_general(
            rows_ref[rows_of(chunk), :], tile_rows, (((1,), (1,)), ((), ())), preferred_element_type=F32
        )

    def masked(scores, chunk, start, last):
        position = key_iota + chunk * CHUNK
        return jnp.where((position >= start) & (position <= last), scores, -1e30)

    def put_keys(chunk, weights, score_grad, q_low, g_low):
        rows = rows_of(chunk)
        dv_acc[rows, :] += jnp.dot(weights.astype(BF16), g_low, preferred_element_type=F32)
        dk_acc[rows, :] += jnp.dot(score_grad, q_low, preferred_element_type=F32)
        return jnp.dot(k_turned[chunk], score_grad, preferred_element_type=F32)

    def query_tiles(step, carry):
        tiles = [step * TOGETHER + n for n in range(TOGETHER)]
        firsts = [spans[2 * tile] for tile in tiles]
        counts = [spans[2 * tile + 1] for tile in tiles]
        most = counts[0]
        for count in counts[1:]:
            most = jnp.maximum(most, count)

        def fixed(chunks):
            begins = [jnp.minimum(first, CHUNKS - chunks) for first in firsts]
            ways = range(TOGETHER)
            q_low = [q_tiles[tile] for tile in tiles]
            g_low = [g_tiles[tile] for tile in tiles]
            start = [bounds[tile, 0:1] for tile in tiles]
            last = [bounds[tile, 1:2] for tile in tiles]
            top = [jnp.full((8, TILE_ROWS), -1e30, F32)] * TOGETHER
            for n in range(chunks):
                for w in ways:
                    chunk = begins[w] + n
                    scores = masked(against(k_pack, chunk, q_low[w]), chunk, start[w], last[w])
                    exps[w * FIXED_MAX + n] = scores
                    top[w] = jnp.maximum(top[w], fold(scores, jnp.max))
            top = [jnp.max(t, axis=0, keepdims=True) for t in top]
            total, weighted = [no_sum] * TOGETHER, [no_sum] * TOGETHER
            for n in range(chunks):
                for w in ways:
                    prob_grad = against(v_pack, begins[w] + n, g_low[w])
                    weights = jnp.exp2((exps[w * FIXED_MAX + n] - top[w]) * EXP2_SCALE)
                    total[w] += fold(weights, jnp.sum)
                    weighted[w] += fold(weights * prob_grad, jnp.sum)
                    exps[w * FIXED_MAX + n] = weights
                    probs[w * FIXED_MAX + n] = prob_grad
            factor = [1.0 / jnp.sum(t, axis=0, keepdims=True) for t in total]
            delta = [jnp.sum(t, axis=0, keepdims=True) * f for t, f in zip(weighted, factor)]
            dq = [jnp.zeros((HEAD_DIM, TILE_ROWS), F32)] * TOGETHER
            for n in range(chunks):
                for w in ways:
                    weights = exps[w * FIXED_MAX + n] * factor[w]
                    score_grad = (weights * (probs[w * FIXED_MAX + n] - delta[w])).astype(BF16)
                    dq[w] += put_keys(begins[w] + n, weights, score_grad, q_low[w], g_low[w])
            for w in ways:
                dq_turned[tiles[w]] = dq[w]

        for chunks in range(1, FIXED_MAX + 1):

            @pl.when(most == chunks)
            def _():
                fixed(chunks)

        @pl.when(most > FIXED_MAX)
        def _():
            for tile, first, count in zip(tiles, firsts, counts):
                any_length(tile, first, count)

        return carry

    def any_length(tile, first, count):
        q_low, g_low = q_tiles[tile], g_tiles[tile]
        start, last = bounds[tile, 0:1], bounds[tile, 1:2]

        def totals(slot, state):
            top, total, weighted = state
            chunk = first + slot
            scores = masked(against(k_pack, chunk, q_low), chunk, start, last)
            prob_grad = against(v_pack, chunk, g_low)
            new_top = jnp.maximum(top, jnp.max(scores, axis=0, keepdims=True))
            weights = jnp.exp2((scores - new_top) * EXP2_SCALE)
            fade = jnp.exp2((top - new_top) * EXP2_SCALE)
            total = total * fade + jnp.sum(weights, axis=0, keepdims=True)
            weighted = weighted * fade + jnp.sum(weights * prob_grad, axis=0, keepdims=True)
            exps[slot] = weights
            probs[slot] = prob_grad
            maxes[slot] = jnp.broadcast_to(new_top, (8, TILE_ROWS))
            return new_top, total, weighted

        top, total, weighted = lax.fori_loop(
            0, count, totals, (jnp.full((1, TILE_ROWS), -1e20, F32), no_sum[:1], no_sum[:1])
        )
        scale_row = 1.0 / total
        delta = weighted * scale_row

        def gradients(slot, dq):
            factor = jnp.exp2((maxes[slot][:1] - top) * EXP2_SCALE) * scale_row
            weights = exps[slot] * factor
            score_grad = (weights * (probs[slot] - delta)).astype(BF16)
            return dq + put_keys(first + slot, weights, score_grad, q_low, g_low)

        dq_turned[tile] = lax.fori_loop(0, count, gradients, jnp.zeros((HEAD_DIM, TILE_ROWS), F32))

    lax.fori_loop(0, TILES // TOGETHER, query_tiles, 0)


def attention(doc_lengths, ranks, block_target, queries, grads, keys, values, keys_turned):
    acc = jax.ShapeDtypeStruct((GROUP_TOKENS, HEAD_DIM), F32)
    return pl.pallas_call(
        attention_kernel,
        name="attention",
        out_shape=(jax.ShapeDtypeStruct((TILES, HEAD_DIM, TILE_ROWS), F32), acc, acc),
        in_specs=[pl.BlockSpec(memory_space=pltpu.SMEM)] * 3 + [pl.BlockSpec(memory_space=pltpu.VMEM)] * 5,
        out_specs=[pl.BlockSpec(memory_space=pltpu.VMEM)] * 3,
        scratch_shapes=[
            pltpu.SMEM((PLANE_BLOCKS,), jnp.int32),
            pltpu.SMEM((PLANE_BLOCKS,), jnp.int32),
            pltpu.SMEM((DOCS,), jnp.int32),
            pltpu.VMEM((TILES, TILE_ROWS, HEAD_DIM), BF16),
            pltpu.VMEM((TILES, TILE_ROWS, HEAD_DIM), BF16),
            pltpu.VMEM((TILES, 8, TILE_ROWS), jnp.int32),
            pltpu.SMEM((2 * TILES,), jnp.int32),
            pltpu.VMEM((CHUNKS, CHUNK, TILE_ROWS), F32),
            pltpu.VMEM((CHUNKS, CHUNK, TILE_ROWS), F32),
            pltpu.VMEM((CHUNKS, 8, TILE_ROWS), F32),
        ],
        compiler_params=pltpu.CompilerParams(vmem_limit_bytes=30 * 1024 * 1024),
    )(doc_lengths, ranks, block_target, queries, grads, keys, values, keys_turned)


def collect_kernel(
    rank_ref,
    target_ref,
    dq_turned,
    dk_ref,
    dv_ref,
    dq_out,
    dk_out,
    dv_out,
    dq_ref,
    dq_tiles,
    outbox,
    inbox,
    total,
    send_sem,
    recv_sem,
    own_sem,
    ring_send,
    ring_recv,
):
    group, head, plane = place()
    me = group * KV_HEADS + head
    greet(group, head, plane)
    here = device_of(group, head, plane)
    parts = (dk_ref, dv_ref)
    outs = (dk_out, dv_out)

    def home_of(ref, width):
        return ref.at[
            pl.ds(pl.multiple_of(group * RUN, RUN), RUN), pl.ds(pl.multiple_of(head * width, width), width)
        ]

    def owner_of(slot):
        peer = lax.rem(me + PEERS - slot, PEERS)
        return device_of(peer // KV_HEADS, lax.rem(peer, KV_HEADS), plane)

    def rows_of(n, slot, chunk):
        halves = []
        for which in range(2):
            block = target_of(target_ref, group, lax.rem(me + PEERS - slot, PEERS), chunk, which)
            halves.append(parts[n][block])
        rows = jnp.concatenate(halves, axis=0)
        return rows * SCORE_SCALE if n == 0 else rows

    def turn(tile, carry):
        rows = jnp.transpose(dq_turned[tile]) * SCORE_SCALE
        dq_tiles[pl.ds(tile * TILE_PARTS, TILE_PARTS)] = rows.reshape(TILE_PARTS, BLOCK_ROWS, HEAD_DIM)
        return carry

    def put_wide(slot):
        halves = []
        for which in range(2):
            first = rank_ref[0, 2 * slot + which] * SHARE
            halves.append(jnp.concatenate([dq_tiles[first + h] for h in range(SHARE)], axis=1))
        dq_ref[slot] = jnp.concatenate(halves, axis=0).astype(BF16)

    def send_wide(slot, carry):
        put_wide(slot)
        remote(dq_ref.at[slot], home_of(dq_out, UNIT), send_sem.at[2], recv_sem.at[2], owner_of(slot)).start()
        return carry

    def ring(way, step, n, part, src):
        target = lax.rem(plane + (1 if way == 0 else PLANES - 1), PLANES)
        return remote(
            src,
            inbox.at[way, n, step, pl.ds(part * PART, PART)],
            ring_send.at[way, n],
            ring_recv.at[way, step, n, part],
            device_of(group, head, target),
        )

    def chunk_at(way, step):
        distance = 4 - step
        return lax.rem(plane + (distance if way == 0 else PLANES - distance), PLANES)

    for step in range(4):
        for part in range(PARTS):
            piece = pl.ds(part * PART, PART)
            for n in range(2):
                for way in range(2):
                    chunk = chunk_at(way, step)
                    if step == 0 and n != way:
                        continue
                    if step == 0 or (step == 1 and n != way):

                        def fill(slot, carry):
                            outbox[way, n, slot] = rows_of(n, slot, chunk).astype(BF16)
                            return carry

                        lax.fori_loop(part * PART, (part + 1) * PART, fill, 0, unroll=4)
                        ring(way, step, n, part, outbox.at[way, n, piece]).start()
                    else:
                        held = inbox.at[way, n, step - 1, piece]
                        ring(way, step - 1, n, part, held).wait_recv()

                        def add(slot, carry):
                            sum_so_far = inbox[way, n, step - 1, slot].astype(F32)
                            inbox[way, n, step - 1, slot] = (sum_so_far + rows_of(n, slot, chunk)).astype(BF16)
                            return carry

                        lax.fori_loop(part * PART, (part + 1) * PART, add, 0, unroll=4)
                        ring(way, step, n, part, held).start()
                if step > 0:
                    wide_after = min(wide_next + 2, PEERS)
                    lax.fori_loop(wide_next, wide_after, send_wide, 0)
                    wide_next = wide_after
        if step == 0:
            lax.fori_loop(0, TILES, turn, 0)
            put_wide(0)
            own_wide = pltpu.make_async_copy(dq_ref.at[0], home_of(dq_out, UNIT), own_sem.at[2])
            own_wide.start()
            lax.fori_loop(1, 4, send_wide, 0)
            wide_next = 4
    own = [pltpu.make_async_copy(total.at[n, 0], home_of(outs[n], HEAD_DIM), own_sem.at[n]) for n in range(2)]
    for part in range(PARTS):
        piece = pl.ds(part * PART, PART)
        for n in range(2):
            for way in range(2):
                ring(way, 3, n, part, inbox.at[way, n, 3, piece]).wait_recv()

            def sum_up(slot, carry):
                arrived = inbox[0, n, 3, slot].astype(F32) + inbox[1, n, 3, slot].astype(F32)
                total[n, slot] = (rows_of(n, slot, plane) + arrived).astype(BF16)
                return carry

            lax.fori_loop(part * PART, (part + 1) * PART, sum_up, 0, unroll=4)

            def send_narrow(slot, carry):
                remote(
                    total.at[n, slot], home_of(outs[n], HEAD_DIM), send_sem.at[n], recv_sem.at[n], owner_of(slot)
                ).start()
                return carry

            if part == 0:
                own[n].start()
            lax.fori_loop(max(1, part * PART), (part + 1) * PART, send_narrow, 0)
    for way in range(2):
        for n in range(2):
            sent = inbox.at[way, n, pl.ds(0, 4 if n == way else 3)]
            remote(sent, sent, ring_send.at[way, n], ring_recv.at[way, 0, n, 0], here).wait_send()
    own_wide.wait()
    sent = dq_ref.at[pl.ds(0, PEERS - 1)]
    rest = remote(sent, sent, send_sem.at[2], recv_sem.at[2], here)
    rest.wait_send()
    rest.wait_recv()
    for n in range(2):
        sent = total.at[n, pl.ds(0, PEERS - 1)]
        rest = remote(sent, sent, send_sem.at[n], recv_sem.at[n], here)
        rest.wait_send()
        rest.wait_recv()
        own[n].wait()


def collect(ranks, block_target, dq, dk, dv):
    return pl.pallas_call(
        collect_kernel,
        name="collect",
        out_shape=(
            jax.ShapeDtypeStruct((GROUPS * RUN, KV_HEADS * UNIT), BF16),
            jax.ShapeDtypeStruct((GROUPS * RUN, KV_HEADS * HEAD_DIM), BF16),
            jax.ShapeDtypeStruct((GROUPS * RUN, KV_HEADS * HEAD_DIM), BF16),
        ),
        in_specs=[pl.BlockSpec(memory_space=pltpu.SMEM)] * 2 + [pl.BlockSpec(memory_space=pltpu.VMEM)] * 3,
        out_specs=[pl.BlockSpec(memory_space=pl.ANY)] * 3,
        scratch_shapes=[
            pltpu.VMEM((PEERS, RUN, UNIT), BF16),
            pltpu.VMEM((TILES * TILE_PARTS, BLOCK_ROWS, HEAD_DIM), F32),
            pltpu.VMEM((2, 2, PEERS, RUN, HEAD_DIM), BF16),
            pltpu.VMEM((2, 2, 4, PEERS, RUN, HEAD_DIM), BF16),
            pltpu.VMEM((2, PEERS, RUN, HEAD_DIM), BF16),
            pltpu.SemaphoreType.DMA((3,)),
            pltpu.SemaphoreType.DMA((3,)),
            pltpu.SemaphoreType.DMA((3,)),
            pltpu.SemaphoreType.DMA((2, 2)),
            pltpu.SemaphoreType.DMA((2, 4, 2, PARTS)),
        ],
        compiler_params=pltpu.CompilerParams(
            collective_id=1, has_side_effects=True, vmem_limit_bytes=24 * 1024 * 1024
        ),
    )(ranks, block_target, dq, dk, dv)


def deliver_kernel(*refs):
    copies = [pltpu.make_async_copy(refs[n], refs[3 + n], refs[6].at[n]) for n in range(3)]
    for copy in copies:
        copy.start()
    for copy in copies:
        copy.wait()


def deliver(*grads):
    return pl.pallas_call(
        deliver_kernel,
        name="deliver",
        out_shape=tuple(jax.ShapeDtypeStruct(grad.shape, grad.dtype) for grad in grads),
        in_specs=[pl.BlockSpec(memory_space=pl.ANY)] * 3,
        out_specs=[pl.BlockSpec(memory_space=pl.ANY)] * 3,
        scratch_shapes=[pltpu.SemaphoreType.DMA((3,))],
        compiler_params=pltpu.CompilerParams(vmem_limit_bytes=1024 * 1024),
    )(*grads)


def on_device(query_rows, key_rows, value_rows, output_grad, block_target, doc_lengths):
    queries, grads, keys, values, keys_turned, targets, lengths, ranks = scatter(
        query_rows, output_grad, key_rows, value_rows, block_target.transpose(0, 2, 1), doc_lengths
    )
    dq, dk, dv = attention(lengths, ranks, targets, queries, grads, keys, values, keys_turned)
    blocks = (GROUP_BLOCKS, BLOCK_ROWS, HEAD_DIM)
    return deliver(*collect(ranks, targets, dq, dk.reshape(blocks), dv.reshape(blocks)))


def solution(mesh):
    in_specs = (
        P(("grp", "ctx"), None),
        P(("grp", "ctx"), None),
        P(("grp", "ctx"), None),
        P(("grp", "ctx"), None),
        P(),
        P("grp", None),
    )
    out_specs = (P(("grp", "ctx"), None), P(("grp", "ctx"), None), P(("grp", "ctx"), None))
    return jax.shard_map(
        on_device, mesh=mesh, in_specs=in_specs, out_specs=out_specs, check_vma=False
    )
```

```python
import jax
import jax.numpy as jnp
from jax import lax
from jax.experimental import pallas as pl
from jax.experimental.pallas import tpu as pltpu
from jax.sharding import PartitionSpec as P

KV_HEADS = 4
HEAD_DIM = 128
SHARE = 8
BLOCK_ROWS = 8
GROUPS = 8
PLANES = 8
PEERS = 32
RUN = 16
UNIT = SHARE * HEAD_DIM
GROUP_BLOCKS = 512
GROUP_TOKENS = 4096
PLANE_BLOCKS = 64
DOCS = 16
TILE_BLOCKS = 4
TILE_ROWS = TILE_BLOCKS * SHARE * BLOCK_ROWS
TILE_PARTS = TILE_ROWS // BLOCK_ROWS
TILES = PLANE_BLOCKS // TILE_BLOCKS
CHUNK = 128
CHUNKS = GROUP_TOKENS // CHUNK
CHUNK_BLOCKS = CHUNK // BLOCK_ROWS
FIXED_MAX = 7
TOGETHER = 2
UNROLL_PREP = 2
SCORE_SCALE = HEAD_DIM**-0.5
EXP2_SCALE = SCORE_SCALE * 1.4426950408889634
PARTS = 4
PART = PEERS // PARTS
WIDE_EARLY = 4
WIDE_EACH = 2
MESH = pl.DeviceIdType.MESH
F32 = jnp.float32
BF16 = jnp.bfloat16


def place():
    group = lax.axis_index("grp")
    ctx = lax.axis_index("ctx")
    y_hi = ctx // 16
    plane = (ctx // 2) % PLANES
    core = ctx % 2
    head = y_hi * 2 + core
    return group, head, plane


def device_of(group, head, plane):
    return {"grp": group, "ctx": (head // 2) * 16 + plane * 2 + head % 2}


def half_of(pair, which):
    wide = pair.astype(F32)
    return jnp.where(which == 0, wide[:BLOCK_ROWS], wide[BLOCK_ROWS:])


def target_of(target_ref, group, source, from_plane, which):
    ctx = ((source >> 1) & 1) * 16 + (source & 1) + from_plane * 2
    return target_ref[source >> 2, 2 * group + which, ctx] & (GROUP_BLOCKS - 1)


def greet(group, head, plane):
    barrier = pltpu.get_barrier_semaphore()
    me = group * KV_HEADS + head

    def one(step, carry):
        peer = lax.rem(me + step, PEERS)
        pl.semaphore_signal(
            barrier,
            inc=1,
            device_id=device_of(peer // KV_HEADS, lax.rem(peer, KV_HEADS), plane),
            device_id_type=MESH,
        )
        return carry

    lax.fori_loop(1, PEERS, one, 0)
    for by in (1, PLANES - 1):
        pl.semaphore_signal(
            barrier,
            inc=1,
            device_id=device_of(group, head, lax.rem(plane + by, PLANES)),
            device_id_type=MESH,
        )
    pl.semaphore_wait(barrier, PEERS - 1 + 2)


def remote(src, dst, send, recv, device):
    return pltpu.make_async_remote_copy(
        src_ref=src, dst_ref=dst, send_sem=send, recv_sem=recv, device_id=device, device_id_type=MESH
    )


def scatter_kernel(
    q_ref,
    g_ref,
    k_ref,
    v_ref,
    target_ref,
    length_ref,
    q_out,
    g_out,
    k_pack,
    v_pack,
    k_turned,
    target_out,
    length_out,
    ranks_out,
    k_out,
    v_out,
    table,
    packed_from,
    send_sem,
    narrow_recv,
    wide_recv,
    own_sem,
    ring_send,
    ring_recv,
):
    group, head, plane = place()
    me = group * KV_HEADS + head
    greet(group, head, plane)
    here = device_of(group, head, plane)
    narrow = ((k_ref, k_out), (v_ref, v_out))
    wide = ((q_ref, q_out), (g_ref, g_out))

    def run_of(ref, to_group, to_head, width):
        return ref.at[
            pl.ds(pl.multiple_of(to_group * RUN, RUN), RUN),
            pl.ds(pl.multiple_of(to_head * width, width), width),
        ]

    def send_narrow(step, carry):
        peer = lax.rem(me + step, PEERS)
        to_group, to_head = peer // KV_HEADS, lax.rem(peer, KV_HEADS)
        for n, (src, dst) in enumerate(narrow):
            remote(
                run_of(src, to_group, to_head, HEAD_DIM),
                dst.at[plane, step],
                send_sem.at[n],
                narrow_recv.at[n, step // PART],
                device_of(to_group, to_head, plane),
            ).start()
        return carry

    def send_wide(step, carry):
        peer = lax.rem(me + step, PEERS)
        to_group, to_head = peer // KV_HEADS, lax.rem(peer, KV_HEADS)
        for n, (src, dst) in enumerate(wide):
            remote(
                run_of(src, to_group, to_head, UNIT),
                dst.at[step],
                send_sem.at[2 + n],
                wide_recv.at[n],
                device_of(to_group, to_head, plane),
            ).start()
        return carry

    own = [
        pltpu.make_async_copy(run_of(src, group, head, HEAD_DIM), dst.at[plane, 0], own_sem.at[n])
        for n, (src, dst) in enumerate(narrow)
    ] + [
        pltpu.make_async_copy(run_of(src, group, head, UNIT), dst.at[0], own_sem.at[2 + n])
        for n, (src, dst) in enumerate(wide)
    ]
    own += [
        pltpu.make_async_copy(target_ref, target_out, own_sem.at[4]),
        pltpu.make_async_copy(length_ref, length_out, own_sem.at[5]),
    ]
    own[0].start()
    own[1].start()
    lax.fori_loop(1, PEERS, send_narrow, 0)
    for copy in own[2:]:
        copy.start()

    def ring(way, step, n, part):
        chunk = lax.rem(plane + (PLANES - step if way == 0 else step), PLANES)
        target = lax.rem(plane + (1 if way == 0 else PLANES - 1), PLANES)
        piece = narrow[n][1].at[chunk, pl.ds(part * PART, PART)]
        return remote(
            piece,
            piece,
            ring_send.at[way, n],
            ring_recv.at[way, step, n, part],
            device_of(group, head, target),
        )

    def make_tables():
        own[4].wait()
        own[5].wait()
        lane = lax.broadcasted_iota(jnp.int32, (8, 128), 1)
        place_of = lax.broadcasted_iota(jnp.int32, (8, 128), 0) * 128 + lane

        def invert(source, inverse):
            slot = (me - source) & (PEERS - 1)
            for from_plane in range(PLANES):
                for which in range(2):
                    block = target_of(target_out, group, source, from_plane, which)
                    inverse = jnp.where(place_of == block, 2 * (from_plane * PEERS + slot) + which, inverse)
            return inverse

        table[0] = lax.fori_loop(0, PEERS, invert, jnp.zeros((8, 128), jnp.int32))

        def mine(step):
            return target_of(target_out, group, (me - (step >> 1)) & (PEERS - 1), plane, step & 1)

        blocks = lax.fori_loop(
            0,
            PLANE_BLOCKS,
            lambda step, blocks: jnp.where(lane == step, mine(step), blocks),
            jnp.full((8, 128), GROUP_BLOCKS, jnp.int32),
            unroll=8,
        )
        table[1] = lax.fori_loop(
            0,
            PLANE_BLOCKS,
            lambda step, rank: rank + jnp.where(blocks > mine(step), 1, 0),
            jnp.zeros((8, 128), jnp.int32),
            unroll=8,
        )
        for n, dst in enumerate((packed_from, ranks_out)):
            copy = pltpu.make_async_copy(table.at[n], dst, own_sem.at[6 + n])
            copy.start()
            copy.wait()

    lax.fori_loop(1, WIDE_EARLY, send_wide, 0)
    wide_next = WIDE_EARLY
    for step in range(4):
        for part in range(PARTS):
            for n in range(2):
                if step == 0:
                    if part == 0:
                        own[n].wait()
                    landed = narrow[n][1].at[plane, pl.ds(part * PART, PART - (part == 0))]
                    remote(landed, landed, send_sem.at[n], narrow_recv.at[n, part], here).wait_recv()
                for way in range(2):
                    if step == 3 and n != way:
                        continue
                    if step > 0:
                        ring(way, step - 1, n, part).wait_recv()
                    ring(way, step, n, part).start()
                wide_after = min(wide_next + WIDE_EACH, PEERS)
                lax.fori_loop(wide_next, wide_after, send_wide, 0)
                wide_next = wide_after
        if step == 1:
            make_tables()
    for part in range(PARTS):
        for way in range(2):
            ring(way, 2, 1 - way, part).wait_recv()
    for part in range(PARTS):
        for way in range(2):
            ring(way, 3, way, part).wait_recv()
    for way in range(2):
        for n in range(2):
            sent = narrow[n][1].at[pl.ds(0, 4 if n == way else 3)]
            remote(sent, sent, ring_send.at[way, n], ring_recv.at[way, 0, n, 0], here).wait_send()

    def pack(chunk, carry):
        first = chunk * CHUNK_BLOCKS
        rows = pl.ds(pl.multiple_of(chunk * CHUNK, CHUNK), CHUNK)
        held = [packed_from[(first + n) >> 7, (first + n) & 127] for n in range(CHUNK_BLOCKS)]
        keys = jnp.concatenate([half_of(k_out[h >> 6, (h >> 1) & (PEERS - 1)], h & 1) for h in held], axis=0)
        k_pack[rows, :] = keys.astype(BF16)
        k_turned[chunk] = jnp.transpose(keys).astype(BF16)
        values = jnp.concatenate([half_of(v_out[h >> 6, (h >> 1) & (PEERS - 1)], h & 1) for h in held], axis=0)
        v_pack[rows, :] = values.astype(BF16)
        return carry

    lax.fori_loop(0, CHUNKS, pack, 0)
    for n in range(2):
        sent = narrow[n][1].at[0, pl.ds(0, PEERS - 1)]
        remote(sent, sent, send_sem.at[n], narrow_recv.at[n, 0], here).wait_send()
        own[2 + n].wait()
        landed = wide[n][1].at[pl.ds(0, PEERS - 1)]
        rest = remote(landed, landed, send_sem.at[2 + n], wide_recv.at[n], here)
        rest.wait_recv()
        rest.wait_send()


def scatter(query_rows, output_grad, key_rows, value_rows, block_target, doc_lengths):
    wide = jax.ShapeDtypeStruct((PEERS, RUN, UNIT), BF16)
    narrow = pltpu.VMEM((PLANES, PEERS, RUN, HEAD_DIM), BF16)
    packed = jax.ShapeDtypeStruct((GROUP_TOKENS, HEAD_DIM), BF16)
    return pl.pallas_call(
        scatter_kernel,
        name="scatter",
        out_shape=(
            wide,
            wide,
            packed,
            packed,
            jax.ShapeDtypeStruct((CHUNKS, HEAD_DIM, CHUNK), BF16),
            jax.ShapeDtypeStruct(block_target.shape, jnp.int32),
            jax.ShapeDtypeStruct(doc_lengths.shape, jnp.int32),
            jax.ShapeDtypeStruct((8, 128), jnp.int32),
        ),
        in_specs=[pl.BlockSpec(memory_space=pltpu.HBM)] * 6,
        out_specs=[pl.BlockSpec(memory_space=pl.ANY)] * 2
        + [pl.BlockSpec(memory_space=pltpu.VMEM)] * 3
        + [pl.BlockSpec(memory_space=pltpu.SMEM)] * 3,
        scratch_shapes=[
            narrow,
            narrow,
            pltpu.VMEM((2, 8, 128), jnp.int32),
            pltpu.SMEM((8, 128), jnp.int32),
            pltpu.SemaphoreType.DMA((4,)),
            pltpu.SemaphoreType.DMA((2, PARTS)),
            pltpu.SemaphoreType.DMA((2,)),
            pltpu.SemaphoreType.DMA((8,)),
            pltpu.SemaphoreType.DMA((2, 2)),
            pltpu.SemaphoreType.DMA((2, 4, 2, PARTS)),
        ],
        compiler_params=pltpu.CompilerParams(
            collective_id=0, has_side_effects=True, vmem_limit_bytes=10 * 1024 * 1024
        ),
    )(
        *(
            pltpu.with_memory_space_constraint(rows, pltpu.HBM)
            for rows in (query_rows, output_grad, key_rows, value_rows, block_target, doc_lengths)
        )
    )


def attention_kernel(
    length_ref,
    rank_ref,
    target_ref,
    q_ref,
    g_ref,
    k_pack,
    v_pack,
    k_turned,
    dq_turned,
    dk_acc,
    dv_acc,
    query_order,
    query_block,
    doc_ends,
    q_tiles,
    g_tiles,
    bounds,
    spans,
    exps,
    probs,
    maxes,
):
    group, head, plane = place()
    me = group * KV_HEADS + head

    def sort(step, carry):
        rank = rank_ref[0, step]
        query_order[rank] = step
        query_block[rank] = target_of(target_ref, group, (me - (step >> 1)) & (PEERS - 1), plane, step & 1)
        return carry

    lax.fori_loop(0, PLANE_BLOCKS, sort, 0, unroll=8)

    end = jnp.int32(0)
    for n in range(DOCS):
        end = end + length_ref[0, n]
        doc_ends[n] = end

    def clear(step, carry):
        rows = pl.ds(pl.multiple_of(step * CHUNK, CHUNK), CHUNK)
        dk_acc[rows, :] = jnp.zeros((CHUNK, HEAD_DIM), F32)
        dv_acc[rows, :] = jnp.zeros((CHUNK, HEAD_DIM), F32)
        return carry

    lax.fori_loop(0, CHUNKS, clear, 0, unroll=2)

    lane = lax.broadcasted_iota(jnp.int32, (1, TILE_ROWS), 1)
    owner = lane // (SHARE * BLOCK_ROWS)

    def prepare(tile, carry):
        slots = [query_order[tile * TILE_BLOCKS + n] for n in range(TILE_BLOCKS)]
        blocks = [query_block[tile * TILE_BLOCKS + n] for n in range(TILE_BLOCKS)]
        for src, dst in ((q_ref, q_tiles), (g_ref, g_tiles)):
            parts = []
            for slot in slots:
                rows = half_of(src[slot >> 1], slot & 1)
                parts += [rows[:, h * HEAD_DIM : (h + 1) * HEAD_DIM] for h in range(SHARE)]
            dst[tile] = jnp.concatenate(parts, axis=0).astype(BF16)
        last = jnp.full((1, TILE_ROWS), blocks[0], jnp.int32)
        for n in range(1, TILE_BLOCKS):
            last = jnp.where(owner == n, blocks[n], last)
        last = last * BLOCK_ROWS + (lane & (BLOCK_ROWS - 1))
        start = jnp.zeros((1, TILE_ROWS), jnp.int32)
        tile_start = jnp.int32(0)
        for n in range(DOCS):
            end = doc_ends[n]
            start = jnp.where(end <= last, end, start)
            tile_start = jnp.where(end <= blocks[0] * BLOCK_ROWS, end, tile_start)
        bounds[tile, 0:1] = start
        bounds[tile, 1:2] = last
        first_chunk = tile_start // CHUNK
        spans[2 * tile] = first_chunk
        spans[2 * tile + 1] = (blocks[-1] * BLOCK_ROWS + BLOCK_ROWS - 1) // CHUNK - first_chunk + 1
        return carry

    lax.fori_loop(0, TILES, prepare, 0, unroll=UNROLL_PREP)

    key_iota = lax.broadcasted_iota(jnp.int32, (CHUNK, TILE_ROWS), 0)
    no_sum = jnp.zeros((8, TILE_ROWS), F32)

    def fold(array, op):
        return op(array.reshape(CHUNK // 8, 8, TILE_ROWS), axis=0)

    def rows_of(chunk):
        return pl.ds(pl.multiple_of(chunk * CHUNK, CHUNK), CHUNK)

    def against(rows_ref, chunk, tile_rows):
        return lax.dot_general(
            rows_ref[rows_of(chunk), :], tile_rows, (((1,), (1,)), ((), ())), preferred_element_type=F32
        )

    def masked(scores, chunk, start, last):
        position = key_iota + chunk * CHUNK
        return jnp.where((position >= start) & (position <= last), scores, -1e30)

    def put_keys(chunk, weights, score_grad, q_low, g_low):
        rows = rows_of(chunk)
        dv_acc[rows, :] += jnp.dot(weights.astype(BF16), g_low, preferred_element_type=F32)
        dk_acc[rows, :] += jnp.dot(score_grad, q_low, preferred_element_type=F32)
        return jnp.dot(k_turned[chunk], score_grad, preferred_element_type=F32)

    def query_tiles(step, carry):
        tiles = [step * TOGETHER + n for n in range(TOGETHER)]
        firsts = [spans[2 * tile] for tile in tiles]
        counts = [spans[2 * tile + 1] for tile in tiles]
        most = counts[0]
        for count in counts[1:]:
            most = jnp.maximum(most, count)

        def fixed(chunks):
            begins = [jnp.minimum(first, CHUNKS - chunks) for first in firsts]
            ways = range(TOGETHER)
            q_low = [q_tiles[tile] for tile in tiles]
            g_low = [g_tiles[tile] for tile in tiles]
            start = [bounds[tile, 0:1] for tile in tiles]
            last = [bounds[tile, 1:2] for tile in tiles]
            top = [jnp.full((8, TILE_ROWS), -1e30, F32)] * TOGETHER
            for n in range(chunks):
                for w in ways:
                    chunk = begins[w] + n
                    scores = masked(against(k_pack, chunk, q_low[w]), chunk, start[w], last[w])
                    exps[w * FIXED_MAX + n] = scores
                    top[w] = jnp.maximum(top[w], fold(scores, jnp.max))
            top = [jnp.max(t, axis=0, keepdims=True) for t in top]
            total, weighted = [no_sum] * TOGETHER, [no_sum] * TOGETHER
            for n in range(chunks):
                for w in ways:
                    prob_grad = against(v_pack, begins[w] + n, g_low[w])
                    weights = jnp.exp2((exps[w * FIXED_MAX + n] - top[w]) * EXP2_SCALE)
                    total[w] += fold(weights, jnp.sum)
                    weighted[w] += fold(weights * prob_grad, jnp.sum)
                    exps[w * FIXED_MAX + n] = weights
                    probs[w * FIXED_MAX + n] = prob_grad
            factor = [1.0 / jnp.sum(t, axis=0, keepdims=True) for t in total]
            delta = [jnp.sum(t, axis=0, keepdims=True) * f for t, f in zip(weighted, factor)]
            dq = [jnp.zeros((HEAD_DIM, TILE_ROWS), F32)] * TOGETHER
            for n in range(chunks):
                for w in ways:
                    weights = exps[w * FIXED_MAX + n] * factor[w]
                    score_grad = (weights * (probs[w * FIXED_MAX + n] - delta[w])).astype(BF16)
                    dq[w] += put_keys(begins[w] + n, weights, score_grad, q_low[w], g_low[w])
            for w in ways:
                dq_turned[tiles[w]] = dq[w]

        for chunks in range(1, FIXED_MAX + 1):

            @pl.when(most == chunks)
            def _():
                fixed(chunks)

        @pl.when(most > FIXED_MAX)
        def _():
            for tile, first, count in zip(tiles, firsts, counts):
                any_length(tile, first, count)

        return carry

    def any_length(tile, first, count):
        q_low, g_low = q_tiles[tile], g_tiles[tile]
        start, last = bounds[tile, 0:1], bounds[tile, 1:2]

        def totals(slot, state):
            top, total, weighted = state
            chunk = first + slot
            scores = masked(against(k_pack, chunk, q_low), chunk, start, last)
            prob_grad = against(v_pack, chunk, g_low)
            new_top = jnp.maximum(top, jnp.max(scores, axis=0, keepdims=True))
            weights = jnp.exp2((scores - new_top) * EXP2_SCALE)
            fade = jnp.exp2((top - new_top) * EXP2_SCALE)
            total = total * fade + jnp.sum(weights, axis=0, keepdims=True)
            weighted = weighted * fade + jnp.sum(weights * prob_grad, axis=0, keepdims=True)
            exps[slot] = weights
            probs[slot] = prob_grad
            maxes[slot] = jnp.broadcast_to(new_top, (8, TILE_ROWS))
            return new_top, total, weighted

        top, total, weighted = lax.fori_loop(
            0, count, totals, (jnp.full((1, TILE_ROWS), -1e20, F32), no_sum[:1], no_sum[:1])
        )
        scale_row = 1.0 / total
        delta = weighted * scale_row

        def gradients(slot, dq):
            factor = jnp.exp2((maxes[slot][:1] - top) * EXP2_SCALE) * scale_row
            weights = exps[slot] * factor
            score_grad = (weights * (probs[slot] - delta)).astype(BF16)
            return dq + put_keys(first + slot, weights, score_grad, q_low, g_low)

        dq_turned[tile] = lax.fori_loop(0, count, gradients, jnp.zeros((HEAD_DIM, TILE_ROWS), F32))

    lax.fori_loop(0, TILES // TOGETHER, query_tiles, 0)


def attention(doc_lengths, ranks, block_target, queries, grads, keys, values, keys_turned):
    acc = jax.ShapeDtypeStruct((GROUP_TOKENS, HEAD_DIM), F32)
    return pl.pallas_call(
        attention_kernel,
        name="attention",
        out_shape=(jax.ShapeDtypeStruct((TILES, HEAD_DIM, TILE_ROWS), F32), acc, acc),
        in_specs=[pl.BlockSpec(memory_space=pltpu.SMEM)] * 3 + [pl.BlockSpec(memory_space=pltpu.VMEM)] * 5,
        out_specs=[pl.BlockSpec(memory_space=pltpu.VMEM)] * 3,
        scratch_shapes=[
            pltpu.SMEM((PLANE_BLOCKS,), jnp.int32),
            pltpu.SMEM((PLANE_BLOCKS,), jnp.int32),
            pltpu.SMEM((DOCS,), jnp.int32),
            pltpu.VMEM((TILES, TILE_ROWS, HEAD_DIM), BF16),
            pltpu.VMEM((TILES, TILE_ROWS, HEAD_DIM), BF16),
            pltpu.VMEM((TILES, 8, TILE_ROWS), jnp.int32),
            pltpu.SMEM((2 * TILES,), jnp.int32),
            pltpu.VMEM((CHUNKS, CHUNK, TILE_ROWS), F32),
            pltpu.VMEM((CHUNKS, CHUNK, TILE_ROWS), F32),
            pltpu.VMEM((CHUNKS, 8, TILE_ROWS), F32),
        ],
        compiler_params=pltpu.CompilerParams(vmem_limit_bytes=30 * 1024 * 1024),
    )(doc_lengths, ranks, block_target, queries, grads, keys, values, keys_turned)


def collect_kernel(
    rank_ref,
    target_ref,
    dq_turned,
    dk_ref,
    dv_ref,
    dq_out,
    dk_out,
    dv_out,
    dq_ref,
    dq_tiles,
    outbox,
    inbox,
    total,
    send_sem,
    recv_sem,
    own_sem,
    ring_send,
    ring_recv,
):
    group, head, plane = place()
    me = group * KV_HEADS + head
    greet(group, head, plane)
    here = device_of(group, head, plane)
    parts = (dk_ref, dv_ref)
    outs = (dk_out, dv_out)

    def home_of(ref, width):
        return ref.at[
            pl.ds(pl.multiple_of(group * RUN, RUN), RUN), pl.ds(pl.multiple_of(head * width, width), width)
        ]

    def owner_of(slot):
        peer = lax.rem(me + PEERS - slot, PEERS)
        return device_of(peer // KV_HEADS, lax.rem(peer, KV_HEADS), plane)

    def rows_of(n, slot, chunk):
        halves = []
        for which in range(2):
            block = target_of(target_ref, group, (me - slot) & (PEERS - 1), chunk, which)
            halves.append(parts[n][block])
        rows = jnp.concatenate(halves, axis=0)
        return rows * SCORE_SCALE if n == 0 else rows

    def turn(tile, carry):
        rows = jnp.transpose(dq_turned[tile]) * SCORE_SCALE
        dq_tiles[pl.ds(tile * TILE_PARTS, TILE_PARTS)] = rows.reshape(TILE_PARTS, BLOCK_ROWS, HEAD_DIM)
        return carry

    def put_wide(slot):
        halves = []
        for which in range(2):
            first = rank_ref[0, 2 * slot + which] * SHARE
            halves.append(jnp.concatenate([dq_tiles[first + h] for h in range(SHARE)], axis=1))
        dq_ref[slot] = jnp.concatenate(halves, axis=0).astype(BF16)

    def send_wide(slot, carry):
        put_wide(slot)
        remote(dq_ref.at[slot], home_of(dq_out, UNIT), send_sem.at[2], recv_sem.at[2], owner_of(slot)).start()
        return carry

    def ring(way, step, n, part, src):
        target = lax.rem(plane + (1 if way == 0 else PLANES - 1), PLANES)
        return remote(
            src,
            inbox.at[way, n, step, pl.ds(part * PART, PART)],
            ring_send.at[way, n],
            ring_recv.at[way, step, n, part],
            device_of(group, head, target),
        )

    def chunk_at(way, step):
        distance = 4 - step
        return lax.rem(plane + (distance if way == 0 else PLANES - distance), PLANES)

    for step in range(4):
        for part in range(PARTS):
            piece = pl.ds(part * PART, PART)
            for n in range(2):
                for way in range(2):
                    chunk = chunk_at(way, step)
                    if step == 0 and n != way:
                        continue
                    if step == 0 or (step == 1 and n != way):

                        def fill(slot, carry):
                            outbox[way, n, slot] = rows_of(n, slot, chunk).astype(BF16)
                            return carry

                        lax.fori_loop(part * PART, (part + 1) * PART, fill, 0, unroll=4)
                        ring(way, step, n, part, outbox.at[way, n, piece]).start()
                    else:
                        held = inbox.at[way, n, step - 1, piece]
                        ring(way, step - 1, n, part, held).wait_recv()

                        def add(slot, carry):
                            sum_so_far = inbox[way, n, step - 1, slot].astype(F32)
                            inbox[way, n, step - 1, slot] = (sum_so_far + rows_of(n, slot, chunk)).astype(BF16)
                            return carry

                        lax.fori_loop(part * PART, (part + 1) * PART, add, 0, unroll=4)
                        ring(way, step, n, part, held).start()
                if step > 0:
                    wide_after = min(wide_next + 2, PEERS)
                    lax.fori_loop(wide_next, wide_after, send_wide, 0)
                    wide_next = wide_after
        if step == 0:
            lax.fori_loop(0, TILES, turn, 0)
            put_wide(0)
            own_wide = pltpu.make_async_copy(dq_ref.at[0], home_of(dq_out, UNIT), own_sem.at[2])
            own_wide.start()
            lax.fori_loop(1, 4, send_wide, 0)
            wide_next = 4
    own = [pltpu.make_async_copy(total.at[n, 0], home_of(outs[n], HEAD_DIM), own_sem.at[n]) for n in range(2)]
    for part in range(PARTS):
        piece = pl.ds(part * PART, PART)
        for n in range(2):
            for way in range(2):
                ring(way, 3, n, part, inbox.at[way, n, 3, piece]).wait_recv()

            def sum_up(slot, carry):
                arrived = inbox[0, n, 3, slot].astype(F32) + inbox[1, n, 3, slot].astype(F32)
                total[n, slot] = (rows_of(n, slot, plane) + arrived).astype(BF16)
                return carry

            lax.fori_loop(part * PART, (part + 1) * PART, sum_up, 0, unroll=4)

            def send_narrow(slot, carry):
                remote(
                    total.at[n, slot], home_of(outs[n], HEAD_DIM), send_sem.at[n], recv_sem.at[n], owner_of(slot)
                ).start()
                return carry

            if part == 0:
                own[n].start()
            lax.fori_loop(max(1, part * PART), (part + 1) * PART, send_narrow, 0)
    for way in range(2):
        for n in range(2):
            sent = inbox.at[way, n, pl.ds(0, 4 if n == way else 3)]
            remote(sent, sent, ring_send.at[way, n], ring_recv.at[way, 0, n, 0], here).wait_send()
    own_wide.wait()
    sent = dq_ref.at[pl.ds(0, PEERS - 1)]
    rest = remote(sent, sent, send_sem.at[2], recv_sem.at[2], here)
    rest.wait_send()
    rest.wait_recv()
    for n in range(2):
        sent = total.at[n, pl.ds(0, PEERS - 1)]
        rest = remote(sent, sent, send_sem.at[n], recv_sem.at[n], here)
        rest.wait_send()
        rest.wait_recv()
        own[n].wait()


def collect(ranks, block_target, dq, dk, dv):
    return pl.pallas_call(
        collect_kernel,
        name="collect",
        out_shape=(
            jax.ShapeDtypeStruct((GROUPS * RUN, KV_HEADS * UNIT), BF16),
            jax.ShapeDtypeStruct((GROUPS * RUN, KV_HEADS * HEAD_DIM), BF16),
            jax.ShapeDtypeStruct((GROUPS * RUN, KV_HEADS * HEAD_DIM), BF16),
        ),
        in_specs=[pl.BlockSpec(memory_space=pltpu.SMEM)] * 2 + [pl.BlockSpec(memory_space=pltpu.VMEM)] * 3,
        out_specs=[pl.BlockSpec(memory_space=pl.ANY)] * 3,
        scratch_shapes=[
            pltpu.VMEM((PEERS, RUN, UNIT), BF16),
            pltpu.VMEM((TILES * TILE_PARTS, BLOCK_ROWS, HEAD_DIM), F32),
            pltpu.VMEM((2, 2, PEERS, RUN, HEAD_DIM), BF16),
            pltpu.VMEM((2, 2, 4, PEERS, RUN, HEAD_DIM), BF16),
            pltpu.VMEM((2, PEERS, RUN, HEAD_DIM), BF16),
            pltpu.SemaphoreType.DMA((3,)),
            pltpu.SemaphoreType.DMA((3,)),
            pltpu.SemaphoreType.DMA((3,)),
            pltpu.SemaphoreType.DMA((2, 2)),
            pltpu.SemaphoreType.DMA((2, 4, 2, PARTS)),
        ],
        compiler_params=pltpu.CompilerParams(
            collective_id=1, has_side_effects=True, vmem_limit_bytes=24 * 1024 * 1024
        ),
    )(ranks, block_target, dq, dk, dv)


def deliver_kernel(*refs):
    copies = [pltpu.make_async_copy(refs[n], refs[3 + n], refs[6].at[n]) for n in range(3)]
    for copy in copies:
        copy.start()
    for copy in copies:
        copy.wait()


def deliver(*grads):
    return pl.pallas_call(
        deliver_kernel,
        name="deliver",
        out_shape=tuple(jax.ShapeDtypeStruct(grad.shape, grad.dtype) for grad in grads),
        in_specs=[pl.BlockSpec(memory_space=pl.ANY)] * 3,
        out_specs=[pl.BlockSpec(memory_space=pl.ANY)] * 3,
        scratch_shapes=[pltpu.SemaphoreType.DMA((3,))],
        compiler_params=pltpu.CompilerParams(vmem_limit_bytes=1024 * 1024),
    )(*grads)


def on_device(query_rows, key_rows, value_rows, output_grad, block_target, doc_lengths):
    queries, grads, keys, values, keys_turned, targets, lengths, ranks = scatter(
        query_rows, output_grad, key_rows, value_rows, block_target.transpose(0, 2, 1), doc_lengths
    )
    dq, dk, dv = attention(lengths, ranks, targets, queries, grads, keys, values, keys_turned)
    blocks = (GROUP_BLOCKS, BLOCK_ROWS, HEAD_DIM)
    return deliver(*collect(ranks, targets, dq, dk.reshape(blocks), dv.reshape(blocks)))


def solution(mesh):
    in_specs = (
        P(("grp", "ctx"), None),
        P(("grp", "ctx"), None),
        P(("grp", "ctx"), None),
        P(("grp", "ctx"), None),
        P(),
        P("grp", None),
    )
    out_specs = (P(("grp", "ctx"), None), P(("grp", "ctx"), None), P(("grp", "ctx"), None))
    return jax.shard_map(
        on_device, mesh=mesh, in_specs=in_specs, out_specs=out_specs, check_vma=False
    )
```

```python
import jax
import jax.numpy as jnp
from jax import lax
from jax.experimental import pallas as pl
from jax.experimental.pallas import tpu as pltpu
from jax.sharding import PartitionSpec as P

KV_HEADS = 4
HEAD_DIM = 128
SHARE = 8
BLOCK_ROWS = 8
GROUPS = 8
PLANES = 8
PEERS = 32
RUN = 16
UNIT = SHARE * HEAD_DIM
GROUP_BLOCKS = 512
GROUP_TOKENS = 4096
PLANE_BLOCKS = 64
DOCS = 16
TILE_BLOCKS = 4
TILE_ROWS = TILE_BLOCKS * SHARE * BLOCK_ROWS
TILE_PARTS = TILE_ROWS // BLOCK_ROWS
TILES = PLANE_BLOCKS // TILE_BLOCKS
CHUNK = 128
CHUNKS = GROUP_TOKENS // CHUNK
CHUNK_BLOCKS = CHUNK // BLOCK_ROWS
FIXED_MAX = 7
TOGETHER = 2
UNROLL_PREP = 4
SCORE_SCALE = HEAD_DIM**-0.5
EXP2_SCALE = SCORE_SCALE * 1.4426950408889634
PARTS = 4
PART = PEERS // PARTS
WIDE_EARLY = 4
WIDE_EACH = 2
MESH = pl.DeviceIdType.MESH
F32 = jnp.float32
BF16 = jnp.bfloat16


def place():
    group = lax.axis_index("grp")
    ctx = lax.axis_index("ctx")
    y_hi = ctx // 16
    plane = (ctx // 2) % PLANES
    core = ctx % 2
    head = y_hi * 2 + core
    return group, head, plane


def device_of(group, head, plane):
    return {"grp": group, "ctx": lax.div(head, 2) * 16 + plane * 2 + lax.rem(head, 2)}


def half_of(pair, which):
    wide = pair.astype(F32)
    return jnp.where(which == 0, wide[:BLOCK_ROWS], wide[BLOCK_ROWS:])


def target_of(target_ref, group, source, from_plane, which):
    ctx = ((source >> 1) & 1) * 16 + (source & 1) + from_plane * 2
    return target_ref[source >> 2, 2 * group + which, ctx] & (GROUP_BLOCKS - 1)


def greet(group, head, plane):
    barrier = pltpu.get_barrier_semaphore()
    me = group * KV_HEADS + head

    def one(step, carry):
        peer = lax.rem(me + step, PEERS)
        pl.semaphore_signal(
            barrier,
            inc=1,
            device_id=device_of(lax.div(peer, KV_HEADS), lax.rem(peer, KV_HEADS), plane),
            device_id_type=MESH,
        )
        return carry

    lax.fori_loop(1, PEERS, one, 0)
    for by in (1, PLANES - 1):
        pl.semaphore_signal(
            barrier,
            inc=1,
            device_id=device_of(group, head, lax.rem(plane + by, PLANES)),
            device_id_type=MESH,
        )
    pl.semaphore_wait(barrier, PEERS - 1 + 2)


def remote(src, dst, send, recv, device):
    return pltpu.make_async_remote_copy(
        src_ref=src, dst_ref=dst, send_sem=send, recv_sem=recv, device_id=device, device_id_type=MESH
    )


def scatter_kernel(
    q_ref,
    g_ref,
    k_ref,
    v_ref,
    target_ref,
    length_ref,
    q_out,
    g_out,
    k_pack,
    v_pack,
    k_turned,
    target_out,
    length_out,
    ranks_out,
    k_out,
    v_out,
    table,
    packed_from,
    send_sem,
    narrow_recv,
    wide_recv,
    own_sem,
    ring_send,
    ring_recv,
):
    group, head, plane = place()
    me = group * KV_HEADS + head
    greet(group, head, plane)
    here = device_of(group, head, plane)
    narrow = ((k_ref, k_out), (v_ref, v_out))
    wide = ((q_ref, q_out), (g_ref, g_out))

    def run_of(ref, to_group, to_head, width):
        return ref.at[
            pl.ds(pl.multiple_of(to_group * RUN, RUN), RUN),
            pl.ds(pl.multiple_of(to_head * width, width), width),
        ]

    def send_narrow(step, carry):
        peer = lax.rem(me + step, PEERS)
        to_group, to_head = lax.div(peer, KV_HEADS), lax.rem(peer, KV_HEADS)
        for n, (src, dst) in enumerate(narrow):
            remote(
                run_of(src, to_group, to_head, HEAD_DIM),
                dst.at[plane, step],
                send_sem.at[n],
                narrow_recv.at[n, lax.div(step, PART)],
                device_of(to_group, to_head, plane),
            ).start()
        return carry

    def send_wide(step, carry):
        peer = lax.rem(me + step, PEERS)
        to_group, to_head = lax.div(peer, KV_HEADS), lax.rem(peer, KV_HEADS)
        for n, (src, dst) in enumerate(wide):
            remote(
                run_of(src, to_group, to_head, UNIT),
                dst.at[step],
                send_sem.at[2 + n],
                wide_recv.at[n],
                device_of(to_group, to_head, plane),
            ).start()
        return carry

    own = [
        pltpu.make_async_copy(run_of(src, group, head, HEAD_DIM), dst.at[plane, 0], own_sem.at[n])
        for n, (src, dst) in enumerate(narrow)
    ] + [
        pltpu.make_async_copy(run_of(src, group, head, UNIT), dst.at[0], own_sem.at[2 + n])
        for n, (src, dst) in enumerate(wide)
    ]
    own += [
        pltpu.make_async_copy(target_ref, target_out, own_sem.at[4]),
        pltpu.make_async_copy(length_ref, length_out, own_sem.at[5]),
    ]
    own[0].start()
    own[1].start()
    lax.fori_loop(1, PEERS, send_narrow, 0)
    for copy in own[2:]:
        copy.start()

    def ring(way, step, n, part):
        chunk = lax.rem(plane + (PLANES - step if way == 0 else step), PLANES)
        target = lax.rem(plane + (1 if way == 0 else PLANES - 1), PLANES)
        piece = narrow[n][1].at[chunk, pl.ds(part * PART, PART)]
        return remote(
            piece,
            piece,
            ring_send.at[way, n],
            ring_recv.at[way, step, n, part],
            device_of(group, head, target),
        )

    def make_tables():
        own[4].wait()
        own[5].wait()
        lane = lax.broadcasted_iota(jnp.int32, (8, 128), 1)
        place_of = lax.broadcasted_iota(jnp.int32, (8, 128), 0) * 128 + lane

        def invert(source, inverse):
            slot = (me - source) & (PEERS - 1)
            for from_plane in range(PLANES):
                for which in range(2):
                    block = target_of(target_out, group, source, from_plane, which)
                    inverse = jnp.where(place_of == block, 2 * (from_plane * PEERS + slot) + which, inverse)
            return inverse

        table[0] = lax.fori_loop(0, PEERS, invert, jnp.zeros((8, 128), jnp.int32))

        def mine(step):
            return target_of(target_out, group, (me - (step >> 1)) & (PEERS - 1), plane, step & 1)

        blocks = lax.fori_loop(
            0,
            PLANE_BLOCKS,
            lambda step, blocks: jnp.where(lane == step, mine(step), blocks),
            jnp.full((8, 128), GROUP_BLOCKS, jnp.int32),
            unroll=8,
        )
        table[1] = lax.fori_loop(
            0,
            PLANE_BLOCKS,
            lambda step, rank: rank + jnp.where(blocks > mine(step), 1, 0),
            jnp.zeros((8, 128), jnp.int32),
            unroll=8,
        )
        for n, dst in enumerate((packed_from, ranks_out)):
            copy = pltpu.make_async_copy(table.at[n], dst, own_sem.at[6 + n])
            copy.start()
            copy.wait()

    lax.fori_loop(1, WIDE_EARLY, send_wide, 0)
    wide_next = WIDE_EARLY
    for step in range(4):
        for part in range(PARTS):
            for n in range(2):
                if step == 0:
                    if part == 0:
                        own[n].wait()
                    landed = narrow[n][1].at[plane, pl.ds(part * PART, PART - (part == 0))]
                    remote(landed, landed, send_sem.at[n], narrow_recv.at[n, part], here).wait_recv()
                for way in range(2):
                    if step == 3 and n != way:
                        continue
                    if step > 0:
                        ring(way, step - 1, n, part).wait_recv()
                    ring(way, step, n, part).start()
                wide_after = min(wide_next + WIDE_EACH, PEERS)
                lax.fori_loop(wide_next, wide_after, send_wide, 0)
                wide_next = wide_after
        if step == 1:
            make_tables()
    for part in range(PARTS):
        for way in range(2):
            ring(way, 2, 1 - way, part).wait_recv()
    for part in range(PARTS):
        for way in range(2):
            ring(way, 3, way, part).wait_recv()
    for way in range(2):
        for n in range(2):
            sent = narrow[n][1].at[pl.ds(0, 4 if n == way else 3)]
            remote(sent, sent, ring_send.at[way, n], ring_recv.at[way, 0, n, 0], here).wait_send()

    def pack(chunk, carry):
        first = chunk * CHUNK_BLOCKS
        rows = pl.ds(pl.multiple_of(chunk * CHUNK, CHUNK), CHUNK)
        held = [packed_from[(first + n) >> 7, (first + n) & 127] for n in range(CHUNK_BLOCKS)]
        keys = jnp.concatenate([half_of(k_out[h >> 6, (h >> 1) & (PEERS - 1)], h & 1) for h in held], axis=0)
        k_pack[rows, :] = keys.astype(BF16)
        k_turned[chunk] = jnp.transpose(keys).astype(BF16)
        values = jnp.concatenate([half_of(v_out[h >> 6, (h >> 1) & (PEERS - 1)], h & 1) for h in held], axis=0)
        v_pack[rows, :] = values.astype(BF16)
        return carry

    lax.fori_loop(0, CHUNKS, pack, 0, unroll=4)
    for n in range(2):
        sent = narrow[n][1].at[0, pl.ds(0, PEERS - 1)]
        remote(sent, sent, send_sem.at[n], narrow_recv.at[n, 0], here).wait_send()
        own[2 + n].wait()
        landed = wide[n][1].at[pl.ds(0, PEERS - 1)]
        rest = remote(landed, landed, send_sem.at[2 + n], wide_recv.at[n], here)
        rest.wait_recv()
        rest.wait_send()


def scatter(query_rows, output_grad, key_rows, value_rows, block_target, doc_lengths):
    wide = jax.ShapeDtypeStruct((PEERS, RUN, UNIT), BF16)
    narrow = pltpu.VMEM((PLANES, PEERS, RUN, HEAD_DIM), BF16)
    packed = jax.ShapeDtypeStruct((GROUP_TOKENS, HEAD_DIM), BF16)
    return pl.pallas_call(
        scatter_kernel,
        name="scatter",
        out_shape=(
            wide,
            wide,
            packed,
            packed,
            jax.ShapeDtypeStruct((CHUNKS, HEAD_DIM, CHUNK), BF16),
            jax.ShapeDtypeStruct(block_target.shape, jnp.int32),
            jax.ShapeDtypeStruct(doc_lengths.shape, jnp.int32),
            jax.ShapeDtypeStruct((8, 128), jnp.int32),
        ),
        in_specs=[pl.BlockSpec(memory_space=pltpu.HBM)] * 6,
        out_specs=[pl.BlockSpec(memory_space=pl.ANY)] * 2
        + [pl.BlockSpec(memory_space=pltpu.VMEM)] * 3
        + [pl.BlockSpec(memory_space=pltpu.SMEM)] * 3,
        scratch_shapes=[
            narrow,
            narrow,
            pltpu.VMEM((2, 8, 128), jnp.int32),
            pltpu.SMEM((8, 128), jnp.int32),
            pltpu.SemaphoreType.DMA((4,)),
            pltpu.SemaphoreType.DMA((2, PARTS)),
            pltpu.SemaphoreType.DMA((2,)),
            pltpu.SemaphoreType.DMA((8,)),
            pltpu.SemaphoreType.DMA((2, 2)),
            pltpu.SemaphoreType.DMA((2, 4, 2, PARTS)),
        ],
        compiler_params=pltpu.CompilerParams(
            collective_id=0, has_side_effects=True, vmem_limit_bytes=10 * 1024 * 1024
        ),
    )(
        *(
            pltpu.with_memory_space_constraint(rows, pltpu.HBM)
            for rows in (query_rows, output_grad, key_rows, value_rows, block_target, doc_lengths)
        )
    )


def attention_kernel(
    length_ref,
    rank_ref,
    target_ref,
    q_ref,
    g_ref,
    k_pack,
    v_pack,
    k_turned,
    dq_turned,
    dk_acc,
    dv_acc,
    query_order,
    query_block,
    doc_ends,
    q_tiles,
    g_tiles,
    bounds,
    spans,
    exps,
    probs,
    maxes,
):
    group, head, plane = place()
    me = group * KV_HEADS + head

    def sort(step, carry):
        rank = rank_ref[0, step]
        query_order[rank] = step
        query_block[rank] = target_of(target_ref, group, (me - (step >> 1)) & (PEERS - 1), plane, step & 1)
        return carry

    lax.fori_loop(0, PLANE_BLOCKS, sort, 0, unroll=8)

    end = jnp.int32(0)
    for n in range(DOCS):
        end = end + length_ref[0, n]
        doc_ends[n] = end

    def clear(step, carry):
        rows = pl.ds(pl.multiple_of(step * CHUNK, CHUNK), CHUNK)
        dk_acc[rows, :] = jnp.zeros((CHUNK, HEAD_DIM), F32)
        dv_acc[rows, :] = jnp.zeros((CHUNK, HEAD_DIM), F32)
        return carry

    lax.fori_loop(0, CHUNKS, clear, 0, unroll=2)

    lane = lax.broadcasted_iota(jnp.int32, (1, TILE_ROWS), 1)
    owner = lane // (SHARE * BLOCK_ROWS)

    def prepare(tile, carry):
        slots = [query_order[tile * TILE_BLOCKS + n] for n in range(TILE_BLOCKS)]
        blocks = [query_block[tile * TILE_BLOCKS + n] for n in range(TILE_BLOCKS)]
        for src, dst in ((q_ref, q_tiles), (g_ref, g_tiles)):
            parts = []
            for slot in slots:
                rows = half_of(src[slot >> 1], slot & 1)
                parts += [rows[:, h * HEAD_DIM : (h + 1) * HEAD_DIM] for h in range(SHARE)]
            dst[tile] = jnp.concatenate(parts, axis=0).astype(BF16)
        last = jnp.full((1, TILE_ROWS), blocks[0], jnp.int32)
        for n in range(1, TILE_BLOCKS):
            last = jnp.where(owner == n, blocks[n], last)
        last = last * BLOCK_ROWS + (lane & (BLOCK_ROWS - 1))
        start = jnp.zeros((1, TILE_ROWS), jnp.int32)
        tile_start = jnp.int32(0)
        for n in range(DOCS):
            end = doc_ends[n]
            start = jnp.where(end <= last, end, start)
            tile_start = jnp.where(end <= blocks[0] * BLOCK_ROWS, end, tile_start)
        bounds[tile, 0:1] = start
        bounds[tile, 1:2] = last
        first_chunk = tile_start // CHUNK
        spans[2 * tile] = first_chunk
        spans[2 * tile + 1] = (blocks[-1] * BLOCK_ROWS + BLOCK_ROWS - 1) // CHUNK - first_chunk + 1
        return carry

    lax.fori_loop(0, TILES, prepare, 0, unroll=UNROLL_PREP)

    key_iota = lax.broadcasted_iota(jnp.int32, (CHUNK, TILE_ROWS), 0)
    no_sum = jnp.zeros((8, TILE_ROWS), F32)

    def fold(array, op):
        return op(array.reshape(CHUNK // 8, 8, TILE_ROWS), axis=0)

    def rows_of(chunk):
        return pl.ds(pl.multiple_of(chunk * CHUNK, CHUNK), CHUNK)

    def against(rows_ref, chunk, tile_rows):
        return lax.dot_general(
            rows_ref[rows_of(chunk), :], tile_rows, (((1,), (1,)), ((), ())), preferred_element_type=F32
        )

    def masked(scores, chunk, start, last):
        position = key_iota + chunk * CHUNK
        return jnp.where((position >= start) & (position <= last), scores, -1e30)

    def put_keys(chunk, weights, score_grad, q_low, g_low):
        rows = rows_of(chunk)
        dv_acc[rows, :] += jnp.dot(weights.astype(BF16), g_low, preferred_element_type=F32)
        dk_acc[rows, :] += jnp.dot(score_grad, q_low, preferred_element_type=F32)
        return jnp.dot(k_turned[chunk], score_grad, preferred_element_type=F32)

    def query_tiles(step, carry):
        tiles = [step * TOGETHER + n for n in range(TOGETHER)]
        firsts = [spans[2 * tile] for tile in tiles]
        counts = [spans[2 * tile + 1] for tile in tiles]
        most = counts[0]
        for count in counts[1:]:
            most = jnp.maximum(most, count)

        def fixed(chunks):
            begins = [jnp.minimum(first, CHUNKS - chunks) for first in firsts]
            ways = range(TOGETHER)
            q_low = [q_tiles[tile] for tile in tiles]
            g_low = [g_tiles[tile] for tile in tiles]
            start = [bounds[tile, 0:1] for tile in tiles]
            last = [bounds[tile, 1:2] for tile in tiles]
            top = [jnp.full((8, TILE_ROWS), -1e30, F32)] * TOGETHER
            for n in range(chunks):
                for w in ways:
                    chunk = begins[w] + n
                    scores = masked(against(k_pack, chunk, q_low[w]), chunk, start[w], last[w])
                    exps[w * FIXED_MAX + n] = scores
                    top[w] = jnp.maximum(top[w], fold(scores, jnp.max))
            top = [jnp.max(t, axis=0, keepdims=True) for t in top]
            total, weighted = [no_sum] * TOGETHER, [no_sum] * TOGETHER
            for n in range(chunks):
                for w in ways:
                    prob_grad = against(v_pack, begins[w] + n, g_low[w])
                    weights = jnp.exp2((exps[w * FIXED_MAX + n] - top[w]) * EXP2_SCALE)
                    total[w] += fold(weights, jnp.sum)
                    weighted[w] += fold(weights * prob_grad, jnp.sum)
                    exps[w * FIXED_MAX + n] = weights
                    probs[w * FIXED_MAX + n] = prob_grad
            factor = [1.0 / jnp.sum(t, axis=0, keepdims=True) for t in total]
            delta = [jnp.sum(t, axis=0, keepdims=True) * f for t, f in zip(weighted, factor)]
            dq = [jnp.zeros((HEAD_DIM, TILE_ROWS), F32)] * TOGETHER
            for n in range(chunks):
                for w in ways:
                    weights = exps[w * FIXED_MAX + n] * factor[w]
                    score_grad = (weights * (probs[w * FIXED_MAX + n] - delta[w])).astype(BF16)
                    dq[w] += put_keys(begins[w] + n, weights, score_grad, q_low[w], g_low[w])
            for w in ways:
                dq_turned[tiles[w]] = dq[w]

        for chunks in range(1, FIXED_MAX + 1):

            @pl.when(most == chunks)
            def _():
                fixed(chunks)

        @pl.when(most > FIXED_MAX)
        def _():
            for tile, first, count in zip(tiles, firsts, counts):
                any_length(tile, first, count)

        return carry

    def any_length(tile, first, count):
        q_low, g_low = q_tiles[tile], g_tiles[tile]
        start, last = bounds[tile, 0:1], bounds[tile, 1:2]

        def totals(slot, state):
            top, total, weighted = state
            chunk = first + slot
            scores = masked(against(k_pack, chunk, q_low), chunk, start, last)
            prob_grad = against(v_pack, chunk, g_low)
            new_top = jnp.maximum(top, jnp.max(scores, axis=0, keepdims=True))
            weights = jnp.exp2((scores - new_top) * EXP2_SCALE)
            fade = jnp.exp2((top - new_top) * EXP2_SCALE)
            total = total * fade + jnp.sum(weights, axis=0, keepdims=True)
            weighted = weighted * fade + jnp.sum(weights * prob_grad, axis=0, keepdims=True)
            exps[slot] = weights
            probs[slot] = prob_grad
            maxes[slot] = jnp.broadcast_to(new_top, (8, TILE_ROWS))
            return new_top, total, weighted

        top, total, weighted = lax.fori_loop(
            0, count, totals, (jnp.full((1, TILE_ROWS), -1e20, F32), no_sum[:1], no_sum[:1])
        )
        scale_row = 1.0 / total
        delta = weighted * scale_row

        def gradients(slot, dq):
            factor = jnp.exp2((maxes[slot][:1] - top) * EXP2_SCALE) * scale_row
            weights = exps[slot] * factor
            score_grad = (weights * (probs[slot] - delta)).astype(BF16)
            return dq + put_keys(first + slot, weights, score_grad, q_low, g_low)

        dq_turned[tile] = lax.fori_loop(0, count, gradients, jnp.zeros((HEAD_DIM, TILE_ROWS), F32))

    lax.fori_loop(0, TILES // TOGETHER, query_tiles, 0)


def attention(doc_lengths, ranks, block_target, queries, grads, keys, values, keys_turned):
    acc = jax.ShapeDtypeStruct((GROUP_TOKENS, HEAD_DIM), F32)
    return pl.pallas_call(
        attention_kernel,
        name="attention",
        out_shape=(jax.ShapeDtypeStruct((TILES, HEAD_DIM, TILE_ROWS), F32), acc, acc),
        in_specs=[pl.BlockSpec(memory_space=pltpu.SMEM)] * 3 + [pl.BlockSpec(memory_space=pltpu.VMEM)] * 5,
        out_specs=[pl.BlockSpec(memory_space=pltpu.VMEM)] * 3,
        scratch_shapes=[
            pltpu.SMEM((PLANE_BLOCKS,), jnp.int32),
            pltpu.SMEM((PLANE_BLOCKS,), jnp.int32),
            pltpu.SMEM((DOCS,), jnp.int32),
            pltpu.VMEM((TILES, TILE_ROWS, HEAD_DIM), BF16),
            pltpu.VMEM((TILES, TILE_ROWS, HEAD_DIM), BF16),
            pltpu.VMEM((TILES, 8, TILE_ROWS), jnp.int32),
            pltpu.SMEM((2 * TILES,), jnp.int32),
            pltpu.VMEM((CHUNKS, CHUNK, TILE_ROWS), F32),
            pltpu.VMEM((CHUNKS, CHUNK, TILE_ROWS), F32),
            pltpu.VMEM((CHUNKS, 8, TILE_ROWS), F32),
        ],
        compiler_params=pltpu.CompilerParams(vmem_limit_bytes=30 * 1024 * 1024),
    )(doc_lengths, ranks, block_target, queries, grads, keys, values, keys_turned)


def collect_kernel(
    rank_ref,
    target_ref,
    dq_turned,
    dk_ref,
    dv_ref,
    dq_out,
    dk_out,
    dv_out,
    dq_ref,
    dq_tiles,
    outbox,
    inbox,
    total,
    send_sem,
    recv_sem,
    own_sem,
    ring_send,
    ring_recv,
):
    group, head, plane = place()
    me = group * KV_HEADS + head
    greet(group, head, plane)
    here = device_of(group, head, plane)
    parts = (dk_ref, dv_ref)
    outs = (dk_out, dv_out)

    def home_of(ref, width):
        return ref.at[
            pl.ds(pl.multiple_of(group * RUN, RUN), RUN), pl.ds(pl.multiple_of(head * width, width), width)
        ]

    def owner_of(slot):
        peer = lax.rem(me + PEERS - slot, PEERS)
        return device_of(lax.div(peer, KV_HEADS), lax.rem(peer, KV_HEADS), plane)

    def rows_of(n, slot, chunk):
        halves = []
        for which in range(2):
            block = target_of(target_ref, group, (me - slot) & (PEERS - 1), chunk, which)
            halves.append(parts[n][block])
        rows = jnp.concatenate(halves, axis=0)
        return rows * SCORE_SCALE if n == 0 else rows

    def turn(tile, carry):
        rows = jnp.transpose(dq_turned[tile]) * SCORE_SCALE
        dq_tiles[pl.ds(tile * TILE_PARTS, TILE_PARTS)] = rows.reshape(TILE_PARTS, BLOCK_ROWS, HEAD_DIM)
        return carry

    def put_wide(slot):
        halves = []
        for which in range(2):
            first = rank_ref[0, 2 * slot + which] * SHARE
            halves.append(jnp.concatenate([dq_tiles[first + h] for h in range(SHARE)], axis=1))
        dq_ref[slot] = jnp.concatenate(halves, axis=0).astype(BF16)

    def send_wide(slot, carry):
        put_wide(slot)
        remote(dq_ref.at[slot], home_of(dq_out, UNIT), send_sem.at[2], recv_sem.at[2], owner_of(slot)).start()
        return carry

    def ring(way, step, n, part, src):
        target = lax.rem(plane + (1 if way == 0 else PLANES - 1), PLANES)
        return remote(
            src,
            inbox.at[way, n, step, pl.ds(part * PART, PART)],
            ring_send.at[way, n],
            ring_recv.at[way, step, n, part],
            device_of(group, head, target),
        )

    def chunk_at(way, step):
        distance = 4 - step
        return lax.rem(plane + (distance if way == 0 else PLANES - distance), PLANES)

    for step in range(4):
        for part in range(PARTS):
            piece = pl.ds(part * PART, PART)
            for n in range(2):
                for way in range(2):
                    chunk = chunk_at(way, step)
                    if step == 0 and n != way:
                        continue
                    if step == 0 or (step == 1 and n != way):

                        def fill(slot, carry):
                            outbox[way, n, slot] = rows_of(n, slot, chunk).astype(BF16)
                            return carry

                        lax.fori_loop(part * PART, (part + 1) * PART, fill, 0, unroll=4)
                        ring(way, step, n, part, outbox.at[way, n, piece]).start()
                    else:
                        held = inbox.at[way, n, step - 1, piece]
                        ring(way, step - 1, n, part, held).wait_recv()

                        def add(slot, carry):
                            sum_so_far = inbox[way, n, step - 1, slot].astype(F32)
                            inbox[way, n, step - 1, slot] = (sum_so_far + rows_of(n, slot, chunk)).astype(BF16)
                            return carry

                        lax.fori_loop(part * PART, (part + 1) * PART, add, 0, unroll=8)
                        ring(way, step, n, part, held).start()
                if step > 0:
                    wide_after = min(wide_next + 2, PEERS)
                    lax.fori_loop(wide_next, wide_after, send_wide, 0)
                    wide_next = wide_after
        if step == 0:
            lax.fori_loop(0, TILES, turn, 0, unroll=4)
            put_wide(0)
            own_wide = pltpu.make_async_copy(dq_ref.at[0], home_of(dq_out, UNIT), own_sem.at[2])
            own_wide.start()
            lax.fori_loop(1, 4, send_wide, 0)
            wide_next = 4
    own = [pltpu.make_async_copy(total.at[n, 0], home_of(outs[n], HEAD_DIM), own_sem.at[n]) for n in range(2)]
    for part in range(PARTS):
        piece = pl.ds(part * PART, PART)
        for n in range(2):
            for way in range(2):
                ring(way, 3, n, part, inbox.at[way, n, 3, piece]).wait_recv()

            def sum_up(slot, carry):
                arrived = inbox[0, n, 3, slot].astype(F32) + inbox[1, n, 3, slot].astype(F32)
                total[n, slot] = (rows_of(n, slot, plane) + arrived).astype(BF16)
                return carry

            lax.fori_loop(part * PART, (part + 1) * PART, sum_up, 0, unroll=8)

            def send_narrow(slot, carry):
                remote(
                    total.at[n, slot], home_of(outs[n], HEAD_DIM), send_sem.at[n], recv_sem.at[n], owner_of(slot)
                ).start()
                return carry

            if part == 0:
                own[n].start()
            lax.fori_loop(max(1, part * PART), (part + 1) * PART, send_narrow, 0)
    for way in range(2):
        for n in range(2):
            sent = inbox.at[way, n, pl.ds(0, 4 if n == way else 3)]
            remote(sent, sent, ring_send.at[way, n], ring_recv.at[way, 0, n, 0], here).wait_send()
    own_wide.wait()
    sent = dq_ref.at[pl.ds(0, PEERS - 1)]
    rest = remote(sent, sent, send_sem.at[2], recv_sem.at[2], here)
    rest.wait_send()
    rest.wait_recv()
    for n in range(2):
        sent = total.at[n, pl.ds(0, PEERS - 1)]
        rest = remote(sent, sent, send_sem.at[n], recv_sem.at[n], here)
        rest.wait_send()
        rest.wait_recv()
        own[n].wait()


def collect(ranks, block_target, dq, dk, dv):
    return pl.pallas_call(
        collect_kernel,
        name="collect",
        out_shape=(
            jax.ShapeDtypeStruct((GROUPS * RUN, KV_HEADS * UNIT), BF16),
            jax.ShapeDtypeStruct((GROUPS * RUN, KV_HEADS * HEAD_DIM), BF16),
            jax.ShapeDtypeStruct((GROUPS * RUN, KV_HEADS * HEAD_DIM), BF16),
        ),
        in_specs=[pl.BlockSpec(memory_space=pltpu.SMEM)] * 2 + [pl.BlockSpec(memory_space=pltpu.VMEM)] * 3,
        out_specs=[pl.BlockSpec(memory_space=pl.ANY)] * 3,
        scratch_shapes=[
            pltpu.VMEM((PEERS, RUN, UNIT), BF16),
            pltpu.VMEM((TILES * TILE_PARTS, BLOCK_ROWS, HEAD_DIM), F32),
            pltpu.VMEM((2, 2, PEERS, RUN, HEAD_DIM), BF16),
            pltpu.VMEM((2, 2, 4, PEERS, RUN, HEAD_DIM), BF16),
            pltpu.VMEM((2, PEERS, RUN, HEAD_DIM), BF16),
            pltpu.SemaphoreType.DMA((3,)),
            pltpu.SemaphoreType.DMA((3,)),
            pltpu.SemaphoreType.DMA((3,)),
            pltpu.SemaphoreType.DMA((2, 2)),
            pltpu.SemaphoreType.DMA((2, 4, 2, PARTS)),
        ],
        compiler_params=pltpu.CompilerParams(
            collective_id=1, has_side_effects=True, vmem_limit_bytes=24 * 1024 * 1024
        ),
    )(ranks, block_target, dq, dk, dv)


def deliver_kernel(*refs):
    copies = [pltpu.make_async_copy(refs[n], refs[3 + n], refs[6].at[n]) for n in range(3)]
    for copy in copies:
        copy.start()
    for copy in copies:
        copy.wait()


def deliver(*grads):
    return pl.pallas_call(
        deliver_kernel,
        name="deliver",
        out_shape=tuple(jax.ShapeDtypeStruct(grad.shape, grad.dtype) for grad in grads),
        in_specs=[pl.BlockSpec(memory_space=pl.ANY)] * 3,
        out_specs=[pl.BlockSpec(memory_space=pl.ANY)] * 3,
        scratch_shapes=[pltpu.SemaphoreType.DMA((3,))],
        compiler_params=pltpu.CompilerParams(vmem_limit_bytes=1024 * 1024),
    )(*grads)


def on_device(query_rows, key_rows, value_rows, output_grad, block_target, doc_lengths):
    queries, grads, keys, values, keys_turned, targets, lengths, ranks = scatter(
        query_rows, output_grad, key_rows, value_rows, block_target.transpose(0, 2, 1), doc_lengths
    )
    dq, dk, dv = attention(lengths, ranks, targets, queries, grads, keys, values, keys_turned)
    blocks = (GROUP_BLOCKS, BLOCK_ROWS, HEAD_DIM)
    return deliver(*collect(ranks, targets, dq, dk.reshape(blocks), dv.reshape(blocks)))


def solution(mesh):
    in_specs = (
        P(("grp", "ctx"), None),
        P(("grp", "ctx"), None),
        P(("grp", "ctx"), None),
        P(("grp", "ctx"), None),
        P(),
        P("grp", None),
    )
    out_specs = (P(("grp", "ctx"), None), P(("grp", "ctx"), None), P(("grp", "ctx"), None))
    return jax.shard_map(
        on_device, mesh=mesh, in_specs=in_specs, out_specs=out_specs, check_vma=False
    )
```

```python
import jax
import jax.numpy as jnp
from jax import lax
from jax.experimental import pallas as pl
from jax.experimental.pallas import tpu as pltpu
from jax.sharding import PartitionSpec as P

KV_HEADS = 4
HEAD_DIM = 128
SHARE = 8
BLOCK_ROWS = 8
GROUPS = 8
PLANES = 8
PEERS = 32
RUN = 16
UNIT = SHARE * HEAD_DIM
GROUP_BLOCKS = 512
GROUP_TOKENS = 4096
PLANE_BLOCKS = 64
DOCS = 16
TILE_BLOCKS = 4
TILE_ROWS = TILE_BLOCKS * SHARE * BLOCK_ROWS
TILE_PARTS = TILE_ROWS // BLOCK_ROWS
TILES = PLANE_BLOCKS // TILE_BLOCKS
CHUNK = 128
CHUNKS = GROUP_TOKENS // CHUNK
CHUNK_BLOCKS = CHUNK // BLOCK_ROWS
FIXED_MAX = 7
TOGETHER = 2
UNROLL_PREP = 4
SCORE_SCALE = HEAD_DIM**-0.5
EXP2_SCALE = SCORE_SCALE * 1.4426950408889634
PARTS = 4
PART = PEERS // PARTS
WIDE_EARLY = 4
WIDE_EACH = 2
MESH = pl.DeviceIdType.MESH
F32 = jnp.float32
BF16 = jnp.bfloat16


def place():
    group = lax.axis_index("grp")
    ctx = lax.axis_index("ctx")
    y_hi = ctx // 16
    plane = (ctx // 2) % PLANES
    core = ctx % 2
    head = y_hi * 2 + core
    return group, head, plane


def device_of(group, head, plane):
    return {"grp": group, "ctx": lax.div(head, 2) * 16 + plane * 2 + lax.rem(head, 2)}


def half_of(pair, which):
    wide = pair.astype(F32)
    return jnp.where(which == 0, wide[:BLOCK_ROWS], wide[BLOCK_ROWS:])


def target_of(target_ref, group, source, from_plane, which):
    ctx = ((source >> 1) & 1) * 16 + (source & 1) + from_plane * 2
    return target_ref[source >> 2, 2 * group + which, ctx] & (GROUP_BLOCKS - 1)


def greet(group, head, plane, meanwhile=None):
    barrier = pltpu.get_barrier_semaphore()
    me = group * KV_HEADS + head

    def one(step, carry):
        peer = lax.rem(me + step, PEERS)
        pl.semaphore_signal(
            barrier,
            inc=1,
            device_id=device_of(lax.div(peer, KV_HEADS), lax.rem(peer, KV_HEADS), plane),
            device_id_type=MESH,
        )
        return carry

    lax.fori_loop(1, PEERS, one, 0)
    for by in (1, PLANES - 1):
        pl.semaphore_signal(
            barrier,
            inc=1,
            device_id=device_of(group, head, lax.rem(plane + by, PLANES)),
            device_id_type=MESH,
        )
    if meanwhile is not None:
        meanwhile()
    pl.semaphore_wait(barrier, PEERS - 1 + 2)


def remote(src, dst, send, recv, device):
    return pltpu.make_async_remote_copy(
        src_ref=src, dst_ref=dst, send_sem=send, recv_sem=recv, device_id=device, device_id_type=MESH
    )


def scatter_kernel(
    q_ref,
    g_ref,
    k_ref,
    v_ref,
    target_ref,
    length_ref,
    q_out,
    g_out,
    k_pack,
    v_pack,
    k_turned,
    target_out,
    length_out,
    ranks_out,
    k_out,
    v_out,
    table,
    packed_from,
    send_sem,
    narrow_recv,
    wide_recv,
    own_sem,
    ring_send,
    ring_recv,
):
    group, head, plane = place()
    me = group * KV_HEADS + head
    greet(group, head, plane)
    here = device_of(group, head, plane)
    narrow = ((k_ref, k_out), (v_ref, v_out))
    wide = ((q_ref, q_out), (g_ref, g_out))

    def run_of(ref, to_group, to_head, width):
        return ref.at[
            pl.ds(pl.multiple_of(to_group * RUN, RUN), RUN),
            pl.ds(pl.multiple_of(to_head * width, width), width),
        ]

    def send_narrow(step, carry):
        peer = lax.rem(me + step, PEERS)
        to_group, to_head = lax.div(peer, KV_HEADS), lax.rem(peer, KV_HEADS)
        for n, (src, dst) in enumerate(narrow):
            remote(
                run_of(src, to_group, to_head, HEAD_DIM),
                dst.at[plane, step],
                send_sem.at[n],
                narrow_recv.at[n, lax.div(step, PART)],
                device_of(to_group, to_head, plane),
            ).start()
        return carry

    def send_wide(step, carry):
        peer = lax.rem(me + step, PEERS)
        to_group, to_head = lax.div(peer, KV_HEADS), lax.rem(peer, KV_HEADS)
        for n, (src, dst) in enumerate(wide):
            remote(
                run_of(src, to_group, to_head, UNIT),
                dst.at[step],
                send_sem.at[2 + n],
                wide_recv.at[n],
                device_of(to_group, to_head, plane),
            ).start()
        return carry

    own = [
        pltpu.make_async_copy(run_of(src, group, head, HEAD_DIM), dst.at[plane, 0], own_sem.at[n])
        for n, (src, dst) in enumerate(narrow)
    ] + [
        pltpu.make_async_copy(run_of(src, group, head, UNIT), dst.at[0], own_sem.at[2 + n])
        for n, (src, dst) in enumerate(wide)
    ]
    own += [
        pltpu.make_async_copy(target_ref, target_out, own_sem.at[4]),
        pltpu.make_async_copy(length_ref, length_out, own_sem.at[5]),
    ]
    own[0].start()
    own[1].start()
    lax.fori_loop(1, PEERS, send_narrow, 0)
    for copy in own[2:]:
        copy.start()

    def ring(way, step, n, part):
        chunk = lax.rem(plane + (PLANES - step if way == 0 else step), PLANES)
        target = lax.rem(plane + (1 if way == 0 else PLANES - 1), PLANES)
        piece = narrow[n][1].at[chunk, pl.ds(part * PART, PART)]
        return remote(
            piece,
            piece,
            ring_send.at[way, n],
            ring_recv.at[way, step, n, part],
            device_of(group, head, target),
        )

    def make_tables():
        own[4].wait()
        own[5].wait()
        lane = lax.broadcasted_iota(jnp.int32, (8, 128), 1)
        place_of = lax.broadcasted_iota(jnp.int32, (8, 128), 0) * 128 + lane

        def invert(source, inverse):
            slot = (me - source) & (PEERS - 1)
            for from_plane in range(PLANES):
                for which in range(2):
                    block = target_of(target_out, group, source, from_plane, which)
                    inverse = jnp.where(place_of == block, 2 * (from_plane * PEERS + slot) + which, inverse)
            return inverse

        table[0] = lax.fori_loop(0, PEERS, invert, jnp.zeros((8, 128), jnp.int32))

        def mine(step):
            return target_of(target_out, group, (me - (step >> 1)) & (PEERS - 1), plane, step & 1)

        blocks = lax.fori_loop(
            0,
            PLANE_BLOCKS,
            lambda step, blocks: jnp.where(lane == step, mine(step), blocks),
            jnp.full((8, 128), GROUP_BLOCKS, jnp.int32),
            unroll=8,
        )
        table[1] = lax.fori_loop(
            0,
            PLANE_BLOCKS,
            lambda step, rank: rank + jnp.where(blocks > mine(step), 1, 0),
            jnp.zeros((8, 128), jnp.int32),
            unroll=8,
        )
        for n, dst in enumerate((packed_from, ranks_out)):
            copy = pltpu.make_async_copy(table.at[n], dst, own_sem.at[6 + n])
            copy.start()
            copy.wait()

    lax.fori_loop(1, WIDE_EARLY, send_wide, 0)
    wide_next = WIDE_EARLY
    for step in range(4):
        for part in range(PARTS):
            for n in range(2):
                if step == 0:
                    if part == 0:
                        own[n].wait()
                    landed = narrow[n][1].at[plane, pl.ds(part * PART, PART - (part == 0))]
                    remote(landed, landed, send_sem.at[n], narrow_recv.at[n, part], here).wait_recv()
                for way in range(2):
                    if step == 3 and n != way:
                        continue
                    if step > 0:
                        ring(way, step - 1, n, part).wait_recv()
                    ring(way, step, n, part).start()
                wide_after = min(wide_next + WIDE_EACH, PEERS)
                lax.fori_loop(wide_next, wide_after, send_wide, 0)
                wide_next = wide_after
        if step == 1:
            make_tables()
    for part in range(PARTS):
        for way in range(2):
            ring(way, 2, 1 - way, part).wait_recv()
    for part in range(PARTS):
        for way in range(2):
            ring(way, 3, way, part).wait_recv()
    for way in range(2):
        for n in range(2):
            sent = narrow[n][1].at[pl.ds(0, 4 if n == way else 3)]
            remote(sent, sent, ring_send.at[way, n], ring_recv.at[way, 0, n, 0], here).wait_send()

    def pack(chunk, carry):
        first = chunk * CHUNK_BLOCKS
        rows = pl.ds(pl.multiple_of(chunk * CHUNK, CHUNK), CHUNK)
        held = [packed_from[(first + n) >> 7, (first + n) & 127] for n in range(CHUNK_BLOCKS)]
        keys = jnp.concatenate([half_of(k_out[h >> 6, (h >> 1) & (PEERS - 1)], h & 1) for h in held], axis=0)
        k_pack[rows, :] = keys.astype(BF16)
        k_turned[chunk] = jnp.transpose(keys).astype(BF16)
        values = jnp.concatenate([half_of(v_out[h >> 6, (h >> 1) & (PEERS - 1)], h & 1) for h in held], axis=0)
        v_pack[rows, :] = values.astype(BF16)
        return carry

    lax.fori_loop(0, CHUNKS, pack, 0, unroll=4)
    for n in range(2):
        sent = narrow[n][1].at[0, pl.ds(0, PEERS - 1)]
        remote(sent, sent, send_sem.at[n], narrow_recv.at[n, 0], here).wait_send()
        own[2 + n].wait()
        landed = wide[n][1].at[pl.ds(0, PEERS - 1)]
        rest = remote(landed, landed, send_sem.at[2 + n], wide_recv.at[n], here)
        rest.wait_recv()
        rest.wait_send()


def scatter(query_rows, output_grad, key_rows, value_rows, block_target, doc_lengths):
    wide = jax.ShapeDtypeStruct((PEERS, RUN, UNIT), BF16)
    narrow = pltpu.VMEM((PLANES, PEERS, RUN, HEAD_DIM), BF16)
    packed = jax.ShapeDtypeStruct((GROUP_TOKENS, HEAD_DIM), BF16)
    return pl.pallas_call(
        scatter_kernel,
        name="scatter",
        out_shape=(
            wide,
            wide,
            packed,
            packed,
            jax.ShapeDtypeStruct((CHUNKS, HEAD_DIM, CHUNK), BF16),
            jax.ShapeDtypeStruct(block_target.shape, jnp.int32),
            jax.ShapeDtypeStruct(doc_lengths.shape, jnp.int32),
            jax.ShapeDtypeStruct((8, 128), jnp.int32),
        ),
        in_specs=[pl.BlockSpec(memory_space=pltpu.HBM)] * 6,
        out_specs=[pl.BlockSpec(memory_space=pl.ANY)] * 2
        + [pl.BlockSpec(memory_space=pltpu.VMEM)] * 3
        + [pl.BlockSpec(memory_space=pltpu.SMEM)] * 3,
        scratch_shapes=[
            narrow,
            narrow,
            pltpu.VMEM((2, 8, 128), jnp.int32),
            pltpu.SMEM((8, 128), jnp.int32),
            pltpu.SemaphoreType.DMA((4,)),
            pltpu.SemaphoreType.DMA((2, PARTS)),
            pltpu.SemaphoreType.DMA((2,)),
            pltpu.SemaphoreType.DMA((8,)),
            pltpu.SemaphoreType.DMA((2, 2)),
            pltpu.SemaphoreType.DMA((2, 4, 2, PARTS)),
        ],
        compiler_params=pltpu.CompilerParams(
            collective_id=0, has_side_effects=True, vmem_limit_bytes=10 * 1024 * 1024
        ),
    )(
        *(
            pltpu.with_memory_space_constraint(rows, pltpu.HBM)
            for rows in (query_rows, output_grad, key_rows, value_rows, block_target, doc_lengths)
        )
    )


def attention_kernel(
    length_ref,
    rank_ref,
    target_ref,
    q_ref,
    g_ref,
    k_pack,
    v_pack,
    k_turned,
    dq_turned,
    dk_acc,
    dv_acc,
    query_order,
    query_block,
    doc_ends,
    q_tiles,
    g_tiles,
    bounds,
    spans,
    exps,
    probs,
    maxes,
):
    group, head, plane = place()
    me = group * KV_HEADS + head

    def sort(step, carry):
        rank = rank_ref[0, step]
        query_order[rank] = step
        query_block[rank] = target_of(target_ref, group, (me - (step >> 1)) & (PEERS - 1), plane, step & 1)
        return carry

    lax.fori_loop(0, PLANE_BLOCKS, sort, 0, unroll=8)

    end = jnp.int32(0)
    for n in range(DOCS):
        end = end + length_ref[0, n]
        doc_ends[n] = end

    def clear(step, carry):
        rows = pl.ds(pl.multiple_of(step * CHUNK, CHUNK), CHUNK)
        dk_acc[rows, :] = jnp.zeros((CHUNK, HEAD_DIM), F32)
        dv_acc[rows, :] = jnp.zeros((CHUNK, HEAD_DIM), F32)
        return carry

    lax.fori_loop(0, CHUNKS, clear, 0, unroll=2)

    lane = lax.broadcasted_iota(jnp.int32, (1, TILE_ROWS), 1)
    owner = lane // (SHARE * BLOCK_ROWS)

    def prepare(tile, carry):
        slots = [query_order[tile * TILE_BLOCKS + n] for n in range(TILE_BLOCKS)]
        blocks = [query_block[tile * TILE_BLOCKS + n] for n in range(TILE_BLOCKS)]
        for src, dst in ((q_ref, q_tiles), (g_ref, g_tiles)):
            parts = []
            for slot in slots:
                rows = half_of(src[slot >> 1], slot & 1)
                parts += [rows[:, h * HEAD_DIM : (h + 1) * HEAD_DIM] for h in range(SHARE)]
            dst[tile] = jnp.concatenate(parts, axis=0).astype(BF16)
        last = jnp.full((1, TILE_ROWS), blocks[0], jnp.int32)
        for n in range(1, TILE_BLOCKS):
            last = jnp.where(owner == n, blocks[n], last)
        last = last * BLOCK_ROWS + (lane & (BLOCK_ROWS - 1))
        start = jnp.zeros((1, TILE_ROWS), jnp.int32)
        tile_start = jnp.int32(0)
        for n in range(DOCS):
            end = doc_ends[n]
            start = jnp.where(end <= last, end, start)
            tile_start = jnp.where(end <= blocks[0] * BLOCK_ROWS, end, tile_start)
        bounds[tile, 0:1] = start
        bounds[tile, 1:2] = last
        first_chunk = tile_start // CHUNK
        spans[2 * tile] = first_chunk
        spans[2 * tile + 1] = (blocks[-1] * BLOCK_ROWS + BLOCK_ROWS - 1) // CHUNK - first_chunk + 1
        return carry

    lax.fori_loop(0, TILES, prepare, 0, unroll=UNROLL_PREP)

    key_iota = lax.broadcasted_iota(jnp.int32, (CHUNK, TILE_ROWS), 0)
    no_sum = jnp.zeros((8, TILE_ROWS), F32)

    def fold(array, op):
        return op(array.reshape(CHUNK // 8, 8, TILE_ROWS), axis=0)

    def rows_of(chunk):
        return pl.ds(pl.multiple_of(chunk * CHUNK, CHUNK), CHUNK)

    def against(rows_ref, chunk, tile_rows):
        return lax.dot_general(
            rows_ref[rows_of(chunk), :], tile_rows, (((1,), (1,)), ((), ())), preferred_element_type=F32
        )

    def masked(scores, chunk, start, last):
        position = key_iota + chunk * CHUNK
        return jnp.where((position >= start) & (position <= last), scores, -1e30)

    def put_keys(chunk, weights, score_grad, q_low, g_low):
        rows = rows_of(chunk)
        dv_acc[rows, :] += jnp.dot(weights.astype(BF16), g_low, preferred_element_type=F32)
        dk_acc[rows, :] += jnp.dot(score_grad, q_low, preferred_element_type=F32)
        return jnp.dot(k_turned[chunk], score_grad, preferred_element_type=F32)

    def query_tiles(step, carry):
        tiles = [step * TOGETHER + n for n in range(TOGETHER)]
        firsts = [spans[2 * tile] for tile in tiles]
        counts = [spans[2 * tile + 1] for tile in tiles]
        most = counts[0]
        for count in counts[1:]:
            most = jnp.maximum(most, count)

        def fixed(chunks):
            begins = [jnp.minimum(first, CHUNKS - chunks) for first in firsts]
            ways = range(TOGETHER)
            q_low = [q_tiles[tile] for tile in tiles]
            g_low = [g_tiles[tile] for tile in tiles]
            start = [bounds[tile, 0:1] for tile in tiles]
            last = [bounds[tile, 1:2] for tile in tiles]
            top = [jnp.full((8, TILE_ROWS), -1e30, F32)] * TOGETHER
            for n in range(chunks):
                for w in ways:
                    chunk = begins[w] + n
                    scores = masked(against(k_pack, chunk, q_low[w]), chunk, start[w], last[w])
                    exps[w * FIXED_MAX + n] = scores
                    top[w] = jnp.maximum(top[w], fold(scores, jnp.max))
            top = [jnp.max(t, axis=0, keepdims=True) for t in top]
            total, weighted = [no_sum] * TOGETHER, [no_sum] * TOGETHER
            for n in range(chunks):
                for w in ways:
                    prob_grad = against(v_pack, begins[w] + n, g_low[w])
                    weights = jnp.exp2((exps[w * FIXED_MAX + n] - top[w]) * EXP2_SCALE)
                    total[w] += fold(weights, jnp.sum)
                    weighted[w] += fold(weights * prob_grad, jnp.sum)
                    exps[w * FIXED_MAX + n] = weights
                    probs[w * FIXED_MAX + n] = prob_grad
            factor = [1.0 / jnp.sum(t, axis=0, keepdims=True) for t in total]
            delta = [jnp.sum(t, axis=0, keepdims=True) * f for t, f in zip(weighted, factor)]
            dq = [jnp.zeros((HEAD_DIM, TILE_ROWS), F32)] * TOGETHER
            for n in range(chunks):
                for w in ways:
                    weights = exps[w * FIXED_MAX + n] * factor[w]
                    score_grad = (weights * (probs[w * FIXED_MAX + n] - delta[w])).astype(BF16)
                    dq[w] += put_keys(begins[w] + n, weights, score_grad, q_low[w], g_low[w])
            for w in ways:
                dq_turned[tiles[w]] = dq[w]

        for chunks in range(1, FIXED_MAX + 1):

            @pl.when(most == chunks)
            def _():
                fixed(chunks)

        @pl.when(most > FIXED_MAX)
        def _():
            for tile, first, count in zip(tiles, firsts, counts):
                any_length(tile, first, count)

        return carry

    def any_length(tile, first, count):
        q_low, g_low = q_tiles[tile], g_tiles[tile]
        start, last = bounds[tile, 0:1], bounds[tile, 1:2]

        def totals(slot, state):
            top, total, weighted = state
            chunk = first + slot
            scores = masked(against(k_pack, chunk, q_low), chunk, start, last)
            prob_grad = against(v_pack, chunk, g_low)
            new_top = jnp.maximum(top, jnp.max(scores, axis=0, keepdims=True))
            weights = jnp.exp2((scores - new_top) * EXP2_SCALE)
            fade = jnp.exp2((top - new_top) * EXP2_SCALE)
            total = total * fade + jnp.sum(weights, axis=0, keepdims=True)
            weighted = weighted * fade + jnp.sum(weights * prob_grad, axis=0, keepdims=True)
            exps[slot] = weights
            probs[slot] = prob_grad
            maxes[slot] = jnp.broadcast_to(new_top, (8, TILE_ROWS))
            return new_top, total, weighted

        top, total, weighted = lax.fori_loop(
            0, count, totals, (jnp.full((1, TILE_ROWS), -1e20, F32), no_sum[:1], no_sum[:1])
        )
        scale_row = 1.0 / total
        delta = weighted * scale_row

        def gradients(slot, dq):
            factor = jnp.exp2((maxes[slot][:1] - top) * EXP2_SCALE) * scale_row
            weights = exps[slot] * factor
            score_grad = (weights * (probs[slot] - delta)).astype(BF16)
            return dq + put_keys(first + slot, weights, score_grad, q_low, g_low)

        dq_turned[tile] = lax.fori_loop(0, count, gradients, jnp.zeros((HEAD_DIM, TILE_ROWS), F32))

    lax.fori_loop(0, TILES // TOGETHER, query_tiles, 0)


def attention(doc_lengths, ranks, block_target, queries, grads, keys, values, keys_turned):
    acc = jax.ShapeDtypeStruct((GROUP_TOKENS, HEAD_DIM), F32)
    return pl.pallas_call(
        attention_kernel,
        name="attention",
        out_shape=(jax.ShapeDtypeStruct((TILES, HEAD_DIM, TILE_ROWS), F32), acc, acc),
        in_specs=[pl.BlockSpec(memory_space=pltpu.SMEM)] * 3 + [pl.BlockSpec(memory_space=pltpu.VMEM)] * 5,
        out_specs=[pl.BlockSpec(memory_space=pltpu.VMEM)] * 3,
        scratch_shapes=[
            pltpu.SMEM((PLANE_BLOCKS,), jnp.int32),
            pltpu.SMEM((PLANE_BLOCKS,), jnp.int32),
            pltpu.SMEM((DOCS,), jnp.int32),
            pltpu.VMEM((TILES, TILE_ROWS, HEAD_DIM), BF16),
            pltpu.VMEM((TILES, TILE_ROWS, HEAD_DIM), BF16),
            pltpu.VMEM((TILES, 8, TILE_ROWS), jnp.int32),
            pltpu.SMEM((2 * TILES,), jnp.int32),
            pltpu.VMEM((CHUNKS, CHUNK, TILE_ROWS), F32),
            pltpu.VMEM((CHUNKS, CHUNK, TILE_ROWS), F32),
            pltpu.VMEM((CHUNKS, 8, TILE_ROWS), F32),
        ],
        compiler_params=pltpu.CompilerParams(vmem_limit_bytes=30 * 1024 * 1024),
    )(doc_lengths, ranks, block_target, queries, grads, keys, values, keys_turned)


def collect_kernel(
    rank_ref,
    target_ref,
    dq_turned,
    dk_ref,
    dv_ref,
    dq_out,
    dk_out,
    dv_out,
    dq_ref,
    dq_tiles,
    outbox,
    inbox,
    total,
    send_sem,
    recv_sem,
    own_sem,
    ring_send,
    ring_recv,
):
    group, head, plane = place()
    me = group * KV_HEADS + head
    here = device_of(group, head, plane)
    parts = (dk_ref, dv_ref)
    outs = (dk_out, dv_out)

    def home_of(ref, width):
        return ref.at[
            pl.ds(pl.multiple_of(group * RUN, RUN), RUN), pl.ds(pl.multiple_of(head * width, width), width)
        ]

    def owner_of(slot):
        peer = lax.rem(me + PEERS - slot, PEERS)
        return device_of(lax.div(peer, KV_HEADS), lax.rem(peer, KV_HEADS), plane)

    def rows_of(n, slot, chunk):
        halves = []
        for which in range(2):
            block = target_of(target_ref, group, (me - slot) & (PEERS - 1), chunk, which)
            halves.append(parts[n][block])
        rows = jnp.concatenate(halves, axis=0)
        return rows * SCORE_SCALE if n == 0 else rows

    def turn(tile, carry):
        rows = jnp.transpose(dq_turned[tile]) * SCORE_SCALE
        dq_tiles[pl.ds(tile * TILE_PARTS, TILE_PARTS)] = rows.reshape(TILE_PARTS, BLOCK_ROWS, HEAD_DIM)
        return carry

    def put_wide(slot):
        halves = []
        for which in range(2):
            first = rank_ref[0, 2 * slot + which] * SHARE
            halves.append(jnp.concatenate([dq_tiles[first + h] for h in range(SHARE)], axis=1))
        dq_ref[slot] = jnp.concatenate(halves, axis=0).astype(BF16)

    def send_wide(slot, carry):
        put_wide(slot)
        remote(dq_ref.at[slot], home_of(dq_out, UNIT), send_sem.at[2], recv_sem.at[2], owner_of(slot)).start()
        return carry

    def ring(way, step, n, part, src):
        target = lax.rem(plane + (1 if way == 0 else PLANES - 1), PLANES)
        return remote(
            src,
            inbox.at[way, n, step, pl.ds(part * PART, PART)],
            ring_send.at[way, n],
            ring_recv.at[way, step, n, part],
            device_of(group, head, target),
        )

    def chunk_at(way, step):
        distance = 4 - step
        return lax.rem(plane + (distance if way == 0 else PLANES - distance), PLANES)

    def fill_box(way, n, first, after, chunk):
        def fill(slot, carry):
            outbox[way, n, slot] = rows_of(n, slot, chunk).astype(BF16)
            return carry

        lax.fori_loop(first, after, fill, 0, unroll=4)

    def fill_first():
        for way in range(2):
            fill_box(way, way, 0, PEERS, chunk_at(way, 0))

    greet(group, head, plane, fill_first)

    for step in range(4):
        for part in range(PARTS):
            piece = pl.ds(part * PART, PART)
            for n in range(2):
                for way in range(2):
                    chunk = chunk_at(way, step)
                    if step == 0 and n != way:
                        continue
                    if step == 0 or (step == 1 and n != way):
                        if step == 1:
                            fill_box(way, n, part * PART, (part + 1) * PART, chunk)
                        ring(way, step, n, part, outbox.at[way, n, piece]).start()
                    else:
                        held = inbox.at[way, n, step - 1, piece]
                        ring(way, step - 1, n, part, held).wait_recv()

                        def add(slot, carry):
                            sum_so_far = inbox[way, n, step - 1, slot].astype(F32)
                            inbox[way, n, step - 1, slot] = (sum_so_far + rows_of(n, slot, chunk)).astype(BF16)
                            return carry

                        lax.fori_loop(part * PART, (part + 1) * PART, add, 0, unroll=8)
                        ring(way, step, n, part, held).start()
                if step > 0:
                    wide_after = min(wide_next + 2, PEERS)
                    lax.fori_loop(wide_next, wide_after, send_wide, 0)
                    wide_next = wide_after
        if step == 0:
            lax.fori_loop(0, TILES, turn, 0, unroll=4)
            put_wide(0)
            own_wide = pltpu.make_async_copy(dq_ref.at[0], home_of(dq_out, UNIT), own_sem.at[2])
            own_wide.start()
            lax.fori_loop(1, 4, send_wide, 0)
            wide_next = 4
    own = [pltpu.make_async_copy(total.at[n, 0], home_of(outs[n], HEAD_DIM), own_sem.at[n]) for n in range(2)]
    for part in range(PARTS):
        piece = pl.ds(part * PART, PART)
        for n in range(2):
            for way in range(2):
                ring(way, 3, n, part, inbox.at[way, n, 3, piece]).wait_recv()

            def sum_up(slot, carry):
                arrived = inbox[0, n, 3, slot].astype(F32) + inbox[1, n, 3, slot].astype(F32)
                total[n, slot] = (rows_of(n, slot, plane) + arrived).astype(BF16)
                return carry

            lax.fori_loop(part * PART, (part + 1) * PART, sum_up, 0, unroll=8)

            def send_narrow(slot, carry):
                remote(
                    total.at[n, slot], home_of(outs[n], HEAD_DIM), send_sem.at[n], recv_sem.at[n], owner_of(slot)
                ).start()
                return carry

            if part == 0:
                own[n].start()
            lax.fori_loop(max(1, part * PART), (part + 1) * PART, send_narrow, 0)
    for way in range(2):
        for n in range(2):
            sent = inbox.at[way, n, pl.ds(0, 4 if n == way else 3)]
            remote(sent, sent, ring_send.at[way, n], ring_recv.at[way, 0, n, 0], here).wait_send()
    own_wide.wait()
    sent = dq_ref.at[pl.ds(0, PEERS - 1)]
    rest = remote(sent, sent, send_sem.at[2], recv_sem.at[2], here)
    rest.wait_send()
    rest.wait_recv()
    for n in range(2):
        sent = total.at[n, pl.ds(0, PEERS - 1)]
        rest = remote(sent, sent, send_sem.at[n], recv_sem.at[n], here)
        rest.wait_send()
        rest.wait_recv()
        own[n].wait()


def collect(ranks, block_target, dq, dk, dv):
    return pl.pallas_call(
        collect_kernel,
        name="collect",
        out_shape=(
            jax.ShapeDtypeStruct((GROUPS * RUN, KV_HEADS * UNIT), BF16),
            jax.ShapeDtypeStruct((GROUPS * RUN, KV_HEADS * HEAD_DIM), BF16),
            jax.ShapeDtypeStruct((GROUPS * RUN, KV_HEADS * HEAD_DIM), BF16),
        ),
        in_specs=[pl.BlockSpec(memory_space=pltpu.SMEM)] * 2 + [pl.BlockSpec(memory_space=pltpu.VMEM)] * 3,
        out_specs=[pl.BlockSpec(memory_space=pl.ANY)] * 3,
        scratch_shapes=[
            pltpu.VMEM((PEERS, RUN, UNIT), BF16),
            pltpu.VMEM((TILES * TILE_PARTS, BLOCK_ROWS, HEAD_DIM), F32),
            pltpu.VMEM((2, 2, PEERS, RUN, HEAD_DIM), BF16),
            pltpu.VMEM((2, 2, 4, PEERS, RUN, HEAD_DIM), BF16),
            pltpu.VMEM((2, PEERS, RUN, HEAD_DIM), BF16),
            pltpu.SemaphoreType.DMA((3,)),
            pltpu.SemaphoreType.DMA((3,)),
            pltpu.SemaphoreType.DMA((3,)),
            pltpu.SemaphoreType.DMA((2, 2)),
            pltpu.SemaphoreType.DMA((2, 4, 2, PARTS)),
        ],
        compiler_params=pltpu.CompilerParams(
            collective_id=1, has_side_effects=True, vmem_limit_bytes=24 * 1024 * 1024
        ),
    )(ranks, block_target, dq, dk, dv)


def deliver_kernel(*refs):
    copies = [pltpu.make_async_copy(refs[n], refs[3 + n], refs[6].at[n]) for n in range(3)]
    for copy in copies:
        copy.start()
    for copy in copies:
        copy.wait()


def deliver(*grads):
    return pl.pallas_call(
        deliver_kernel,
        name="deliver",
        out_shape=tuple(jax.ShapeDtypeStruct(grad.shape, grad.dtype) for grad in grads),
        in_specs=[pl.BlockSpec(memory_space=pl.ANY)] * 3,
        out_specs=[pl.BlockSpec(memory_space=pl.ANY)] * 3,
        scratch_shapes=[pltpu.SemaphoreType.DMA((3,))],
        compiler_params=pltpu.CompilerParams(vmem_limit_bytes=1024 * 1024),
    )(*grads)


def on_device(query_rows, key_rows, value_rows, output_grad, block_target, doc_lengths):
    queries, grads, keys, values, keys_turned, targets, lengths, ranks = scatter(
        query_rows, output_grad, key_rows, value_rows, block_target.transpose(0, 2, 1), doc_lengths
    )
    dq, dk, dv = attention(lengths, ranks, targets, queries, grads, keys, values, keys_turned)
    blocks = (GROUP_BLOCKS, BLOCK_ROWS, HEAD_DIM)
    return deliver(*collect(ranks, targets, dq, dk.reshape(blocks), dv.reshape(blocks)))


def solution(mesh):
    in_specs = (
        P(("grp", "ctx"), None),
        P(("grp", "ctx"), None),
        P(("grp", "ctx"), None),
        P(("grp", "ctx"), None),
        P(),
        P("grp", None),
    )
    out_specs = (P(("grp", "ctx"), None), P(("grp", "ctx"), None), P(("grp", "ctx"), None))
    return jax.shard_map(
        on_device, mesh=mesh, in_specs=in_specs, out_specs=out_specs, check_vma=False
    )
```

```python
import jax
import jax.numpy as jnp
from jax import lax
from jax.experimental import pallas as pl
from jax.experimental.pallas import tpu as pltpu
from jax.sharding import PartitionSpec as P

KV_HEADS = 4
HEAD_DIM = 128
SHARE = 8
BLOCK_ROWS = 8
GROUPS = 8
PLANES = 8
PEERS = 32
RUN = 16
UNIT = SHARE * HEAD_DIM
GROUP_BLOCKS = 512
GROUP_TOKENS = 4096
PLANE_BLOCKS = 64
DOCS = 16
TILE_BLOCKS = 4
TILE_ROWS = TILE_BLOCKS * SHARE * BLOCK_ROWS
TILE_PARTS = TILE_ROWS // BLOCK_ROWS
TILES = PLANE_BLOCKS // TILE_BLOCKS
CHUNK = 128
CHUNKS = GROUP_TOKENS // CHUNK
CHUNK_BLOCKS = CHUNK // BLOCK_ROWS
FIXED_MAX = 7
TOGETHER = 2
UNROLL_PREP = 4
SCORE_SCALE = HEAD_DIM**-0.5
EXP2_SCALE = SCORE_SCALE * 1.4426950408889634
PARTS = 4
PART = PEERS // PARTS
WIDE_EARLY = 8
WIDE_EACH = 2
MESH = pl.DeviceIdType.MESH
F32 = jnp.float32
BF16 = jnp.bfloat16


def place():
    group = lax.axis_index("grp")
    ctx = lax.axis_index("ctx")
    y_hi = ctx // 16
    plane = (ctx // 2) % PLANES
    core = ctx % 2
    head = y_hi * 2 + core
    return group, head, plane


def device_of(group, head, plane):
    return {"grp": group, "ctx": lax.div(head, 2) * 16 + plane * 2 + lax.rem(head, 2)}


def half_of(pair, which):
    wide = pair.astype(F32)
    return jnp.where(which == 0, wide[:BLOCK_ROWS], wide[BLOCK_ROWS:])


def target_of(target_ref, group, source, from_plane, which):
    ctx = ((source >> 1) & 1) * 16 + (source & 1) + from_plane * 2
    return target_ref[source >> 2, 2 * group + which, ctx] & (GROUP_BLOCKS - 1)


def greet(group, head, plane, meanwhile=None):
    barrier = pltpu.get_barrier_semaphore()
    me = group * KV_HEADS + head

    def one(step, carry):
        peer = lax.rem(me + step, PEERS)
        pl.semaphore_signal(
            barrier,
            inc=1,
            device_id=device_of(lax.div(peer, KV_HEADS), lax.rem(peer, KV_HEADS), plane),
            device_id_type=MESH,
        )
        return carry

    lax.fori_loop(1, PEERS, one, 0)
    for by in (1, PLANES - 1):
        pl.semaphore_signal(
            barrier,
            inc=1,
            device_id=device_of(group, head, lax.rem(plane + by, PLANES)),
            device_id_type=MESH,
        )
    if meanwhile is not None:
        meanwhile()
    pl.semaphore_wait(barrier, PEERS - 1 + 2)


def remote(src, dst, send, recv, device):
    return pltpu.make_async_remote_copy(
        src_ref=src, dst_ref=dst, send_sem=send, recv_sem=recv, device_id=device, device_id_type=MESH
    )


def scatter_kernel(
    q_ref,
    g_ref,
    k_ref,
    v_ref,
    target_ref,
    length_ref,
    q_out,
    g_out,
    k_pack,
    v_pack,
    k_turned,
    target_out,
    length_out,
    ranks_out,
    k_out,
    v_out,
    table,
    packed_from,
    send_sem,
    narrow_recv,
    wide_recv,
    own_sem,
    ring_send,
    ring_recv,
):
    group, head, plane = place()
    me = group * KV_HEADS + head
    greet(group, head, plane)
    here = device_of(group, head, plane)
    narrow = ((k_ref, k_out), (v_ref, v_out))
    wide = ((q_ref, q_out), (g_ref, g_out))

    def run_of(ref, to_group, to_head, width):
        return ref.at[
            pl.ds(pl.multiple_of(to_group * RUN, RUN), RUN),
            pl.ds(pl.multiple_of(to_head * width, width), width),
        ]

    def send_narrow(step, carry):
        peer = lax.rem(me + step, PEERS)
        to_group, to_head = lax.div(peer, KV_HEADS), lax.rem(peer, KV_HEADS)
        for n, (src, dst) in enumerate(narrow):
            remote(
                run_of(src, to_group, to_head, HEAD_DIM),
                dst.at[plane, step],
                send_sem.at[n],
                narrow_recv.at[n, lax.div(step, PART)],
                device_of(to_group, to_head, plane),
            ).start()
        return carry

    def send_wide(step, carry):
        peer = lax.rem(me + step, PEERS)
        to_group, to_head = lax.div(peer, KV_HEADS), lax.rem(peer, KV_HEADS)
        for n, (src, dst) in enumerate(wide):
            remote(
                run_of(src, to_group, to_head, UNIT),
                dst.at[step],
                send_sem.at[2 + n],
                wide_recv.at[n],
                device_of(to_group, to_head, plane),
            ).start()
        return carry

    own = [
        pltpu.make_async_copy(run_of(src, group, head, HEAD_DIM), dst.at[plane, 0], own_sem.at[n])
        for n, (src, dst) in enumerate(narrow)
    ] + [
        pltpu.make_async_copy(run_of(src, group, head, UNIT), dst.at[0], own_sem.at[2 + n])
        for n, (src, dst) in enumerate(wide)
    ]
    own += [
        pltpu.make_async_copy(target_ref, target_out, own_sem.at[4]),
        pltpu.make_async_copy(length_ref, length_out, own_sem.at[5]),
    ]
    own[0].start()
    own[1].start()
    lax.fori_loop(1, PEERS, send_narrow, 0)
    for copy in own[2:]:
        copy.start()

    def ring(way, step, n, part):
        chunk = lax.rem(plane + (PLANES - step if way == 0 else step), PLANES)
        target = lax.rem(plane + (1 if way == 0 else PLANES - 1), PLANES)
        piece = narrow[n][1].at[chunk, pl.ds(part * PART, PART)]
        return remote(
            piece,
            piece,
            ring_send.at[way, n],
            ring_recv.at[way, step, n, part],
            device_of(group, head, target),
        )

    def make_tables():
        own[4].wait()
        own[5].wait()
        lane = lax.broadcasted_iota(jnp.int32, (8, 128), 1)
        place_of = lax.broadcasted_iota(jnp.int32, (8, 128), 0) * 128 + lane

        def invert(source, inverse):
            slot = (me - source) & (PEERS - 1)
            for from_plane in range(PLANES):
                for which in range(2):
                    block = target_of(target_out, group, source, from_plane, which)
                    inverse = jnp.where(place_of == block, 2 * (from_plane * PEERS + slot) + which, inverse)
            return inverse

        table[0] = lax.fori_loop(0, PEERS, invert, jnp.zeros((8, 128), jnp.int32))

        def mine(step):
            return target_of(target_out, group, (me - (step >> 1)) & (PEERS - 1), plane, step & 1)

        blocks = lax.fori_loop(
            0,
            PLANE_BLOCKS,
            lambda step, blocks: jnp.where(lane == step, mine(step), blocks),
            jnp.full((8, 128), GROUP_BLOCKS, jnp.int32),
            unroll=8,
        )
        table[1] = lax.fori_loop(
            0,
            PLANE_BLOCKS,
            lambda step, rank: rank + jnp.where(blocks > mine(step), 1, 0),
            jnp.zeros((8, 128), jnp.int32),
            unroll=8,
        )
        for n, dst in enumerate((packed_from, ranks_out)):
            copy = pltpu.make_async_copy(table.at[n], dst, own_sem.at[6 + n])
            copy.start()
            copy.wait()

    lax.fori_loop(1, WIDE_EARLY, send_wide, 0)
    wide_next = WIDE_EARLY
    for step in range(4):
        for part in range(PARTS):
            for n in range(2):
                if step == 0:
                    if part == 0:
                        own[n].wait()
                    landed = narrow[n][1].at[plane, pl.ds(part * PART, PART - (part == 0))]
                    remote(landed, landed, send_sem.at[n], narrow_recv.at[n, part], here).wait_recv()
                for way in range(2):
                    if step == 3 and n != way:
                        continue
                    if step > 0:
                        ring(way, step - 1, n, part).wait_recv()
                    ring(way, step, n, part).start()
                wide_after = min(wide_next + WIDE_EACH, PEERS)
                lax.fori_loop(wide_next, wide_after, send_wide, 0)
                wide_next = wide_after
        if step == 1:
            make_tables()
    for part in range(PARTS):
        for way in range(2):
            ring(way, 2, 1 - way, part).wait_recv()
    for part in range(PARTS):
        for way in range(2):
            ring(way, 3, way, part).wait_recv()
    for way in range(2):
        for n in range(2):
            sent = narrow[n][1].at[pl.ds(0, 4 if n == way else 3)]
            remote(sent, sent, ring_send.at[way, n], ring_recv.at[way, 0, n, 0], here).wait_send()

    def pack(chunk, carry):
        first = chunk * CHUNK_BLOCKS
        rows = pl.ds(pl.multiple_of(chunk * CHUNK, CHUNK), CHUNK)
        held = [packed_from[(first + n) >> 7, (first + n) & 127] for n in range(CHUNK_BLOCKS)]
        keys = jnp.concatenate([half_of(k_out[h >> 6, (h >> 1) & (PEERS - 1)], h & 1) for h in held], axis=0)
        k_pack[rows, :] = keys.astype(BF16)
        k_turned[chunk] = jnp.transpose(keys).astype(BF16)
        values = jnp.concatenate([half_of(v_out[h >> 6, (h >> 1) & (PEERS - 1)], h & 1) for h in held], axis=0)
        v_pack[rows, :] = values.astype(BF16)
        return carry

    lax.fori_loop(0, CHUNKS, pack, 0, unroll=4)
    for n in range(2):
        sent = narrow[n][1].at[0, pl.ds(0, PEERS - 1)]
        remote(sent, sent, send_sem.at[n], narrow_recv.at[n, 0], here).wait_send()
        own[2 + n].wait()
        landed = wide[n][1].at[pl.ds(0, PEERS - 1)]
        rest = remote(landed, landed, send_sem.at[2 + n], wide_recv.at[n], here)
        rest.wait_recv()
        rest.wait_send()


def scatter(query_rows, output_grad, key_rows, value_rows, block_target, doc_lengths):
    wide = jax.ShapeDtypeStruct((PEERS, RUN, UNIT), BF16)
    narrow = pltpu.VMEM((PLANES, PEERS, RUN, HEAD_DIM), BF16)
    packed = jax.ShapeDtypeStruct((GROUP_TOKENS, HEAD_DIM), BF16)
    return pl.pallas_call(
        scatter_kernel,
        name="scatter",
        out_shape=(
            wide,
            wide,
            packed,
            packed,
            jax.ShapeDtypeStruct((CHUNKS, HEAD_DIM, CHUNK), BF16),
            jax.ShapeDtypeStruct(block_target.shape, jnp.int32),
            jax.ShapeDtypeStruct(doc_lengths.shape, jnp.int32),
            jax.ShapeDtypeStruct((8, 128), jnp.int32),
        ),
        in_specs=[pl.BlockSpec(memory_space=pltpu.HBM)] * 6,
        out_specs=[pl.BlockSpec(memory_space=pl.ANY)] * 2
        + [pl.BlockSpec(memory_space=pltpu.VMEM)] * 3
        + [pl.BlockSpec(memory_space=pltpu.SMEM)] * 3,
        scratch_shapes=[
            narrow,
            narrow,
            pltpu.VMEM((2, 8, 128), jnp.int32),
            pltpu.SMEM((8, 128), jnp.int32),
            pltpu.SemaphoreType.DMA((4,)),
            pltpu.SemaphoreType.DMA((2, PARTS)),
            pltpu.SemaphoreType.DMA((2,)),
            pltpu.SemaphoreType.DMA((8,)),
            pltpu.SemaphoreType.DMA((2, 2)),
            pltpu.SemaphoreType.DMA((2, 4, 2, PARTS)),
        ],
        compiler_params=pltpu.CompilerParams(
            collective_id=0, has_side_effects=True, vmem_limit_bytes=10 * 1024 * 1024
        ),
    )(
        *(
            pltpu.with_memory_space_constraint(rows, pltpu.HBM)
            for rows in (query_rows, output_grad, key_rows, value_rows, block_target, doc_lengths)
        )
    )


def attention_kernel(
    length_ref,
    rank_ref,
    target_ref,
    q_ref,
    g_ref,
    k_pack,
    v_pack,
    k_turned,
    dq_turned,
    dk_acc,
    dv_acc,
    query_order,
    query_block,
    doc_ends,
    q_tiles,
    g_tiles,
    bounds,
    spans,
    exps,
    probs,
    maxes,
):
    group, head, plane = place()
    me = group * KV_HEADS + head

    def sort(step, carry):
        rank = rank_ref[0, step]
        query_order[rank] = step
        query_block[rank] = target_of(target_ref, group, (me - (step >> 1)) & (PEERS - 1), plane, step & 1)
        return carry

    lax.fori_loop(0, PLANE_BLOCKS, sort, 0, unroll=8)

    end = jnp.int32(0)
    for n in range(DOCS):
        end = end + length_ref[0, n]
        doc_ends[n] = end

    def clear(step, carry):
        rows = pl.ds(pl.multiple_of(step * CHUNK, CHUNK), CHUNK)
        dk_acc[rows, :] = jnp.zeros((CHUNK, HEAD_DIM), F32)
        dv_acc[rows, :] = jnp.zeros((CHUNK, HEAD_DIM), F32)
        return carry

    lax.fori_loop(0, CHUNKS, clear, 0, unroll=2)

    lane = lax.broadcasted_iota(jnp.int32, (1, TILE_ROWS), 1)
    owner = lane // (SHARE * BLOCK_ROWS)

    def prepare(tile, carry):
        slots = [query_order[tile * TILE_BLOCKS + n] for n in range(TILE_BLOCKS)]
        blocks = [query_block[tile * TILE_BLOCKS + n] for n in range(TILE_BLOCKS)]
        for src, dst in ((q_ref, q_tiles), (g_ref, g_tiles)):
            parts = []
            for slot in slots:
                rows = half_of(src[slot >> 1], slot & 1)
                parts += [rows[:, h * HEAD_DIM : (h + 1) * HEAD_DIM] for h in range(SHARE)]
            dst[tile] = jnp.concatenate(parts, axis=0).astype(BF16)
        last = jnp.full((1, TILE_ROWS), blocks[0], jnp.int32)
        for n in range(1, TILE_BLOCKS):
            last = jnp.where(owner == n, blocks[n], last)
        last = last * BLOCK_ROWS + (lane & (BLOCK_ROWS - 1))
        start = jnp.zeros((1, TILE_ROWS), jnp.int32)
        tile_start = jnp.int32(0)
        for n in range(DOCS):
            end = doc_ends[n]
            start = jnp.where(end <= last, end, start)
            tile_start = jnp.where(end <= blocks[0] * BLOCK_ROWS, end, tile_start)
        bounds[tile, 0:1] = start
        bounds[tile, 1:2] = last
        first_chunk = tile_start // CHUNK
        spans[2 * tile] = first_chunk
        spans[2 * tile + 1] = (blocks[-1] * BLOCK_ROWS + BLOCK_ROWS - 1) // CHUNK - first_chunk + 1
        return carry

    lax.fori_loop(0, TILES, prepare, 0, unroll=UNROLL_PREP)

    key_iota = lax.broadcasted_iota(jnp.int32, (CHUNK, TILE_ROWS), 0)
    no_sum = jnp.zeros((8, TILE_ROWS), F32)

    def fold(array, op):
        return op(array.reshape(CHUNK // 8, 8, TILE_ROWS), axis=0)

    def rows_of(chunk):
        return pl.ds(pl.multiple_of(chunk * CHUNK, CHUNK), CHUNK)

    def against(rows_ref, chunk, tile_rows):
        return lax.dot_general(
            rows_ref[rows_of(chunk), :], tile_rows, (((1,), (1,)), ((), ())), preferred_element_type=F32
        )

    def masked(scores, chunk, start, last):
        position = key_iota + chunk * CHUNK
        return jnp.where((position >= start) & (position <= last), scores, -1e30)

    def put_keys(chunk, weights, score_grad, q_low, g_low):
        rows = rows_of(chunk)
        dv_acc[rows, :] += jnp.dot(weights.astype(BF16), g_low, preferred_element_type=F32)
        dk_acc[rows, :] += jnp.dot(score_grad, q_low, preferred_element_type=F32)
        return jnp.dot(k_turned[chunk], score_grad, preferred_element_type=F32)

    def query_tiles(step, carry):
        tiles = [step * TOGETHER + n for n in range(TOGETHER)]
        firsts = [spans[2 * tile] for tile in tiles]
        counts = [spans[2 * tile + 1] for tile in tiles]
        most = counts[0]
        for count in counts[1:]:
            most = jnp.maximum(most, count)

        def fixed(chunks):
            begins = [jnp.minimum(first, CHUNKS - chunks) for first in firsts]
            ways = range(TOGETHER)
            q_low = [q_tiles[tile] for tile in tiles]
            g_low = [g_tiles[tile] for tile in tiles]
            start = [bounds[tile, 0:1] for tile in tiles]
            last = [bounds[tile, 1:2] for tile in tiles]
            top = [jnp.full((8, TILE_ROWS), -1e30, F32)] * TOGETHER
            for n in range(chunks):
                for w in ways:
                    chunk = begins[w] + n
                    scores = masked(against(k_pack, chunk, q_low[w]), chunk, start[w], last[w])
                    exps[w * FIXED_MAX + n] = scores
                    top[w] = jnp.maximum(top[w], fold(scores, jnp.max))
            top = [jnp.max(t, axis=0, keepdims=True) for t in top]
            total, weighted = [no_sum] * TOGETHER, [no_sum] * TOGETHER
            for n in range(chunks):
                for w in ways:
                    prob_grad = against(v_pack, begins[w] + n, g_low[w])
                    weights = jnp.exp2((exps[w * FIXED_MAX + n] - top[w]) * EXP2_SCALE)
                    total[w] += fold(weights, jnp.sum)
                    weighted[w] += fold(weights * prob_grad, jnp.sum)
                    exps[w * FIXED_MAX + n] = weights
                    probs[w * FIXED_MAX + n] = prob_grad
            factor = [1.0 / jnp.sum(t, axis=0, keepdims=True) for t in total]
            delta = [jnp.sum(t, axis=0, keepdims=True) * f for t, f in zip(weighted, factor)]
            dq = [jnp.zeros((HEAD_DIM, TILE_ROWS), F32)] * TOGETHER
            for n in range(chunks):
                for w in ways:
                    weights = exps[w * FIXED_MAX + n] * factor[w]
                    score_grad = (weights * (probs[w * FIXED_MAX + n] - delta[w])).astype(BF16)
                    dq[w] += put_keys(begins[w] + n, weights, score_grad, q_low[w], g_low[w])
            for w in ways:
                dq_turned[tiles[w]] = dq[w]

        for chunks in range(1, FIXED_MAX + 1):

            @pl.when(most == chunks)
            def _():
                fixed(chunks)

        @pl.when(most > FIXED_MAX)
        def _():
            for tile, first, count in zip(tiles, firsts, counts):
                any_length(tile, first, count)

        return carry

    def any_length(tile, first, count):
        q_low, g_low = q_tiles[tile], g_tiles[tile]
        start, last = bounds[tile, 0:1], bounds[tile, 1:2]

        def totals(slot, state):
            top, total, weighted = state
            chunk = first + slot
            scores = masked(against(k_pack, chunk, q_low), chunk, start, last)
            prob_grad = against(v_pack, chunk, g_low)
            new_top = jnp.maximum(top, jnp.max(scores, axis=0, keepdims=True))
            weights = jnp.exp2((scores - new_top) * EXP2_SCALE)
            fade = jnp.exp2((top - new_top) * EXP2_SCALE)
            total = total * fade + jnp.sum(weights, axis=0, keepdims=True)
            weighted = weighted * fade + jnp.sum(weights * prob_grad, axis=0, keepdims=True)
            exps[slot] = weights
            probs[slot] = prob_grad
            maxes[slot] = jnp.broadcast_to(new_top, (8, TILE_ROWS))
            return new_top, total, weighted

        top, total, weighted = lax.fori_loop(
            0, count, totals, (jnp.full((1, TILE_ROWS), -1e20, F32), no_sum[:1], no_sum[:1])
        )
        scale_row = 1.0 / total
        delta = weighted * scale_row

        def gradients(slot, dq):
            factor = jnp.exp2((maxes[slot][:1] - top) * EXP2_SCALE) * scale_row
            weights = exps[slot] * factor
            score_grad = (weights * (probs[slot] - delta)).astype(BF16)
            return dq + put_keys(first + slot, weights, score_grad, q_low, g_low)

        dq_turned[tile] = lax.fori_loop(0, count, gradients, jnp.zeros((HEAD_DIM, TILE_ROWS), F32))

    lax.fori_loop(0, TILES // TOGETHER, query_tiles, 0)


def attention(doc_lengths, ranks, block_target, queries, grads, keys, values, keys_turned):
    acc = jax.ShapeDtypeStruct((GROUP_TOKENS, HEAD_DIM), F32)
    return pl.pallas_call(
        attention_kernel,
        name="attention",
        out_shape=(jax.ShapeDtypeStruct((TILES, HEAD_DIM, TILE_ROWS), F32), acc, acc),
        in_specs=[pl.BlockSpec(memory_space=pltpu.SMEM)] * 3 + [pl.BlockSpec(memory_space=pltpu.VMEM)] * 5,
        out_specs=[pl.BlockSpec(memory_space=pltpu.VMEM)] * 3,
        scratch_shapes=[
            pltpu.SMEM((PLANE_BLOCKS,), jnp.int32),
            pltpu.SMEM((PLANE_BLOCKS,), jnp.int32),
            pltpu.SMEM((DOCS,), jnp.int32),
            pltpu.VMEM((TILES, TILE_ROWS, HEAD_DIM), BF16),
            pltpu.VMEM((TILES, TILE_ROWS, HEAD_DIM), BF16),
            pltpu.VMEM((TILES, 8, TILE_ROWS), jnp.int32),
            pltpu.SMEM((2 * TILES,), jnp.int32),
            pltpu.VMEM((CHUNKS, CHUNK, TILE_ROWS), F32),
            pltpu.VMEM((CHUNKS, CHUNK, TILE_ROWS), F32),
            pltpu.VMEM((CHUNKS, 8, TILE_ROWS), F32),
        ],
        compiler_params=pltpu.CompilerParams(vmem_limit_bytes=30 * 1024 * 1024),
    )(doc_lengths, ranks, block_target, queries, grads, keys, values, keys_turned)


def collect_kernel(
    rank_ref,
    target_ref,
    dq_turned,
    dk_ref,
    dv_ref,
    dq_out,
    dk_out,
    dv_out,
    dq_ref,
    dq_tiles,
    outbox,
    inbox,
    total,
    send_sem,
    recv_sem,
    own_sem,
    ring_send,
    ring_recv,
):
    group, head, plane = place()
    me = group * KV_HEADS + head
    here = device_of(group, head, plane)
    parts = (dk_ref, dv_ref)
    outs = (dk_out, dv_out)

    def home_of(ref, width):
        return ref.at[
            pl.ds(pl.multiple_of(group * RUN, RUN), RUN), pl.ds(pl.multiple_of(head * width, width), width)
        ]

    def owner_of(slot):
        peer = lax.rem(me + PEERS - slot, PEERS)
        return device_of(lax.div(peer, KV_HEADS), lax.rem(peer, KV_HEADS), plane)

    def rows_of(n, slot, chunk):
        halves = []
        for which in range(2):
            block = target_of(target_ref, group, (me - slot) & (PEERS - 1), chunk, which)
            halves.append(parts[n][block])
        rows = jnp.concatenate(halves, axis=0)
        return rows * SCORE_SCALE if n == 0 else rows

    def turn(tile, carry):
        rows = jnp.transpose(dq_turned[tile]) * SCORE_SCALE
        dq_tiles[pl.ds(tile * TILE_PARTS, TILE_PARTS)] = rows.reshape(TILE_PARTS, BLOCK_ROWS, HEAD_DIM)
        return carry

    def put_wide(slot):
        halves = []
        for which in range(2):
            first = rank_ref[0, 2 * slot + which] * SHARE
            halves.append(jnp.concatenate([dq_tiles[first + h] for h in range(SHARE)], axis=1))
        dq_ref[slot] = jnp.concatenate(halves, axis=0).astype(BF16)

    def send_wide(slot, carry):
        put_wide(slot)
        remote(dq_ref.at[slot], home_of(dq_out, UNIT), send_sem.at[2], recv_sem.at[2], owner_of(slot)).start()
        return carry

    def ring(way, step, n, part, src):
        target = lax.rem(plane + (1 if way == 0 else PLANES - 1), PLANES)
        return remote(
            src,
            inbox.at[way, n, step, pl.ds(part * PART, PART)],
            ring_send.at[way, n],
            ring_recv.at[way, step, n, part],
            device_of(group, head, target),
        )

    def chunk_at(way, step):
        distance = 4 - step
        return lax.rem(plane + (distance if way == 0 else PLANES - distance), PLANES)

    def fill_box(way, n, first, after, chunk):
        def fill(slot, carry):
            outbox[way, n, slot] = rows_of(n, slot, chunk).astype(BF16)
            return carry

        lax.fori_loop(first, after, fill, 0, unroll=4)

    def fill_first():
        for way in range(2):
            fill_box(way, way, 0, PEERS, chunk_at(way, 0))

    greet(group, head, plane, fill_first)

    for step in range(4):
        for part in range(PARTS):
            piece = pl.ds(part * PART, PART)
            for n in range(2):
                for way in range(2):
                    chunk = chunk_at(way, step)
                    if step == 0 and n != way:
                        continue
                    if step == 0 or (step == 1 and n != way):
                        if step == 1:
                            fill_box(way, n, part * PART, (part + 1) * PART, chunk)
                        ring(way, step, n, part, outbox.at[way, n, piece]).start()
                    else:
                        held = inbox.at[way, n, step - 1, piece]
                        ring(way, step - 1, n, part, held).wait_recv()

                        def add(slot, carry):
                            sum_so_far = inbox[way, n, step - 1, slot].astype(F32)
                            inbox[way, n, step - 1, slot] = (sum_so_far + rows_of(n, slot, chunk)).astype(BF16)
                            return carry

                        lax.fori_loop(part * PART, (part + 1) * PART, add, 0, unroll=8)
                        ring(way, step, n, part, held).start()
                if step > 0:
                    wide_after = min(wide_next + 2, PEERS)
                    lax.fori_loop(wide_next, wide_after, send_wide, 0)
                    wide_next = wide_after
        if step == 0:
            lax.fori_loop(0, TILES, turn, 0, unroll=4)
            put_wide(0)
            own_wide = pltpu.make_async_copy(dq_ref.at[0], home_of(dq_out, UNIT), own_sem.at[2])
            own_wide.start()
            lax.fori_loop(1, 4, send_wide, 0)
            wide_next = 4
    own = [pltpu.make_async_copy(total.at[n, 0], home_of(outs[n], HEAD_DIM), own_sem.at[n]) for n in range(2)]
    for part in range(PARTS):
        piece = pl.ds(part * PART, PART)
        for n in range(2):
            for way in range(2):
                ring(way, 3, n, part, inbox.at[way, n, 3, piece]).wait_recv()

            def sum_up(slot, carry):
                arrived = inbox[0, n, 3, slot].astype(F32) + inbox[1, n, 3, slot].astype(F32)
                total[n, slot] = (rows_of(n, slot, plane) + arrived).astype(BF16)
                return carry

            lax.fori_loop(part * PART, (part + 1) * PART, sum_up, 0, unroll=8)

            def send_narrow(slot, carry):
                remote(
                    total.at[n, slot], home_of(outs[n], HEAD_DIM), send_sem.at[n], recv_sem.at[n], owner_of(slot)
                ).start()
                return carry

            if part == 0:
                own[n].start()
            lax.fori_loop(max(1, part * PART), (part + 1) * PART, send_narrow, 0)
    for way in range(2):
        for n in range(2):
            sent = inbox.at[way, n, pl.ds(0, 4 if n == way else 3)]
            remote(sent, sent, ring_send.at[way, n], ring_recv.at[way, 0, n, 0], here).wait_send()
    own_wide.wait()
    sent = dq_ref.at[pl.ds(0, PEERS - 1)]
    rest = remote(sent, sent, send_sem.at[2], recv_sem.at[2], here)
    rest.wait_send()
    rest.wait_recv()
    for n in range(2):
        sent = total.at[n, pl.ds(0, PEERS - 1)]
        rest = remote(sent, sent, send_sem.at[n], recv_sem.at[n], here)
        rest.wait_send()
        rest.wait_recv()
        own[n].wait()


def collect(ranks, block_target, dq, dk, dv):
    return pl.pallas_call(
        collect_kernel,
        name="collect",
        out_shape=(
            jax.ShapeDtypeStruct((GROUPS * RUN, KV_HEADS * UNIT), BF16),
            jax.ShapeDtypeStruct((GROUPS * RUN, KV_HEADS * HEAD_DIM), BF16),
            jax.ShapeDtypeStruct((GROUPS * RUN, KV_HEADS * HEAD_DIM), BF16),
        ),
        in_specs=[pl.BlockSpec(memory_space=pltpu.SMEM)] * 2 + [pl.BlockSpec(memory_space=pltpu.VMEM)] * 3,
        out_specs=[pl.BlockSpec(memory_space=pl.ANY)] * 3,
        scratch_shapes=[
            pltpu.VMEM((PEERS, RUN, UNIT), BF16),
            pltpu.VMEM((TILES * TILE_PARTS, BLOCK_ROWS, HEAD_DIM), F32),
            pltpu.VMEM((2, 2, PEERS, RUN, HEAD_DIM), BF16),
            pltpu.VMEM((2, 2, 4, PEERS, RUN, HEAD_DIM), BF16),
            pltpu.VMEM((2, PEERS, RUN, HEAD_DIM), BF16),
            pltpu.SemaphoreType.DMA((3,)),
            pltpu.SemaphoreType.DMA((3,)),
            pltpu.SemaphoreType.DMA((3,)),
            pltpu.SemaphoreType.DMA((2, 2)),
            pltpu.SemaphoreType.DMA((2, 4, 2, PARTS)),
        ],
        compiler_params=pltpu.CompilerParams(
            collective_id=1, has_side_effects=True, vmem_limit_bytes=24 * 1024 * 1024
        ),
    )(ranks, block_target, dq, dk, dv)


def deliver_kernel(*refs):
    copies = [pltpu.make_async_copy(refs[n], refs[3 + n], refs[6].at[n]) for n in range(3)]
    for copy in copies:
        copy.start()
    for copy in copies:
        copy.wait()


def deliver(*grads):
    return pl.pallas_call(
        deliver_kernel,
        name="deliver",
        out_shape=tuple(jax.ShapeDtypeStruct(grad.shape, grad.dtype) for grad in grads),
        in_specs=[pl.BlockSpec(memory_space=pl.ANY)] * 3,
        out_specs=[pl.BlockSpec(memory_space=pl.ANY)] * 3,
        scratch_shapes=[pltpu.SemaphoreType.DMA((3,))],
        compiler_params=pltpu.CompilerParams(vmem_limit_bytes=1024 * 1024),
    )(*grads)


def on_device(query_rows, key_rows, value_rows, output_grad, block_target, doc_lengths):
    queries, grads, keys, values, keys_turned, targets, lengths, ranks = scatter(
        query_rows, output_grad, key_rows, value_rows, block_target.transpose(0, 2, 1), doc_lengths
    )
    dq, dk, dv = attention(lengths, ranks, targets, queries, grads, keys, values, keys_turned)
    blocks = (GROUP_BLOCKS, BLOCK_ROWS, HEAD_DIM)
    return deliver(*collect(ranks, targets, dq, dk.reshape(blocks), dv.reshape(blocks)))


def solution(mesh):
    in_specs = (
        P(("grp", "ctx"), None),
        P(("grp", "ctx"), None),
        P(("grp", "ctx"), None),
        P(("grp", "ctx"), None),
        P(),
        P("grp", None),
    )
    out_specs = (P(("grp", "ctx"), None), P(("grp", "ctx"), None), P(("grp", "ctx"), None))
    return jax.shard_map(
        on_device, mesh=mesh, in_specs=in_specs, out_specs=out_specs, check_vma=False
    )
```
